32 devices in a mesh: cols: 1, trc: 16 (over z, x, core), lev: 2 (over y).
Axes of the slice: x: 2, y: 2, z: 4, core: 2. Of those that a mesh axis runs over, the one named last changes fastest.
Arguments:
- potential_warmth: float32 [128, 8, 128], P('lev', 'cols', 'trc'), may hold values from -6 to 6
- saltiness_anomaly: float32 [128, 8, 128], P('lev', 'cols', 'trc'), may hold values from -6 to 6
- zonal_speed: float32 [128, 8, 128], P('lev', 'cols', 'trc'), may hold values from -3 to 3
- meridional_speed: float32 [128, 8, 128], P('lev', 'cols', 'trc'), may hold values from -3 to 3
- marine_indicator: int32 [128, 8, 128], P('lev', 'cols', 'trc'), may hold values from 0 to 1, as said below
- species_concentrations: float32 [64, 128, 8, 128], P('trc', 'lev', 'cols'), may hold values from 0.1 to 2
- coupling_matrix: bfloat16 [64, 64], replicated, may hold values from -0.75 to 0.75
- species_guild_number: int32 [64], replicated, may hold values from 0 to 7
- guild_extinction_coefficient: float32 [8], replicated, may hold values from 0.0001 to 0.0012
Outputs:
- warmth_final: float32 [128, 8, 128], P('lev', 'cols', 'trc')
- saltiness_final: float32 [128, 8, 128], P('lev', 'cols', 'trc')
- zonal_speed_final: float32 [128, 8, 128], P('lev', 'cols', 'trc')
- meridional_speed_final: float32 [128, 8, 128], P('lev', 'cols', 'trc')
- species_final: float32 [64, 128, 8, 128], P('trc', 'lev', 'cols')
The draws below stay inside these ranges and needn't reach their ends.
Inputs may be any that keep to these rules, and one draw needn't show every extreme that they name: `marine_indicator`: each column is sea from level 0 down to a depth drawn per column and land below it; the columns at the first index and at the last two indices of the second horizontal dimension are sea at every level.
All inputs are finite; a program needn't handle non-finite values.
Results may differ from the reference program's by a relative error of at most 0.00066.
Values may be sent and summed in bfloat16 or wider, within the bound.
No kernel may reach another device: no remote copies, remote signals or barrier semaphores. Data moves between devices by JAX's collectives and lax.ppermute only.
A program may use at most 64 MiB of HBM per device.

```python
import math
import jax
import jax.numpy as jnp
from jax import lax

NT = 64
NGRP = 8
ZONAL_POINTS = 8
MERIDIONAL_POINTS = 128
DEPTH_LAYERS = 128


def draw_marine_indicator(key, part):
    column_depth = jax.random.randint(key, (ZONAL_POINTS, MERIDIONAL_POINTS), -(DEPTH_LAYERS // 4), DEPTH_LAYERS + 1)
    column_depth = jnp.maximum(column_depth, 0)
    row_index = lax.broadcasted_iota(jnp.int32, (ZONAL_POINTS, MERIDIONAL_POINTS), 1)
    full_sea = (row_index == 0) | (row_index >= MERIDIONAL_POINTS - 2)
    column_depth = jnp.where(full_sea, DEPTH_LAYERS, column_depth)
    level_index = lax.broadcasted_iota(jnp.int32, (DEPTH_LAYERS, ZONAL_POINTS, MERIDIONAL_POINTS), 0)
    return (level_index < column_depth[None]).astype(jnp.int32)


def with_ends(entries, own_key, smallest, largest):
    longest = entries.shape.index(max(entries.shape))
    spots = []
    for shift in (0, 1):
        where = [jax.random.randint(jax.random.fold_in(own_key, axis), (), 0, length) for axis, length in enumerate(entries.shape)]
        where[longest] = (where[longest] + shift) % entries.shape[longest]
        spots.append(tuple(where))
    return entries.at[spots[0]].set(smallest).at[spots[1]].set(largest)


def steps_of(rng, shape, shards, smallest, high):
    loudness, own = 1.0, jax.random.fold_in(rng, 6)
    for axis_at, parts in shards:
        draws = jnp.exp(jax.random.uniform(jax.random.fold_in(own, axis_at), (parts,), jnp.float32, smallest / len(shards), high / len(shards)))
        loudness = loudness * jnp.repeat(draws, shape[axis_at] // parts).reshape([-1 if axis == axis_at else 1 for axis in range(len(shape))])
    return loudness


def scatter_about(rng, shape, spread, bound, shards=(), dtype=jnp.bfloat16):
    values = jax.random.normal(rng, shape, jnp.float32) * spread
    if len(shards) > 0:
        values = steps_of(rng, shape, shards, -0.22, 0.18) * values
    return jnp.clip(values, min=-bound, max=bound).astype(dtype)


def setup_inputs(seed: int = 0) -> dict:
    arg_keys = jax.random.split(jax.random.key(seed), 10)
    potential_warmth = scatter_about(arg_keys[0], (DEPTH_LAYERS, ZONAL_POINTS, MERIDIONAL_POINTS), 1.0, 6.0, ((0, 2), (2, 16)), jnp.float32)
    saltiness_anomaly = scatter_about(arg_keys[1], (DEPTH_LAYERS, ZONAL_POINTS, MERIDIONAL_POINTS), 1.0, 6.0, ((0, 2), (2, 16)), jnp.float32)
    zonal_speed = scatter_about(arg_keys[2], (DEPTH_LAYERS, ZONAL_POINTS, MERIDIONAL_POINTS), 0.5, 3.0, ((0, 2), (2, 16)), jnp.float32)
    meridional_speed = scatter_about(arg_keys[3], (DEPTH_LAYERS, ZONAL_POINTS, MERIDIONAL_POINTS), 0.5, 3.0, ((0, 2), (2, 16)), jnp.float32)
    marine_indicator = draw_marine_indicator(jax.random.fold_in(arg_keys[9], 71), 0)
    species_concentrations = jnp.clip(jnp.exp(math.log(2.0) - 2.9957323 * jax.random.uniform(arg_keys[5], (NT, DEPTH_LAYERS, ZONAL_POINTS, MERIDIONAL_POINTS), jnp.float32) ** steps_of(arg_keys[5], (NT, DEPTH_LAYERS, ZONAL_POINTS, MERIDIONAL_POINTS), ((0, 16), (1, 2)), -0.2, 0.2)), 0.1, 2.0)
    coupling_matrix = scatter_about(arg_keys[6], (NT, NT), NT ** -0.5, 0.75)
    species_guild_number = with_ends(jax.random.randint(arg_keys[7], (NT,), 0, NGRP), jax.random.fold_in(arg_keys[7], 1), 0, NGRP - 1).astype(jnp.int32)
    guild_extinction_coefficient = jnp.clip(jnp.exp(jax.random.uniform(arg_keys[8], (NGRP,), jnp.float32, math.log(0.0001), math.log(0.0012))), 0.0001, 0.0012)
    return dict(potential_warmth=potential_warmth, saltiness_anomaly=saltiness_anomaly, zonal_speed=zonal_speed, meridional_speed=meridional_speed, marine_indicator=marine_indicator, species_concentrations=species_concentrations, coupling_matrix=coupling_matrix, species_guild_number=species_guild_number, guild_extinction_coefficient=guild_extinction_coefficient)


viscosity = 0.2
buoyancy = 0.25
marine_advance = 0.05
tracer_step = 0.2
level_step = 0.04
react_step = 0.25
warming_amount = 60.0


def minmod(slope_left, slope_right):
    return 0.5 * (jnp.sign(slope_left) + jnp.sign(slope_right)) * jnp.minimum(jnp.abs(slope_left), jnp.abs(slope_right))


def limited_div(padded, face_speed, dimension):
    length = padded.shape[dimension] - 4
    far_left = lax.slice_in_dim(padded, 0, length + 1, axis=dimension)
    left_cell = lax.slice_in_dim(padded, 1, length + 2, axis=dimension)
    right_cell = lax.slice_in_dim(padded, 2, length + 3, axis=dimension)
    far_right = lax.slice_in_dim(padded, 3, length + 4, axis=dimension)
    plus_side = left_cell + 0.5 * minmod(left_cell - far_left, right_cell - left_cell)
    minus_side = right_cell - 0.5 * minmod(right_cell - left_cell, far_right - right_cell)
    face_flux = jnp.maximum(face_speed, 0.0) * plus_side + jnp.minimum(face_speed, 0.0) * minus_side
    return lax.slice_in_dim(face_flux, 1, length + 1, axis=dimension) - lax.slice_in_dim(face_flux, 0, length, axis=dimension)


def shift_east(values):
    return jnp.roll(values, -1, 1)


def shift_west(values):
    return jnp.roll(values, 1, 1)


def shift_north(values):
    return jnp.roll(values, -1, 2)


def shift_south(values):
    return jnp.roll(values, 1, 2)


def reference(potential_warmth, saltiness_anomaly, zonal_speed, meridional_speed, marine_indicator, species_concentrations, coupling_matrix, species_guild_number, guild_extinction_coefficient):
    marine_indicator_real = marine_indicator.astype(jnp.float32)
    fluid_mass_per_volume = 0.8 * saltiness_anomaly - 0.2 * potential_warmth
    hydrostatic_pressure = buoyancy * (jnp.cumsum(fluid_mass_per_volume, axis=0) - 0.5 * fluid_mass_per_volume)
    mask_east = marine_indicator_real * shift_east(marine_indicator_real)
    mask_north = marine_indicator_real * shift_north(marine_indicator_real)
    east_laplace = shift_east(zonal_speed) + shift_west(zonal_speed) + shift_north(zonal_speed) + shift_south(zonal_speed) - 4.0 * zonal_speed
    north_laplace = shift_east(meridional_speed) + shift_west(meridional_speed) + shift_north(meridional_speed) + shift_south(meridional_speed) - 4.0 * meridional_speed
    zonal_speed_final = mask_east * (zonal_speed + marine_advance * (-(shift_east(hydrostatic_pressure) - hydrostatic_pressure) + viscosity * east_laplace))
    meridional_speed_final = mask_north * (meridional_speed + marine_advance * (-(shift_north(hydrostatic_pressure) - hydrostatic_pressure) + viscosity * north_laplace))
    divergence = zonal_speed_final - shift_west(zonal_speed_final) + meridional_speed_final - shift_south(meridional_speed_final)
    deeper_sum = jnp.cumsum(divergence[::-1], axis=0)[::-1]
    level_index = lax.broadcasted_iota(jnp.int32, divergence.shape, 0)
    faces_vertical = jnp.concatenate([jnp.where(level_index == 0, 0.0, deeper_sum), jnp.zeros_like(deeper_sum[:1])], axis=0)

    def donor_quantity(values):
        flux_east = jnp.maximum(zonal_speed_final, 0.0) * values + jnp.minimum(zonal_speed_final, 0.0) * shift_east(values)
        flux_north = jnp.maximum(meridional_speed_final, 0.0) * values + jnp.minimum(meridional_speed_final, 0.0) * shift_north(values)
        padded = jnp.pad(values, ((1, 1), (0, 0), (0, 0)))
        flux_down = jnp.maximum(faces_vertical, 0.0) * padded[:-1] + jnp.minimum(faces_vertical, 0.0) * padded[1:]
        return (flux_east - shift_west(flux_east)) + (flux_north - shift_south(flux_north)) + (flux_down[1:] - flux_down[:-1])

    faces_east = jnp.concatenate([zonal_speed_final[:, -1:], zonal_speed_final], axis=1)
    faces_north = jnp.concatenate([meridional_speed_final[:, :, -1:], meridional_speed_final], axis=2)

    def advect(values):
        for repeat in range(2):
            beside = jnp.concatenate([values[:, -2:], values, values[:, :2]], axis=1)
            beside_all = jnp.concatenate([values[:, :, -2:], values, values[:, :, :2]], axis=2)
            stacks = jnp.pad(values, ((2, 2), (0, 0), (0, 0)))
            sideways = limited_div(beside, faces_east, 1) + limited_div(beside_all, faces_north, 2)
            upright = limited_div(stacks, faces_vertical, 0)
            values = values - (tracer_step * sideways + level_step * upright)
        return values

    advected = lax.map(advect, species_concentrations)
    onehot = (species_guild_number[:, None] == lax.broadcasted_iota(jnp.int32, (species_guild_number.shape[0], guild_extinction_coefficient.shape[0]), 1)).astype(jnp.float32)
    absorb = jnp.sum(onehot * guild_extinction_coefficient[None, :], axis=1)

    def per_level(level_block):
        rounded = lax.optimization_barrier(level_block.astype(jnp.bfloat16))
        flattened = rounded.reshape(rounded.shape[0], -1)
        reaction = jnp.dot(coupling_matrix, flattened, preferred_element_type=jnp.float32).reshape(level_block.shape)
        updated = level_block + react_step * reaction
        attenuation = jnp.sum(absorb[:, None, None] * rounded.astype(jnp.float32), axis=0)
        return updated, attenuation

    updated, attenuation = lax.map(per_level, jnp.swapaxes(advected, 0, 1))
    species_final = jnp.swapaxes(updated, 0, 1)
    light_path = jnp.cumsum(attenuation, axis=0) - attenuation
    radiation_captured = jnp.exp(-light_path) * (1.0 - jnp.exp(-attenuation))
    warmth_final = potential_warmth - marine_advance * donor_quantity(potential_warmth) + warming_amount * marine_indicator_real * radiation_captured
    saltiness_final = saltiness_anomaly - marine_advance * donor_quantity(saltiness_anomaly)
    return warmth_final, saltiness_final, zonal_speed_final, meridional_speed_final, species_final
```

```python
import math

import jax
import jax.numpy as jnp
from jax import lax
from jax.experimental import pallas as pl
from jax.experimental.pallas import tpu as pltpu
from jax.sharding import PartitionSpec as P

viscosity = 0.2
buoyancy = 0.25
marine_advance = 0.05
tracer_step = 0.2
level_step = 0.04
react_step = 0.25
warming_amount = 60.0

speed_bound = 3.0
hydro_bound = 6.0
species_bound = 2.0
coupling_bound = 0.75

LANES = 128
DRY = 1e30
F32 = jnp.float32


def call(kernel, out_shape, args, specs=None, scratch=(), name=None):
    vmem = pl.BlockSpec(memory_space=pltpu.VMEM)
    outs = jax.tree.map(lambda _: vmem, out_shape)
    return pl.pallas_call(
        kernel,
        out_shape=out_shape,
        in_specs=[vmem] * len(args) if specs is None else specs,
        out_specs=outs,
        scratch_shapes=list(scratch),
        compiler_params=pltpu.CompilerParams(vmem_limit_bytes=40 * 1024 * 1024),
        name=name,
    )(*args)


def f32(*shape):
    return jax.ShapeDtypeStruct(shape, F32)


def shift(a, steps, axis):
    return pltpu.roll(a, (-steps) % a.shape[axis], axis)


def minmod(p, r):
    return jnp.maximum(jnp.minimum(p, r), 0.0) + jnp.minimum(jnp.maximum(p, r), 0.0)


def sideways(c, speed, axis):
    d = shift(c, 1, axis) - c
    half = 0.5 * minmod(shift(d, -1, axis), d)
    flux = speed * jnp.where(speed > 0.0, c + half, shift(c - half, 1, axis))
    return flux - shift(flux, -1, axis)


def exchange_levels(part):
    return lax.ppermute(part, "lev", [(0, 1), (1, 0)])


def shards(
    potential_warmth,
    saltiness_anomaly,
    zonal_speed,
    meridional_speed,
    marine_indicator,
    species_concentrations,
    coupling_matrix,
    species_guild_number,
    guild_extinction_coefficient,
):
    cols, ntrc, nlev = lax.axis_size("cols"), lax.axis_size("trc"), lax.axis_size("lev")
    D, X, Y = potential_warmth.shape
    T = species_concentrations.shape[0]
    NT = coupling_matrix.shape[0]
    YG = species_concentrations.shape[3]
    assert nlev == 2 and YG == LANES and X % 8 == 0 and Y % 8 == 0 and ntrc % 2 == 0
    assert LANES % D == 0 and D % 8 == 0 and X % (LANES // D) == 0
    H = X if cols > 1 else 0
    XE = X + 2 * H
    W, DX = D * XE, D * X
    G = LANES // D
    XL = XE // G

    def widen(block, dim):
        if H == 0:
            return block
        ahead = [(i, (i + 1) % cols) for i in range(cols)]
        back = [(i, (i - 1) % cols) for i in range(cols)]
        low = lax.ppermute(block, "cols", ahead)
        high = lax.ppermute(block, "cols", back)
        return jnp.concatenate([low, block, high], axis=dim)

    warmth, salt, zonal, merid, marine = (
        widen(jnp.transpose(a, (1, 2, 0)), 0)
        for a in (potential_warmth, saltiness_anomaly, zonal_speed, meridional_speed, marine_indicator)
    )
    species = widen(species_concentrations, 2)
    NP = ntrc // 2
    pairs_apart = [[2 * g + c for g in range(NP)] for c in range(2)]

    def pack(t_ref, s_ref, u_ref, v_ref, m_ref, pay_ref, lo_ref, hi_ref, lt_ref):
        t, s = t_ref[...], s_ref[...]
        density = jnp.where(m_ref[...] > 0, 0.8 * s - 0.2 * t, DRY)
        for f, a in enumerate((density, u_ref[...], v_ref[...])):
            rows = jnp.concatenate([a[g * XL : (g + 1) * XL] for g in range(G)], axis=2)
            rows = rows.reshape(XL * Y, LANES)
            for g in range(NP):
                pay_ref[g, f * XL * Y : (f + 1) * XL * Y] = rows
        lane = lax.broadcasted_iota(jnp.int32, (Y, LANES), 1)
        upper = lax.axis_index("lev") == 0
        for i, a in enumerate((t, s)):
            edge = jnp.zeros((Y, LANES), F32)
            for x in range(XE):
                lo_ref[i * XE + x : i * XE + x + 1] = a[x, 0:1]
                hi_ref[i * XE + x : i * XE + x + 1] = a[x, Y - 1 : Y]
                column = jnp.where(upper, a[x, :, D - 1 : D], a[x, :, 0:1])
                edge = jnp.where(lane == x, column, edge)
            lt_ref[i * Y : (i + 1) * Y] = edge

    payload, lo, hi, edges = call(
        pack,
        (f32(NP, 3 * XL * Y, LANES), f32(2 * XE, D), f32(2 * XE, D), f32(2 * Y, LANES)),
        (warmth, salt, zonal, merid, marine),
        name="pack_ocean",
    )
    mine = lax.all_to_all(
        payload, "trc", split_axis=0, concat_axis=0, tiled=True, axis_index_groups=pairs_apart
    )

    start = jnp.where(lax.axis_index("lev") == 0, D - 4, 0)
    outer_levels = exchange_levels(lax.dynamic_slice_in_dim(species, start, 4, 1))
    mine, outer_levels = lax.optimization_barrier((mine, outer_levels))
    other = lax.ppermute(mine, "trc", [(i, i ^ 1) for i in range(ntrc)])

    def unpack(a_ref, b_ref, e_ref, f_ref, l_ref):
        core = lax.axis_index("trc") % 2
        for f in range(3):
            for x in range(XL):
                at = slice((f * XL + x) * Y, (f * XL + x + 1) * Y)
                rows = []
                for g in range(NP):
                    a, b = a_ref[g, at], b_ref[g, at]
                    rows += [jnp.where(core == 0, a, b), jnp.where(core == 0, b, a)]
                turned = jnp.concatenate(rows, axis=0).T
                for g in range(G):
                    f_ref[f, pl.ds(x + g * XL, D, stride=XE), :] = turned[g * D : (g + 1) * D]
        density = f_ref[0].reshape(D, XE, YG)
        l_ref[0:XE] = jnp.sum(jnp.where(density < 0.5 * DRY, density, 0.0), axis=0)
        first = jnp.where(lax.axis_index("lev") == 0, D - 2, 0)
        for f in range(3):
            for k in range(2):
                at = (1 + 2 * f + k) * XE
                l_ref[at : at + XE] = f_ref[f, pl.ds(pl.multiple_of((first + k) * XE, 8), XE)]
        l_ref[7 * XE :] = e_ref[...]

    fields, own_levels = call(
        unpack, (f32(3, W, YG), f32(7 * XE + 2 * Y, YG)), (mine, other, edges), name="unpack_ocean"
    )
    fields = fields.reshape(3, D, XE, YG)
    far_levels = exchange_levels(own_levels)

    def speeds(f_ref, r_ref, uv_ref, fv_ref, sum_ref):
        lev = lax.axis_index("lev")
        above = jnp.where(lev > 0, r_ref[0:XE], 0.0)

        def far(f, k):
            at = (1 + 2 * f + k) * XE
            return r_ref[at : at + XE]

        def dense(raw):
            return jnp.where(raw < 0.5 * DRY, raw, 0.0)

        def level(e, raw, u, v, before):
            wet = jnp.where(raw < 0.5 * DRY, 1.0, 0.0)
            d = dense(raw)
            total = before + d
            p = buoyancy * (total - 0.5 * d)

            def moved(a, axis):
                mask = wet * shift(wet, 1, axis)
                lap = shift(a, 1, 0) + shift(a, -1, 0) + shift(a, 1, 1) + shift(a, -1, 1) - 4.0 * a
                return mask * (a + marine_advance * (-(shift(p, 1, axis) - p) + viscosity * lap))

            uv_ref[0, e] = moved(u, 0)
            uv_ref[1, e] = moved(v, 1)
            return total

        total = above - dense(far(0, 0)) - dense(far(0, 1))
        for k in range(2):
            total = level(k, far(0, k), far(1, k), far(2, k), total)
        total = lax.fori_loop(
            0,
            D,
            lambda k, t: level(k + 2, f_ref[0, k], f_ref[1, k], f_ref[2, k], t),
            above,
            unroll=4,
        )
        for k in range(2):
            total = level(D + 2 + k, far(0, k), far(1, k), far(2, k), total)

        def divergence(e):
            u, v = uv_ref[0, e], uv_ref[1, e]
            return u - shift(u, -1, 0) + v - shift(v, -1, 1)

        fv_ref[D + 2] = jnp.zeros((XE, YG), F32)
        below = -divergence(D + 2)
        fv_ref[D + 3] = below
        fv_ref[D + 4] = below - divergence(D + 3)

        def climb(i, total):
            e = D + 1 - i
            total = total + divergence(e)
            fv_ref[e] = total
            return total

        total = lax.fori_loop(0, D, climb, jnp.zeros((XE, YG), F32), unroll=4)
        sum_ref[...] = total
        for e in (1, 0):
            total = total + divergence(e)
            fv_ref[e] = total

    uv, fv, own_sum = call(
        speeds,
        (f32(2, D + 4, XE, YG), f32(D + 5, XE, YG), f32(XE, YG)),
        (fields, far_levels),
        name="face_speeds",
    )
    far_sum = exchange_levels(own_sum)

    def deeper(r_ref):
        return jnp.where(lax.axis_index("lev") == nlev - 1, 0.0, r_ref[...])

    def advect(c_ref, h_ref, uv_ref, fv_ref, r_ref, adv_ref, msg_ref, c_pad, a_pad, sem):
        lev = lax.axis_index("lev")
        copy = pltpu.make_async_copy(c_ref, c_pad.at[:, pl.ds(4, D)], sem)
        copy.start()
        below = deeper(r_ref)
        has_above, has_below = lev > 0, lev < nlev - 1
        for k in range(4):
            c_pad[:, k] = jnp.where(has_above, h_ref[:, k], 0.0)
            c_pad[:, D + 4 + k] = jnp.where(has_below, h_ref[:, k], 0.0)
        copy.wait()

        def step(src, off, e0, count, put):
            def face(e):
                w = fv_ref[e] + below
                return jnp.where((lev == 0) & (e == 2), 0.0, w)

            def slope(lo, mid, hi):
                return 0.5 * minmod(mid - lo, hi - mid)

            def down(e, up_cell, lo, mid, hi):
                half = slope(lo, mid, hi)
                w = face(e)
                return w * jnp.where(w > 0.0, up_cell, mid - half), mid + half

            c0 = src[:, e0 - 2 + off]
            c1 = src[:, e0 - 1 + off]
            c2 = src[:, e0 + off]
            c3 = src[:, e0 + 1 + off]
            up_cell = c1 + slope(c0, c1, c2)
            flux, up_cell = down(e0, up_cell, c1, c2, c3)

            def one(i, carry):
                mid, hi, flux, up_cell = carry
                e = e0 + i
                nxt = src[:, e + 2 + off]
                flux_next, up_next = down(e + 1, up_cell, mid, hi, nxt)
                u, v = uv_ref[0, e], uv_ref[1, e]
                flat = sideways(mid, u[None], 1) + sideways(mid, v[None], 2)
                put(i, mid - (tracer_step * flat + level_step * (flux_next - flux)))
                return hi, nxt, flux_next, up_next

            lax.fori_loop(0, count, one, (c2, c3, flux, up_cell), unroll=16)

        def keep(i, a):
            a_pad[:, i] = a

        step(c_pad, 2, 0, D + 4, keep)
        for k in range(2):
            a_pad[:, k] = jnp.where(has_above, a_pad[:, k], 0.0)
            a_pad[:, D + 2 + k] = jnp.where(has_below, a_pad[:, D + 2 + k], 0.0)

        def give(i, a):
            adv_ref[:, pl.ds(pl.multiple_of(i * X, 8), X)] = a[:, H : H + X]

        step(a_pad, 0, 2, D, give)
        for w in range(DX // LANES):
            turned = []
            for t in range(T):
                rows = [adv_ref[t, pl.ds(w * G + g, D, stride=X), :] for g in range(G)]
                turned.append(jnp.concatenate(rows, axis=0).T)
            for d in range(ntrc):
                rows = [turned[t][d * Y : (d + 1) * Y] for t in range(T)]
                msg_ref[d, :, w * LANES : (w + 1) * LANES] = jnp.concatenate(rows, axis=0).astype(
                    jnp.bfloat16
                )

    vmem = pl.BlockSpec(memory_space=pltpu.VMEM)
    advected, message = call(
        advect,
        (f32(T, DX, YG), jax.ShapeDtypeStruct((ntrc, T * Y, DX), jnp.bfloat16)),
        (species, outer_levels, uv, fv, far_sum),
        specs=[pl.BlockSpec(memory_space=pl.ANY)] + [vmem] * 4,
        scratch=(
            pltpu.VMEM((T, D + 8, XE, YG), F32),
            pltpu.VMEM((T, D + 4, XE, YG), F32),
            pltpu.SemaphoreType.DMA(()),
        ),
        name="advect_tracers",
    )
    gathered = lax.all_to_all(message, "trc", split_axis=0, concat_axis=0, tiled=True)

    ring = [(i, (i + 1) % ntrc) for i in range(ntrc)]
    south = lax.ppermute(hi, "trc", ring)
    north = lax.ppermute(lo, "trc", [(b, a) for a, b in ring])

    def ocean(
        t_ref, s_ref, uv_ref, fv_ref, r_ref, l_ref, so_ref, no_ref, sa_ref, wa_ref, ua_ref, va_ref, turn
    ):
        me, lev = lax.axis_index("trc"), lax.axis_index("lev")
        below = deeper(r_ref)
        for x in range(XE):
            def level_rows(ref, first):
                return ref[pl.ds(first * XE + x, D, stride=XE), :]

            under = below[x : x + 1]
            turn[0, x] = level_rows(uv_ref.at[0], 2).T
            turn[1, x] = level_rows(uv_ref.at[1], 2).T
            turn[2, x] = (level_rows(fv_ref, 2) + under).T
            turn[3, x] = (level_rows(fv_ref, 3) + under).T
        here = pl.ds(pl.multiple_of(me * Y, 8), Y)
        past = pl.ds(pl.multiple_of(lax.rem(me + ntrc - 1, ntrc) * Y, 8), Y)
        u, v, w, w_next = (turn[i, :, here] for i in range(4))
        v_south = turn[1, :, past][:, Y - 1 : Y]
        level = lax.broadcasted_iota(jnp.int32, (XE, Y, D), 2)
        row = lax.broadcasted_iota(jnp.int32, (XE, Y, D), 1)
        w = jnp.where((lev == 0) & (level == 0), 0.0, w)

        def east(a):
            return jnp.concatenate([a[1:], a[:1]], axis=0)

        def west(a):
            return jnp.concatenate([a[-1:], a[:-1]], axis=0)

        def donor(speed, near, far):
            return jnp.maximum(speed, 0.0) * near + jnp.minimum(speed, 0.0) * far

        def advance(c, i):
            so = jnp.stack([so_ref[i * XE + x : i * XE + x + 1] for x in range(XE)])
            no = jnp.stack([no_ref[i * XE + x : i * XE + x + 1] for x in range(XE)])
            tile = l_ref[7 * XE + i * Y : 7 * XE + (i + 1) * Y]
            edge = jnp.stack([tile[:, x : x + 1] for x in range(XE)])
            wide = jnp.concatenate([c, jnp.zeros((XE, Y, LANES - D), F32)], axis=2) if D < LANES else c
            upper = shift(wide, -1, 2)[:, :, :D]
            upper = jnp.where(level == 0, jnp.where(lev > 0, edge, 0.0), upper)
            lower = shift(wide, 1, 2)[:, :, :D]
            lower = jnp.where(level == D - 1, jnp.where(lev < nlev - 1, edge, 0.0), lower)
            fe = donor(u, c, east(c))
            fn = donor(v, c, jnp.where(row == Y - 1, no, shift(c, 1, 1)))
            fn_south = jnp.where(row == 0, donor(v_south, so, c[:, 0:1]), shift(fn, -1, 1))
            fall = donor(w_next, c, lower) - donor(w, upper, c)
            return c - marine_advance * ((fe - west(fe)) + (fn - fn_south) + fall)

        sa_ref[...] = advance(s_ref[...], 1)[H : H + X]
        wa_ref[...] = advance(t_ref[...], 0)[H : H + X]
        ua_ref[...] = u[H : H + X]
        va_ref[...] = v[H : H + X]

    saltiness_final, warmth_moved, zonal_speed_final, meridional_speed_final = call(
        ocean,
        (f32(X, Y, D),) * 4,
        (
            warmth,
            salt,
            uv.reshape(2, (D + 4) * XE, YG),
            fv.reshape((D + 5) * XE, YG),
            far_sum,
            far_levels,
            south,
            north,
        ),
        scratch=(pltpu.VMEM((4, XE, YG, D), F32),),
        name="own_ocean",
    )

    speed_most = speed_bound + marine_advance * (
        2 * buoyancy * hydro_bound * D * nlev + viscosity * 8 * speed_bound
    )
    growth = 1 + 4 * tracer_step * speed_most + 2 * level_step * (4 * speed_most * D * nlev)
    react_most = NT * coupling_bound * species_bound * growth**2
    unit = 2.0 ** max(0, math.ceil(math.log2(react_most / 65504.0)))

    def spread_columns(c_ref, o_ref):
        n = NT * Y

        def pick(shape, along):
            wide, narrow = (lax.broadcasted_iota(jnp.int32, shape, d) for d in (along, 1 - along))
            return jnp.where(wide // Y == narrow, 1.0, 0.0).astype(jnp.bfloat16)

        tall = jnp.dot(pick((n, NT), 0), c_ref[...], preferred_element_type=F32)
        full = jnp.dot(
            tall.astype(jnp.bfloat16), pick((NT, n), 1), preferred_element_type=F32
        )
        row, lane = (lax.broadcasted_iota(jnp.int32, (n, n), d) for d in (0, 1))
        o_ref[...] = jnp.where(row % Y == lane % Y, full, 0.0).astype(jnp.bfloat16)

    spread = call(
        spread_columns,
        jax.ShapeDtypeStruct((NT * Y, NT * Y), jnp.bfloat16),
        (coupling_matrix,),
        name="spread_coupling",
    )
    flat_tracers = gathered.reshape(NT * Y, DX)
    reaction = jnp.dot(spread, flat_tracers, preferred_element_type=F32)
    reaction = (reaction * (1.0 / unit)).astype(jnp.float16).reshape(ntrc, T * Y, DX)
    returned = lax.all_to_all(reaction, "trc", split_axis=0, concat_axis=0, tiled=True)

    def shade(x_ref, g_ref, k_ref, att_ref, cum_ref):
        att = jnp.zeros((Y, DX), F32)
        for d in range(ntrc):
            rows = x_ref[d].astype(F32)
            for t in range(T):
                att = att + k_ref[g_ref[d * T + t]] * rows[t * Y : (t + 1) * Y]
        att_ref[...] = att
        lane = lax.broadcasted_iota(jnp.int32, (Y, DX), 1)
        total = att
        width = 1
        while width < D:
            total = total + jnp.where(lane % D < width, 0.0, shift(total, -width, 1))
            width *= 2
        cum_ref[...] = total

    smem = pl.BlockSpec(memory_space=pltpu.SMEM)
    attenuation, shaded = call(
        shade,
        (f32(Y, DX), f32(Y, DX)),
        (gathered, species_guild_number, guild_extinction_coefficient),
        specs=[vmem, smem, smem],
        name="shade",
    )
    far_shade = exchange_levels(shaded)

    def heat(att_ref, cum_ref, r_ref, w_ref, m_ref, o_ref):
        att = att_ref[...]
        path = cum_ref[...] - att
        caught = 1.0 - jnp.exp(-att)
        lev = lax.axis_index("lev")
        for x in range(X):
            at = slice(x * D, (x + 1) * D)
            above = jnp.where(lev > 0, r_ref[:, (x + 1) * D - 1 : (x + 1) * D], 0.0)
            absorbed = jnp.exp(-(above + path[:, at])) * caught[:, at]
            o_ref[x] = w_ref[x] + warming_amount * (m_ref[x].astype(F32) * absorbed)

    warmth_final = call(
        heat,
        f32(X, Y, D),
        (attenuation, shaded, far_shade, warmth_moved, jnp.transpose(marine_indicator, (1, 2, 0))),
        name="heat",
    )

    def finish(r_ref, a_ref, o_ref):
        for t in range(T):
            for w in range(DX // LANES):
                rows = [
                    r_ref[d, t * Y : (t + 1) * Y, w * LANES : (w + 1) * LANES] for d in range(ntrc)
                ]
                turned = (react_step * unit) * jnp.concatenate(rows, axis=0).T
                for g in range(G):
                    at = pl.ds(w * G + g, D, stride=X)
                    o_ref[t, at, :] = a_ref[t, at, :] + turned[g * D : (g + 1) * D]

    species_final = call(
        finish, f32(T, DX, YG), (returned.astype(F32), advected), name="finish_tracers"
    )
    ocean_outputs = (warmth_final, saltiness_final, zonal_speed_final, meridional_speed_final)
    ocean_outputs = tuple(jnp.transpose(a, (2, 0, 1)) for a in ocean_outputs)
    return ocean_outputs + (species_final.reshape(T, D, X, YG),)


def solution(mesh):
    ocean = P("lev", "cols", "trc")
    in_specs = (ocean,) * 5 + (P("trc", "lev", "cols", None), P(), P(), P())
    out_specs = (ocean,) * 4 + (P("trc", "lev", "cols", None),)
    return jax.shard_map(shards, mesh=mesh, in_specs=in_specs, out_specs=out_specs, check_vma=False)
```

```python
import math

import jax
import jax.numpy as jnp
from jax import lax
from jax.experimental import pallas as pl
from jax.experimental.pallas import tpu as pltpu
from jax.sharding import PartitionSpec as P

viscosity = 0.2
buoyancy = 0.25
marine_advance = 0.05
tracer_step = 0.2
level_step = 0.04
react_step = 0.25
warming_amount = 60.0

speed_bound = 3.0
hydro_bound = 6.0
species_bound = 2.0
coupling_bound = 0.75

LANES = 128
DRY = 1e30
F32 = jnp.float32


def call(kernel, out_shape, args, specs=None, scratch=(), name=None, mib=40):
    vmem = pl.BlockSpec(memory_space=pltpu.VMEM)
    outs = jax.tree.map(lambda _: vmem, out_shape)
    return pl.pallas_call(
        kernel,
        out_shape=out_shape,
        in_specs=[vmem] * len(args) if specs is None else specs,
        out_specs=outs,
        scratch_shapes=list(scratch),
        compiler_params=pltpu.CompilerParams(vmem_limit_bytes=mib * 1024 * 1024),
        name=name,
    )(*args)


def f32(*shape):
    return jax.ShapeDtypeStruct(shape, F32)


def shift(a, steps, axis):
    return pltpu.roll(a, (-steps) % a.shape[axis], axis)


def minmod(p, r):
    return jnp.maximum(jnp.minimum(p, r), jnp.minimum(jnp.maximum(p, r), 0.0))


def sideways(c, speed, axis):
    d = 0.5 * (shift(c, 1, axis) - c)
    half = minmod(shift(d, -1, axis), d)
    flux = speed * jnp.where(speed > 0.0, c + half, shift(c - half, 1, axis))
    return flux - shift(flux, -1, axis)


def exchange_levels(part):
    return lax.ppermute(part, "lev", [(0, 1), (1, 0)])


def shards(
    potential_warmth,
    saltiness_anomaly,
    zonal_speed,
    meridional_speed,
    marine_indicator,
    species_concentrations,
    coupling_matrix,
    species_guild_number,
    guild_extinction_coefficient,
):
    cols, ntrc, nlev = lax.axis_size("cols"), lax.axis_size("trc"), lax.axis_size("lev")
    D, X, Y = potential_warmth.shape
    T = species_concentrations.shape[0]
    NT = coupling_matrix.shape[0]
    YG = species_concentrations.shape[3]
    assert nlev == 2 and YG == LANES and X % 8 == 0 and Y % 8 == 0 and ntrc % 2 == 0
    assert LANES % D == 0 and D % 8 == 0 and X % (2 * LANES // D) == 0
    H = X if cols > 1 else 0
    XE = X + 2 * H
    W, DX = D * XE, D * X
    G = LANES // D
    XL = XE // G

    def widen(block, dim):
        if H == 0:
            return block
        ahead = [(i, (i + 1) % cols) for i in range(cols)]
        back = [(i, (i - 1) % cols) for i in range(cols)]
        low = lax.ppermute(block, "cols", ahead)
        high = lax.ppermute(block, "cols", back)
        return jnp.concatenate([low, block, high], axis=dim)

    warmth, salt, zonal, merid, marine = (
        widen(jnp.transpose(a, (1, 2, 0)), 0)
        for a in (potential_warmth, saltiness_anomaly, zonal_speed, meridional_speed, marine_indicator)
    )
    species = widen(species_concentrations, 2)
    NP = ntrc // 2
    pairs_apart = [[2 * g + c for g in range(NP)] for c in range(2)]

    UV_ROWS, DENSE_ROWS = XL * Y, XL * Y // 2
    DRY_CODE = -(2**14)
    SCALES = 31

    def top(bound):
        return 2.0 ** math.ceil(math.log2(bound))

    tops = (top(hydro_bound * 1.001), top(speed_bound), top(speed_bound))
    codes = (2**14 - 1, 2**15 - 1, 2**15 - 1)

    def pack(t_any, s_any, u_any, v_any, m_any, c_any, pay_ref, lo_ref, hi_ref, out_ref, held, wet, sems):
        upper = lax.axis_index("lev") == 0
        first = pl.multiple_of(jnp.where(upper, D - 4, 0) * XE, 8)
        copies = [
            pltpu.make_async_copy(a, held.at[i], sems.at[i])
            for i, a in enumerate((t_any, s_any, u_any, v_any))
        ]
        copies.append(pltpu.make_async_copy(m_any, wet, sems.at[4]))
        for t in range(T):
            copies.append(
                pltpu.make_async_copy(
                    c_any.at[t, pl.ds(first, 4 * XE)],
                    out_ref.at[pl.ds(t * 4 * XE, 4 * XE)],
                    sems.at[5 + t],
                )
            )
        for copy in copies:
            copy.start()
        for copy in copies:
            copy.wait()
        t, s = held[0], held[1]
        sea = wet[...] > 0
        density = jnp.where(sea, 0.8 * s - 0.2 * t, 0.0)
        numbers, halves = 0, []
        for i, a in enumerate((density, held[2], held[3])):
            most = jnp.max(jnp.abs(a))
            unit, number = tops[i], 0
            for k in range(1, SCALES + 1):
                fits = most <= tops[i] * 2.0**-k
                unit = jnp.where(fits, tops[i] * 2.0**-k, unit)
                number = jnp.where(fits, k, number)
            code = jnp.floor(jnp.clip(a * (1.0 / unit), -1.0, 1.0) * codes[i] + 0.5).astype(jnp.int32)
            if i == 0:
                code = jnp.where(sea, code, DRY_CODE)
            numbers = numbers + number * 32**i
            code = jnp.concatenate([code[g * XL : (g + 1) * XL] for g in range(G)], axis=2)
            halves.append(code.reshape(XL * Y, LANES))
        density, u, v = halves
        lane = lax.broadcasted_iota(jnp.int32, (XL * Y, LANES), 1)
        density = density * 2 + (lax.shift_right_logical(numbers, lane % 16) & 1)
        rows = jnp.concatenate(
            [u * 65536 + (v & 65535), density[:DENSE_ROWS] * 65536 + (density[DENSE_ROWS:] & 65535)],
            axis=0,
        )
        for g in range(NP):
            pay_ref[g] = rows
        lane = lax.broadcasted_iota(jnp.int32, (Y, LANES), 1)
        for i, a in enumerate((t, s)):
            edge = jnp.zeros((Y, LANES), F32)
            for x in range(XE):
                lo_ref[i * XE + x : i * XE + x + 1] = a[x, 0:1]
                hi_ref[i * XE + x : i * XE + x + 1] = a[x, Y - 1 : Y]
                column = jnp.where(upper, a[x, :, D - 1 : D], a[x, :, 0:1])
                edge = jnp.where(lane == x, column, edge)
            out_ref[4 * T * XE + i * Y : 4 * T * XE + (i + 1) * Y] = edge

    species = species.reshape(T, W, YG)
    payload, lo, hi, outer = call(
        pack,
        (
            jax.ShapeDtypeStruct((NP, UV_ROWS + DENSE_ROWS, LANES), jnp.int32),
            f32(2 * XE, D),
            f32(2 * XE, D),
            f32(4 * T * XE + 2 * Y, LANES),
        ),
        (warmth, salt, zonal, merid, marine, species),
        specs=[pl.BlockSpec(memory_space=pl.ANY)] * 6,
        scratch=(
            pltpu.VMEM((4, XE, Y, D), F32),
            pltpu.VMEM((XE, Y, D), jnp.int32),
            pltpu.SemaphoreType.DMA((5 + T,)),
        ),
        name="pack_ocean",
        mib=60,
    )
    mine = lax.all_to_all(
        payload, "trc", split_axis=0, concat_axis=0, tiled=True, axis_index_groups=pairs_apart
    )
    far_outer = exchange_levels(outer)
    mine, far_outer = lax.optimization_barrier((mine, far_outer))
    other = lax.ppermute(mine, "trc", [(i, i ^ 1) for i in range(ntrc)])

    def plane(ref, i):
        return ref[i * XE : (i + 1) * XE]

    def dense(raw):
        return jnp.where(raw < 0.5 * DRY, raw, 0.0)

    def faces(raw, u, v, before):
        wet = jnp.where(raw < 0.5 * DRY, 1.0, 0.0)
        d = dense(raw)
        total = before + d
        p = buoyancy * (total - 0.5 * d)
        result = []
        for axis, a in enumerate((u, v)):
            mask = wet * shift(wet, 1, axis)
            lap = shift(a, 1, 0) + shift(a, -1, 0) + shift(a, 1, 1) + shift(a, -1, 1) - 4.0 * a
            push = viscosity * lap - (shift(p, 1, axis) - p)
            result.append((mask * (a + marine_advance * push), mask))
        return total, result

    def unpack(a_ref, b_ref, uv_ref, mask_ref, l_ref, f_ref):
        core = lax.axis_index("trc") % 2
        lane = lax.broadcasted_iota(jnp.int32, (YG, LANES), 1)

        def words(at):
            rows = []
            for g in range(NP):
                a, b = a_ref[g, at : at + Y], b_ref[g, at : at + Y]
                rows += [jnp.where(core == 0, a, b), jnp.where(core == 0, b, a)]
            return jnp.concatenate(rows, axis=0)

        def high(w):
            return lax.shift_right_arithmetic(w, 16)

        def low(w):
            return lax.shift_right_arithmetic(lax.shift_left(w, 16), 16)

        bits = high(words(UV_ROWS)) & 1
        numbers = jnp.sum(jnp.where(lane < 16, lax.shift_left(bits, lane % 16), 0), axis=1, keepdims=True)
        units = []
        for i in range(3):
            number = lax.shift_right_logical(numbers, 5 * i) & 31
            unit = jnp.full((YG, 1), tops[i] / codes[i], F32)
            for b in range(5):
                unit = jnp.where(lax.shift_right_logical(number, b) & 1 > 0, unit * 2.0 ** -(2**b), unit)
            units.append(unit)

        def put(f, x, a):
            turned = a.T
            for g in range(G):
                f_ref[f, pl.ds(x + g * XL, D, stride=XE), :] = turned[g * D : (g + 1) * D]

        for x in range(XL):
            w = words(x * Y)
            put(1, x, high(w).astype(F32) * units[1])
            put(2, x, low(w).astype(F32) * units[2])
            if x < XL // 2:
                w = words(UV_ROWS + x * Y)
                for xx, code in ((x, high(w)), (x + XL // 2, low(w))):
                    code = lax.shift_right_arithmetic(code, 1)
                    put(0, xx, jnp.where(code == DRY_CODE, DRY, code.astype(F32) * units[0]))

        def field(f, k):
            return f_ref[f, pl.ds(pl.multiple_of(k * XE, 8), XE)]

        def one(k, carry):
            total, sums = carry
            total, new = faces(field(0, k), field(1, k), field(2, k), total)
            for i, (speed, mask) in enumerate(new):
                uv_ref[i, k] = speed
                mask_ref[i, k] = mask
            parts = (new[0][0], new[1][0], new[0][1], new[1][1])
            return total, tuple(a + b for a, b in zip(sums, parts))

        zero = jnp.zeros((XE, YG), F32)
        total, sums = lax.fori_loop(0, D, one, (zero, (zero,) * 4), unroll=16)
        for i, a in enumerate((total,) + sums):
            l_ref[i * XE : (i + 1) * XE] = a
        first = jnp.where(lax.axis_index("lev") == 0, D - 2, 0)
        for f in range(3):
            for k in range(2):
                at = (5 + 2 * f + k) * XE
                l_ref[at : at + XE] = field(f, first + k)

    near_uv, masks, own_levels = call(
        unpack,
        (f32(2, D, XE, YG), f32(2, D, XE, YG), f32(11 * XE, YG)),
        (mine, other),
        scratch=(pltpu.VMEM((3, W, YG), F32),),
        name="unpack_ocean",
    )
    far_levels = exchange_levels(own_levels)

    def speeds(n_ref, m_ref, o_ref, r_ref, uv_ref, fv_ref):
        lev = lax.axis_index("lev")
        above = jnp.where(lev > 0, plane(r_ref, 0), 0.0)
        sum_here = plane(o_ref, 0)

        def pushes(a):
            return [-marine_advance * buoyancy * (shift(a, 1, i) - a) for i in range(2)]

        def spread_out(u, v):
            return u - shift(u, -1, 0) + v - shift(v, -1, 1)

        def far(e, total):
            k = e % 2 if e < 2 else e - D - 2
            total, new = faces(plane(r_ref, 5 + k), plane(r_ref, 7 + k), plane(r_ref, 9 + k), total)
            for i in range(2):
                uv_ref[i, e] = new[i][0]
            return total

        total = above - dense(plane(r_ref, 5)) - dense(plane(r_ref, 6))
        for e in (0, 1):
            total = far(e, total)
        total = above + sum_here
        for e in (D + 2, D + 3):
            total = far(e, total)

        push = pushes(sum_here)
        lower = [plane(r_ref, 1 + i) + plane(r_ref, 3 + i) * push[i] for i in range(2)]
        below = jnp.where(lev < nlev - 1, spread_out(*lower), 0.0)

        def divergence(e):
            return spread_out(uv_ref[0, e], uv_ref[1, e])

        fv_ref[D + 2] = below
        fv_ref[D + 3] = below - divergence(D + 2)
        fv_ref[D + 4] = below - divergence(D + 2) - divergence(D + 3)
        push = pushes(above)

        def climb(j, total):
            k = D - 1 - j
            new = [n_ref[i, k] + m_ref[i, k] * push[i] for i in range(2)]
            for i in range(2):
                uv_ref[i, k + 2] = new[i]
            total = total + spread_out(*new)
            fv_ref[k + 2] = total
            return total

        total = lax.fori_loop(0, D, climb, below, unroll=16)
        fv_ref[2] = jnp.where(lev == 0, 0.0, total)
        for e in (1, 0):
            total = total + divergence(e)
            fv_ref[e] = total

    uv, fv = call(
        speeds,
        (f32(2, D + 4, XE, YG), f32(D + 5, XE, YG)),
        (near_uv, masks, own_levels, far_levels),
        name="face_speeds",
    )

    def advect(c_ref, h_ref, uv_ref, fv_ref, adv_ref, msg_ref, pad, mid_pad, sem):
        lev = lax.axis_index("lev")
        copy = pltpu.make_async_copy(c_ref, pad.at[:, pl.ds(4 * XE, W)], sem)
        copy.start()
        for t in range(T):
            outer = h_ref[t * 4 * XE : (t + 1) * 4 * XE]
            pad[t, 0 : 4 * XE] = jnp.where(lev > 0, outer, 0.0)
            pad[t, (D + 4) * XE :] = jnp.where(lev < nlev - 1, outer, 0.0)
        copy.wait()

        def step(src, dst, first, count):
            def cells(e):
                return src[:, pl.ds(pl.multiple_of((e + 2) * XE, 8), XE)]

            def half_slope(lo, mid, hi):
                return minmod(0.5 * (mid - lo), 0.5 * (hi - mid))

            def down(e, up_cell, lo, mid, hi):
                half = half_slope(lo, mid, hi)
                w = level_step * fv_ref[e]
                return w * jnp.where(w > 0.0, up_cell, mid - half), mid + half

            c0, c1, c2, c3 = (cells(first + k) for k in range(-2, 2))
            up_cell = c1 + half_slope(c0, c1, c2)
            flux, up_cell = down(first, up_cell, c1, c2, c3)

            def one(i, carry):
                e = first + i
                mid, hi, flux, up_cell = carry
                nxt = cells(e + 2)
                flux_next, up_next = down(e + 1, up_cell, mid, hi, nxt)
                u, v = tracer_step * uv_ref[0, e], tracer_step * uv_ref[1, e]
                new = mid - (sideways(mid, u[None], 1) + sideways(mid, v[None], 2) + (flux_next - flux))
                dst[:, pl.ds(pl.multiple_of((e + 2) * XE, 8), XE)] = new
                return hi, nxt, flux_next, up_next

            lax.fori_loop(0, count, one, (c2, c3, flux, up_cell), unroll=count // 4)

        step(pad, mid_pad, 0, D + 4)
        step(mid_pad, pad, 2, D)
        for w in range(DX // LANES):
            turned = []
            for t in range(T):
                rows = []
                for x in range(w * G, (w + 1) * G):
                    rows.append(pad[t, pl.ds(4 * XE + H + x, D, stride=XE), :])
                rows = jnp.concatenate(rows, axis=0)
                adv_ref[t, w * LANES : (w + 1) * LANES] = rows
                turned.append(rows.T)
            for d in range(ntrc):
                rows = [turned[t][d * Y : (d + 1) * Y] for t in range(T)]
                msg_ref[d, :, w * LANES : (w + 1) * LANES] = jnp.concatenate(rows, axis=0).astype(
                    jnp.bfloat16
                )

    vmem = pl.BlockSpec(memory_space=pltpu.VMEM)
    advected, message = call(
        advect,
        (f32(T, DX, YG), jax.ShapeDtypeStruct((ntrc, T * Y, DX), jnp.bfloat16)),
        (species, far_outer, uv, fv),
        specs=[pl.BlockSpec(memory_space=pl.ANY)] + [vmem] * 3,
        scratch=(pltpu.VMEM((T, (D + 8) * XE, YG), F32),) * 2 + (pltpu.SemaphoreType.DMA(()),),
        name="advect_tracers",
    )
    message, lo, hi = lax.optimization_barrier((message, lo, hi))
    gathered = lax.all_to_all(message, "trc", split_axis=0, concat_axis=0, tiled=True)
    ring = [(i, (i + 1) % ntrc) for i in range(ntrc)]
    south = lax.ppermute(hi, "trc", ring)
    north = lax.ppermute(lo, "trc", [(b, a) for a, b in ring])
    gathered, south, north = lax.optimization_barrier((gathered, south, north))

    def ocean(
        t_ref, s_ref, uv_ref, fv_ref, l_ref, so_ref, no_ref, sa_ref, wa_ref, ua_ref, va_ref, turn
    ):
        me, lev = lax.axis_index("trc"), lax.axis_index("lev")
        for x in range(XE):
            def level_rows(ref, first):
                return ref[pl.ds(first * XE + x, D, stride=XE), :]

            turn[0, x] = level_rows(uv_ref.at[0], 2).T
            turn[1, x] = level_rows(uv_ref.at[1], 2).T
            turn[2, x] = level_rows(fv_ref, 2).T
            turn[3, x] = level_rows(fv_ref, 3).T
        here = pl.ds(pl.multiple_of(me * Y, 8), Y)
        past = pl.ds(pl.multiple_of(lax.rem(me + ntrc - 1, ntrc) * Y, 8), Y)
        u, v, w, w_next = (turn[i, :, here] for i in range(4))
        v_south = turn[1, :, past][:, Y - 1 : Y]
        level = lax.broadcasted_iota(jnp.int32, (XE, Y, D), 2)
        row = lax.broadcasted_iota(jnp.int32, (XE, Y, D), 1)

        def east(a):
            return jnp.concatenate([a[1:], a[:1]], axis=0)

        def west(a):
            return jnp.concatenate([a[-1:], a[:-1]], axis=0)

        def donor(speed, near, far):
            return jnp.maximum(speed, 0.0) * near + jnp.minimum(speed, 0.0) * far

        def advance(c, i):
            so = jnp.stack([so_ref[i * XE + x : i * XE + x + 1] for x in range(XE)])
            no = jnp.stack([no_ref[i * XE + x : i * XE + x + 1] for x in range(XE)])
            tile = l_ref[4 * T * XE + i * Y : 4 * T * XE + (i + 1) * Y]
            edge = jnp.stack([tile[:, x : x + 1] for x in range(XE)])
            wide = jnp.concatenate([c, jnp.zeros((XE, Y, LANES - D), F32)], axis=2) if D < LANES else c
            upper = shift(wide, -1, 2)[:, :, :D]
            upper = jnp.where(level == 0, jnp.where(lev > 0, edge, 0.0), upper)
            lower = shift(wide, 1, 2)[:, :, :D]
            lower = jnp.where(level == D - 1, jnp.where(lev < nlev - 1, edge, 0.0), lower)
            fe = donor(u, c, east(c))
            fn = donor(v, c, jnp.where(row == Y - 1, no, shift(c, 1, 1)))
            fn_south = jnp.where(row == 0, donor(v_south, so, c[:, 0:1]), shift(fn, -1, 1))
            fall = donor(w_next, c, lower) - donor(w, upper, c)
            return c - marine_advance * ((fe - west(fe)) + (fn - fn_south) + fall)

        sa_ref[...] = advance(s_ref[...], 1)[H : H + X]
        wa_ref[...] = advance(t_ref[...], 0)[H : H + X]
        ua_ref[...] = u[H : H + X]
        va_ref[...] = v[H : H + X]

    saltiness_final, warmth_moved, zonal_speed_final, meridional_speed_final = call(
        ocean,
        (f32(X, Y, D),) * 4,
        (
            warmth,
            salt,
            uv.reshape(2, (D + 4) * XE, YG),
            fv.reshape((D + 5) * XE, YG),
            far_outer,
            south,
            north,
        ),
        scratch=(pltpu.VMEM((4, XE, YG, D), F32),),
        name="own_ocean",
    )

    speed_most = speed_bound + marine_advance * (
        2 * buoyancy * hydro_bound * D * nlev + viscosity * 8 * speed_bound
    )
    growth = 1 + 4 * tracer_step * speed_most + 2 * level_step * (4 * speed_most * D * nlev)
    react_most = NT * coupling_bound * species_bound * growth**2
    unit = 2.0 ** max(0, math.ceil(math.log2(react_most / 65504.0)))

    def spread_columns(c_ref, o_ref):
        n = NT * Y

        def pick(shape, along):
            wide, narrow = (lax.broadcasted_iota(jnp.int32, shape, d) for d in (along, 1 - along))
            return jnp.where(wide // Y == narrow, 1.0, 0.0).astype(jnp.bfloat16)

        tall = jnp.dot(pick((n, NT), 0), c_ref[...], preferred_element_type=F32)
        full = jnp.dot(
            tall.astype(jnp.bfloat16), pick((NT, n), 1), preferred_element_type=F32
        )
        row, lane = (lax.broadcasted_iota(jnp.int32, (n, n), d) for d in (0, 1))
        o_ref[...] = jnp.where(row % Y == lane % Y, full, 0.0).astype(jnp.bfloat16)

    spread = call(
        spread_columns,
        jax.ShapeDtypeStruct((NT * Y, NT * Y), jnp.bfloat16),
        (coupling_matrix,),
        name="spread_coupling",
    )
    flat_tracers = gathered.reshape(NT * Y, DX)
    reaction = jnp.dot(spread, flat_tracers, preferred_element_type=F32)
    reaction = (reaction * (1.0 / unit)).astype(jnp.float16).reshape(ntrc, T * Y, DX)
    returned = lax.all_to_all(reaction, "trc", split_axis=0, concat_axis=0, tiled=True)

    def shade(x_ref, g_ref, k_ref, att_ref, cum_ref):
        att = jnp.zeros((Y, DX), F32)
        for d in range(ntrc):
            rows = x_ref[d].astype(F32)
            for t in range(T):
                att = att + k_ref[g_ref[d * T + t]] * rows[t * Y : (t + 1) * Y]
        att_ref[...] = att
        lane = lax.broadcasted_iota(jnp.int32, (Y, DX), 1)
        total = att
        width = 1
        while width < D:
            total = total + jnp.where(lane % D < width, 0.0, shift(total, -width, 1))
            width *= 2
        cum_ref[...] = total

    smem = pl.BlockSpec(memory_space=pltpu.SMEM)
    attenuation, shaded = call(
        shade,
        (f32(Y, DX), f32(Y, DX)),
        (gathered, species_guild_number, guild_extinction_coefficient),
        specs=[vmem, smem, smem],
        name="shade",
    )
    far_shade = exchange_levels(shaded)

    def heat(att_ref, cum_ref, r_ref, w_ref, m_ref, o_ref):
        att = att_ref[...]
        path = cum_ref[...] - att
        caught = 1.0 - jnp.exp(-att)
        lev = lax.axis_index("lev")
        for x in range(X):
            at = slice(x * D, (x + 1) * D)
            above = jnp.where(lev > 0, r_ref[:, (x + 1) * D - 1 : (x + 1) * D], 0.0)
            absorbed = jnp.exp(-(above + path[:, at])) * caught[:, at]
            o_ref[x] = w_ref[x] + warming_amount * (m_ref[x].astype(F32) * absorbed)

    warmth_final = call(
        heat,
        f32(X, Y, D),
        (attenuation, shaded, far_shade, warmth_moved, jnp.transpose(marine_indicator, (1, 2, 0))),
        name="heat",
    )

    def finish(r_ref, a_ref, o_ref):
        for t in range(T):
            for w in range(DX // LANES):
                rows = [
                    r_ref[d, t * Y : (t + 1) * Y, w * LANES : (w + 1) * LANES] for d in range(ntrc)
                ]
                turned = (react_step * unit) * jnp.concatenate(rows, axis=0).T
                for g in range(G):
                    at = pl.ds(w * G + g, D, stride=X)
                    rows = slice(g * D, (g + 1) * D)
                    o_ref[t, at, :] = a_ref[t, w * LANES + g * D : w * LANES + (g + 1) * D] + turned[rows]

    species_final = call(
        finish, f32(T, DX, YG), (returned.astype(F32), advected), name="finish_tracers"
    )
    ocean_outputs = (warmth_final, saltiness_final, zonal_speed_final, meridional_speed_final)
    ocean_outputs = tuple(jnp.transpose(a, (2, 0, 1)) for a in ocean_outputs)
    return ocean_outputs + (species_final.reshape(T, D, X, YG),)


def solution(mesh):
    ocean = P("lev", "cols", "trc")
    in_specs = (ocean,) * 5 + (P("trc", "lev", "cols", None), P(), P(), P())
    out_specs = (ocean,) * 4 + (P("trc", "lev", "cols", None),)
    return jax.shard_map(shards, mesh=mesh, in_specs=in_specs, out_specs=out_specs, check_vma=False)
```

```python
import math

import jax
import jax.numpy as jnp
from jax import lax
from jax.experimental import pallas as pl
from jax.experimental.pallas import tpu as pltpu
from jax.sharding import PartitionSpec as P

viscosity = 0.2
buoyancy = 0.25
marine_advance = 0.05
tracer_step = 0.2
level_step = 0.04
react_step = 0.25
warming_amount = 60.0

speed_bound = 3.0
hydro_bound = 6.0
species_bound = 2.0
coupling_bound = 0.75

LANES = 128
DRY = 1e30
F32 = jnp.float32


def call(kernel, out_shape, args, specs=None, scratch=(), name=None, mib=16, outs=None):
    vmem = pl.BlockSpec(memory_space=pltpu.VMEM)
    outs = jax.tree.map(lambda _: vmem, out_shape) if outs is None else outs
    return pl.pallas_call(
        kernel,
        out_shape=out_shape,
        in_specs=[vmem] * len(args) if specs is None else specs,
        out_specs=outs,
        scratch_shapes=list(scratch),
        compiler_params=pltpu.CompilerParams(vmem_limit_bytes=mib * 1024 * 1024),
        name=name,
    )(*args)


def f32(*shape):
    return jax.ShapeDtypeStruct(shape, F32)


def shift(a, steps, axis):
    return pltpu.roll(a, (-steps) % a.shape[axis], axis)


def minmod(p, r):
    return jnp.maximum(jnp.minimum(p, r), jnp.minimum(jnp.maximum(p, r), 0.0))


def sideways(c, speed, axis):
    d = 0.5 * (shift(c, 1, axis) - c)
    half = minmod(shift(d, -1, axis), d)
    flux = speed * jnp.where(speed > 0.0, c + half, shift(c - half, 1, axis))
    return flux - shift(flux, -1, axis)


def exchange_levels(part):
    return lax.ppermute(part, "lev", [(0, 1), (1, 0)])


def shards(
    potential_warmth,
    saltiness_anomaly,
    zonal_speed,
    meridional_speed,
    marine_indicator,
    species_concentrations,
    coupling_matrix,
    species_guild_number,
    guild_extinction_coefficient,
):
    cols, ntrc, nlev = lax.axis_size("cols"), lax.axis_size("trc"), lax.axis_size("lev")
    D, X, Y = potential_warmth.shape
    T = species_concentrations.shape[0]
    NT = coupling_matrix.shape[0]
    YG = species_concentrations.shape[3]
    assert nlev == 2 and YG == LANES and X % 8 == 0 and Y % 8 == 0 and ntrc % 2 == 0
    assert LANES % D == 0 and D % 8 == 0 and X % (2 * LANES // D) == 0
    H = X if cols > 1 else 0
    XE = X + 2 * H
    W, DX = D * XE, D * X
    G = LANES // D
    XL = XE // G
    RL = LANES // X

    def widen(block, dim):
        if H == 0:
            return block
        ahead = [(i, (i + 1) % cols) for i in range(cols)]
        back = [(i, (i - 1) % cols) for i in range(cols)]
        low = lax.ppermute(block, "cols", ahead)
        high = lax.ppermute(block, "cols", back)
        return jnp.concatenate([low, block, high], axis=dim)

    warmth, salt, zonal, merid, marine = (
        widen(jnp.transpose(a, (1, 2, 0)), 0)
        for a in (potential_warmth, saltiness_anomaly, zonal_speed, meridional_speed, marine_indicator)
    )
    species = widen(species_concentrations, 2)
    NP = ntrc // 2
    pairs_apart = [[2 * g + c for g in range(NP)] for c in range(2)]

    UV_ROWS, DENSE_ROWS = XL * Y, XL * Y // 2
    DRY_CODE = -(2**14)
    SCALES = 31

    def top(bound):
        return 2.0 ** math.ceil(math.log2(bound))

    tops = (top(hydro_bound * 1.001), top(speed_bound), top(speed_bound))
    codes = (2**14 - 1, 2**15 - 1, 2**15 - 1)

    def pack(t_any, s_any, u_any, v_any, m_any, c_any, pay_ref, lo_ref, hi_ref, out_ref, held, wet, sems):
        upper = lax.axis_index("lev") == 0
        first = pl.multiple_of(jnp.where(upper, D - 4, 0) * XE, 8)
        copies = [
            pltpu.make_async_copy(a, held.at[i], sems.at[i])
            for i, a in enumerate((t_any, s_any, u_any, v_any))
        ]
        copies.append(pltpu.make_async_copy(m_any, wet, sems.at[4]))
        for t in range(T):
            copies.append(
                pltpu.make_async_copy(
                    c_any.at[t, pl.ds(first, 4 * XE)],
                    out_ref.at[pl.ds(t * 4 * XE, 4 * XE)],
                    sems.at[5 + t],
                )
            )
        for copy in copies:
            copy.start()
        for copy in copies:
            copy.wait()
        t, s = held[0], held[1]
        sea = wet[...] > 0
        density = jnp.where(sea, 0.8 * s - 0.2 * t, 0.0)
        numbers, halves = 0, []
        for i, a in enumerate((density, held[2], held[3])):
            most = jnp.max(jnp.abs(a))
            unit, number = tops[i], 0
            for k in range(1, SCALES + 1):
                fits = most <= tops[i] * 2.0**-k
                unit = jnp.where(fits, tops[i] * 2.0**-k, unit)
                number = jnp.where(fits, k, number)
            code = jnp.floor(jnp.clip(a * (1.0 / unit), -1.0, 1.0) * codes[i] + 0.5).astype(jnp.int32)
            if i == 0:
                code = jnp.where(sea, code, DRY_CODE)
            numbers = numbers + number * 32**i
            code = jnp.concatenate([code[g * XL : (g + 1) * XL] for g in range(G)], axis=2)
            halves.append(code.reshape(XL * Y, LANES))
        density, u, v = halves
        lane = lax.broadcasted_iota(jnp.int32, (XL * Y, LANES), 1)
        density = density * 2 + (lax.shift_right_logical(numbers, lane % 16) & 1)
        rows = jnp.concatenate(
            [u * 65536 + (v & 65535), density[:DENSE_ROWS] * 65536 + (density[DENSE_ROWS:] & 65535)],
            axis=0,
        )
        for g in range(NP):
            pay_ref[g] = rows
        lane = lax.broadcasted_iota(jnp.int32, (Y, LANES), 1)
        for i, a in enumerate((t, s)):
            edge = jnp.zeros((Y, LANES), F32)
            for x in range(XE):
                lo_ref[i * XE + x : i * XE + x + 1] = a[x, 0:1]
                hi_ref[i * XE + x : i * XE + x + 1] = a[x, Y - 1 : Y]
                column = jnp.where(upper, a[x, :, D - 1 : D], a[x, :, 0:1])
                edge = jnp.where(lane == x, column, edge)
            out_ref[4 * T * XE + i * Y : 4 * T * XE + (i + 1) * Y] = edge

    species = species.reshape(T, W, YG)
    payload, lo, hi, outer = call(
        pack,
        (
            jax.ShapeDtypeStruct((NP, UV_ROWS + DENSE_ROWS, LANES), jnp.int32),
            f32(2 * XE, D),
            f32(2 * XE, D),
            f32(4 * T * XE + 2 * Y, LANES),
        ),
        (warmth, salt, zonal, merid, marine, species),
        specs=[pl.BlockSpec(memory_space=pl.ANY)] * 6,
        scratch=(
            pltpu.VMEM((4, XE, Y, D), F32),
            pltpu.VMEM((XE, Y, D), jnp.int32),
            pltpu.SemaphoreType.DMA((5 + T,)),
        ),
        name="pack_ocean",
        mib=60,
    )
    mine = lax.all_to_all(
        payload, "trc", split_axis=0, concat_axis=0, tiled=True, axis_index_groups=pairs_apart
    )
    far_outer = exchange_levels(outer)


    def rows(k, n=XE):
        return pl.ds(pl.multiple_of(k * XE, 8), n)

    def widen_levels(c_ref, h_ref, pad, sem):
        lev = lax.axis_index("lev")
        copy = pltpu.make_async_copy(c_ref, pad.at[:, pl.ds(4 * XE, W)], sem)
        copy.start()
        for t in range(T):
            outer = h_ref[t * 4 * XE : (t + 1) * 4 * XE]
            pad[t, 0 : 4 * XE] = jnp.where(lev > 0, outer, 0.0)
            pad[t, (D + 4) * XE :] = jnp.where(lev < nlev - 1, outer, 0.0)
        copy.wait()

    pad = call(
        widen_levels,
        f32(T, (D + 8) * XE, YG),
        (species, far_outer),
        specs=[pl.BlockSpec(memory_space=pl.ANY), pl.BlockSpec(memory_space=pltpu.VMEM)],
        scratch=(pltpu.SemaphoreType.DMA(()),),
        name="widen_levels",
    )
    mine, pad = lax.optimization_barrier((mine, pad))
    other = lax.ppermute(mine, "trc", [(i, i ^ 1) for i in range(ntrc)])

    def plane(ref, i):
        return ref[i * XE : (i + 1) * XE]

    def dense(raw):
        return jnp.where(raw < 0.5 * DRY, raw, 0.0)

    def faces(raw, u, v, before):
        wet = jnp.where(raw < 0.5 * DRY, 1.0, 0.0)
        d = dense(raw)
        total = before + d
        p = buoyancy * (total - 0.5 * d)
        result = []
        for axis, a in enumerate((u, v)):
            mask = wet * shift(wet, 1, axis)
            lap = shift(a, 1, 0) + shift(a, -1, 0) + shift(a, 1, 1) + shift(a, -1, 1) - 4.0 * a
            push = viscosity * lap - (shift(p, 1, axis) - p)
            result.append((mask * (a + marine_advance * push), mask))
        return total, result

    def unpack(a_ref, b_ref, uv_ref, mask_ref, l_ref, f_ref):
        core = lax.axis_index("trc") % 2
        lane = lax.broadcasted_iota(jnp.int32, (YG, LANES), 1)

        def words(at):
            rows = []
            for g in range(NP):
                a, b = a_ref[g, at : at + Y], b_ref[g, at : at + Y]
                rows += [jnp.where(core == 0, a, b), jnp.where(core == 0, b, a)]
            return jnp.concatenate(rows, axis=0)

        def high(w):
            return lax.shift_right_arithmetic(w, 16)

        def low(w):
            return lax.shift_right_arithmetic(lax.shift_left(w, 16), 16)

        bits = high(words(UV_ROWS)) & 1
        numbers = jnp.sum(jnp.where(lane < 16, lax.shift_left(bits, lane % 16), 0), axis=1, keepdims=True)
        units = []
        for i in range(3):
            number = lax.shift_right_logical(numbers, 5 * i) & 31
            unit = jnp.full((YG, 1), tops[i] / codes[i], F32)
            for b in range(5):
                unit = jnp.where(lax.shift_right_logical(number, b) & 1 > 0, unit * 2.0 ** -(2**b), unit)
            units.append(unit)

        def put(f, x, a):
            turned = a.T
            for g in range(G):
                f_ref[f, pl.ds(x + g * XL, D, stride=XE), :] = turned[g * D : (g + 1) * D]

        for x in range(XL):
            w = words(x * Y)
            put(1, x, high(w).astype(F32) * units[1])
            put(2, x, low(w).astype(F32) * units[2])
            if x < XL // 2:
                w = words(UV_ROWS + x * Y)
                for xx, code in ((x, high(w)), (x + XL // 2, low(w))):
                    code = lax.shift_right_arithmetic(code, 1)
                    put(0, xx, jnp.where(code == DRY_CODE, DRY, code.astype(F32) * units[0]))

        def field(f, k):
            return f_ref[f, pl.ds(pl.multiple_of(k * XE, 8), XE)]

        def one(k, carry):
            total, sums = carry
            total, new = faces(field(0, k), field(1, k), field(2, k), total)
            for i, (speed, mask) in enumerate(new):
                uv_ref[i, k] = speed
                mask_ref[i, k] = mask
            parts = (new[0][0], new[1][0], new[0][1], new[1][1])
            return total, tuple(a + b for a, b in zip(sums, parts))

        zero = jnp.zeros((XE, YG), F32)
        total, sums = lax.fori_loop(0, D, one, (zero, (zero,) * 4), unroll=16)
        for i, a in enumerate((total,) + sums):
            l_ref[i * XE : (i + 1) * XE] = a
        first = jnp.where(lax.axis_index("lev") == 0, D - 2, 0)
        for f in range(3):
            for k in range(2):
                at = (5 + 2 * f + k) * XE
                l_ref[at : at + XE] = field(f, first + k)

    near_uv, masks, own_levels = call(
        unpack,
        (f32(2, D, XE, YG), f32(2, D, XE, YG), f32(11 * XE, YG)),
        (mine, other),
        scratch=(pltpu.VMEM((3, W, YG), F32),),
        name="unpack_ocean",
    )
    own_levels, pad = lax.optimization_barrier((own_levels, pad))
    far_levels = exchange_levels(own_levels)

    def half_slope(lo, mid, hi):
        return minmod(0.5 * (mid - lo), 0.5 * (hi - mid))

    def edges(c, axis):
        d = 0.5 * (shift(c, 1, axis) - c)
        half = minmod(shift(d, -1, axis), d)
        return c + half, shift(c - half, 1, axis)

    def slopes(pad, side):
        def one(k, carry):
            lo, mid = carry
            hi = pad[:, rows(k + 2)]
            half = half_slope(lo, mid, hi)
            values = edges(mid, 1) + edges(mid, 2) + (mid + half, mid - half)
            for i, a in enumerate(values):
                side[i, :, rows(k)] = a
            return mid, hi

        count = D + 6
        first = (pad[:, 0:XE], pad[:, XE : 2 * XE])
        lax.fori_loop(0, count, one, first, unroll=count // 5)

    side = call(slopes, f32(6, T, (D + 6) * XE, YG), (pad,), name="first_slopes")
    far_levels, side = lax.optimization_barrier((far_levels, side))

    def speeds(n_ref, m_ref, o_ref, r_ref, uv_ref, fv_ref):
        lev = lax.axis_index("lev")
        above = jnp.where(lev > 0, plane(r_ref, 0), 0.0)
        sum_here = plane(o_ref, 0)

        def pushes(a):
            return [-marine_advance * buoyancy * (shift(a, 1, i) - a) for i in range(2)]

        def spread_out(u, v):
            return u - shift(u, -1, 0) + v - shift(v, -1, 1)

        def far(e, total):
            k = e % 2 if e < 2 else e - D - 2
            total, new = faces(plane(r_ref, 5 + k), plane(r_ref, 7 + k), plane(r_ref, 9 + k), total)
            for i in range(2):
                uv_ref[i, e] = new[i][0]
            return total

        total = above - dense(plane(r_ref, 5)) - dense(plane(r_ref, 6))
        for e in (0, 1):
            total = far(e, total)
        total = above + sum_here
        for e in (D + 2, D + 3):
            total = far(e, total)

        push = pushes(sum_here)
        lower = [plane(r_ref, 1 + i) + plane(r_ref, 3 + i) * push[i] for i in range(2)]
        below = jnp.where(lev < nlev - 1, spread_out(*lower), 0.0)

        def divergence(e):
            return spread_out(uv_ref[0, e], uv_ref[1, e])

        fv_ref[D + 2] = below
        fv_ref[D + 3] = below - divergence(D + 2)
        fv_ref[D + 4] = below - divergence(D + 2) - divergence(D + 3)
        push = pushes(above)

        def climb(j, total):
            k = D - 1 - j
            new = [n_ref[i, k] + m_ref[i, k] * push[i] for i in range(2)]
            for i in range(2):
                uv_ref[i, k + 2] = new[i]
            total = total + spread_out(*new)
            fv_ref[k + 2] = total
            return total

        total = lax.fori_loop(0, D, climb, below, unroll=16)
        fv_ref[2] = jnp.where(lev == 0, 0.0, total)
        for e in (1, 0):
            total = total + divergence(e)
            fv_ref[e] = total

    uv, fv = call(
        speeds,
        (f32(2, D + 4, XE, YG), f32(D + 5, XE, YG)),
        (near_uv, masks, own_levels, far_levels),
        name="face_speeds",
    )

    def advect(pad, side, uv_ref, fv_ref, adv_ref, msg_any, mid_pad, held, sems):
        def speeds_at(e):
            return tracer_step * uv_ref[0, e][None], tracer_step * uv_ref[1, e][None]

        def fall(e, up, low):
            w = level_step * fv_ref[e]
            return w * jnp.where(w > 0.0, up, low)

        def first_step(e, flux):
            k = rows(e + 1)
            flux_next = fall(e + 1, side[4, :, k], side[5, :, rows(e + 2)])
            change = flux_next - flux
            for i, speed in enumerate(speeds_at(e)):
                f = speed * jnp.where(speed > 0.0, side[2 * i, :, k], side[2 * i + 1, :, k])
                change = change + (f - shift(f, -1, i + 1))
            mid_pad[:, rows(e)] = pad[:, rows(e + 2)] - change
            return flux_next

        flux = fall(0, side[4, :, rows(0)], side[5, :, rows(1)])
        lax.fori_loop(0, D + 4, first_step, flux, unroll=(D + 4) // 4)

        def second_step(k, carry):
            mid, hi, up, flux = carry
            nxt = mid_pad[:, rows(k + 4)]
            half = half_slope(mid, hi, nxt)
            flux_next = fall(k + 3, up, hi - half)
            u, v = speeds_at(k + 2)
            change = sideways(mid, u, 1) + sideways(mid, v, 2) + (flux_next - flux)
            adv_ref[:, pl.ds(pl.multiple_of(k * X, 8), X)] = (mid - change)[:, H : H + X]
            return hi, nxt, hi + half, flux_next

        c = [mid_pad[:, rows(k)] for k in range(4)]
        half = half_slope(c[1], c[2], c[3])
        flux = fall(2, c[1] + half_slope(c[0], c[1], c[2]), c[2] - half)
        def sending(w):
            here = pl.ds(pl.multiple_of(w * LANES, LANES), LANES)
            return pltpu.make_async_copy(held.at[w], msg_any.at[:, :, here], sems.at[w])

        def turn(w):
            here = pl.ds(pl.multiple_of(w * LANES, LANES), LANES)
            turned = [adv_ref[t, here].T for t in range(T)]
            for d in range(ntrc):
                there = [turned[t][d * Y : (d + 1) * Y] for t in range(T)]
                held[w, d] = jnp.concatenate(there, axis=0).astype(jnp.bfloat16)
            sending(w).start()

        def block(w, carry):
            for k in range(RL):
                carry = second_step(w * RL + k, carry)
            return carry

        count = DX // LANES
        lax.fori_loop(0, count, block, (c[2], c[3], c[2] + half, flux))
        for w in range(count):
            turn(w)
        for w in range(count):
            sending(w).wait()

    vmem = pl.BlockSpec(memory_space=pltpu.VMEM)
    advected, message = call(
        advect,
        (f32(T, DX, YG), pltpu.HBM((ntrc, T * Y, DX), jnp.bfloat16)),
        (pad, side, uv, fv),
        scratch=(
            pltpu.VMEM((T, (D + 4) * XE, YG), F32),
            pltpu.VMEM((DX // LANES, ntrc, T * Y, LANES), jnp.bfloat16),
            pltpu.SemaphoreType.DMA((DX // LANES,)),
        ),
        outs=(vmem, pl.BlockSpec(memory_space=pltpu.HBM)),
        name="advect_tracers",
    )
    message, lo, hi = lax.optimization_barrier((message, lo, hi))
    gathered = lax.all_to_all(message, "trc", split_axis=0, concat_axis=0, tiled=True)
    ring = [(i, (i + 1) % ntrc) for i in range(ntrc)]
    south = lax.ppermute(hi, "trc", ring)
    north = lax.ppermute(lo, "trc", [(b, a) for a, b in ring])
    gathered, south, north = lax.optimization_barrier((gathered, south, north))

    def ocean(
        t_ref, s_ref, uv_ref, fv_ref, l_ref, so_ref, no_ref, sa_ref, wa_ref, ua_ref, va_ref, turn
    ):
        me, lev = lax.axis_index("trc"), lax.axis_index("lev")
        for x in range(XE):
            def level_rows(ref, first):
                return ref[pl.ds(first * XE + x, D, stride=XE), :]

            turn[0, x] = level_rows(uv_ref.at[0], 2).T
            turn[1, x] = level_rows(uv_ref.at[1], 2).T
            turn[2, x] = level_rows(fv_ref, 2).T
            turn[3, x] = level_rows(fv_ref, 3).T
        here = pl.ds(pl.multiple_of(me * Y, 8), Y)
        past = pl.ds(pl.multiple_of(lax.rem(me + ntrc - 1, ntrc) * Y, 8), Y)
        u, v, w, w_next = (turn[i, :, here] for i in range(4))
        v_south = turn[1, :, past][:, Y - 1 : Y]
        level = lax.broadcasted_iota(jnp.int32, (XE, Y, D), 2)
        row = lax.broadcasted_iota(jnp.int32, (XE, Y, D), 1)

        def east(a):
            return jnp.concatenate([a[1:], a[:1]], axis=0)

        def west(a):
            return jnp.concatenate([a[-1:], a[:-1]], axis=0)

        def donor(speed, near, far):
            return jnp.maximum(speed, 0.0) * near + jnp.minimum(speed, 0.0) * far

        def advance(c, i):
            so = jnp.stack([so_ref[i * XE + x : i * XE + x + 1] for x in range(XE)])
            no = jnp.stack([no_ref[i * XE + x : i * XE + x + 1] for x in range(XE)])
            tile = l_ref[4 * T * XE + i * Y : 4 * T * XE + (i + 1) * Y]
            edge = jnp.stack([tile[:, x : x + 1] for x in range(XE)])
            wide = jnp.concatenate([c, jnp.zeros((XE, Y, LANES - D), F32)], axis=2) if D < LANES else c
            upper = shift(wide, -1, 2)[:, :, :D]
            upper = jnp.where(level == 0, jnp.where(lev > 0, edge, 0.0), upper)
            lower = shift(wide, 1, 2)[:, :, :D]
            lower = jnp.where(level == D - 1, jnp.where(lev < nlev - 1, edge, 0.0), lower)
            fe = donor(u, c, east(c))
            fn = donor(v, c, jnp.where(row == Y - 1, no, shift(c, 1, 1)))
            fn_south = jnp.where(row == 0, donor(v_south, so, c[:, 0:1]), shift(fn, -1, 1))
            fall = donor(w_next, c, lower) - donor(w, upper, c)
            return c - marine_advance * ((fe - west(fe)) + (fn - fn_south) + fall)

        sa_ref[...] = advance(s_ref[...], 1)[H : H + X]
        wa_ref[...] = advance(t_ref[...], 0)[H : H + X]
        ua_ref[...] = u[H : H + X]
        va_ref[...] = v[H : H + X]

    saltiness_final, warmth_moved, zonal_speed_final, meridional_speed_final = call(
        ocean,
        (f32(X, Y, D),) * 4,
        (
            warmth,
            salt,
            uv.reshape(2, (D + 4) * XE, YG),
            fv.reshape((D + 5) * XE, YG),
            far_outer,
            south,
            north,
        ),
        scratch=(pltpu.VMEM((4, XE, YG, D), F32),),
        name="own_ocean",
    )

    speed_most = speed_bound + marine_advance * (
        2 * buoyancy * hydro_bound * D * nlev + viscosity * 8 * speed_bound
    )
    growth = 1 + 4 * tracer_step * speed_most + 2 * level_step * (4 * speed_most * D * nlev)
    react_most = NT * coupling_bound * species_bound * growth**2
    unit = 2.0 ** max(0, math.ceil(math.log2(react_most / 65504.0)))

    def spread_columns(c_ref, o_ref):
        n = NT * Y

        def pick(shape, along):
            wide, narrow = (lax.broadcasted_iota(jnp.int32, shape, d) for d in (along, 1 - along))
            return jnp.where(wide // Y == narrow, 1.0, 0.0).astype(jnp.bfloat16)

        tall = jnp.dot(pick((n, NT), 0), c_ref[...], preferred_element_type=F32)
        full = jnp.dot(
            tall.astype(jnp.bfloat16), pick((NT, n), 1), preferred_element_type=F32
        )
        row, lane = (lax.broadcasted_iota(jnp.int32, (n, n), d) for d in (0, 1))
        o_ref[...] = jnp.where(row % Y == lane % Y, full, 0.0).astype(jnp.bfloat16)

    spread = call(
        spread_columns,
        jax.ShapeDtypeStruct((NT * Y, NT * Y), jnp.bfloat16),
        (coupling_matrix,),
        name="spread_coupling",
    )
    flat_tracers = gathered.reshape(NT * Y, DX)
    reaction = jnp.dot(spread, flat_tracers, preferred_element_type=F32)
    reaction = (reaction * (1.0 / unit)).astype(jnp.float16).reshape(ntrc, T * Y, DX)
    returned = lax.all_to_all(reaction, "trc", split_axis=0, concat_axis=0, tiled=True)

    def shade(x_ref, g_ref, k_ref, att_ref, cum_ref):
        att = jnp.zeros((Y, DX), F32)
        for d in range(ntrc):
            rows = x_ref[d].astype(F32)
            for t in range(T):
                att = att + k_ref[g_ref[d * T + t]] * rows[t * Y : (t + 1) * Y]
        att_ref[...] = att
        lane = lax.broadcasted_iota(jnp.int32, (Y, DX), 1)
        total = att
        width = X
        while width < DX:
            total = total + jnp.where(lane < width, 0.0, shift(total, -width, 1))
            width *= 2
        cum_ref[...] = total

    smem = pl.BlockSpec(memory_space=pltpu.SMEM)
    attenuation, shaded = call(
        shade,
        (f32(Y, DX), f32(Y, DX)),
        (gathered, species_guild_number, guild_extinction_coefficient),
        specs=[vmem, smem, smem],
        name="shade",
    )
    far_shade = exchange_levels(shaded)

    def heat(att_ref, cum_ref, r_ref, w_ref, m_ref, o_ref, turn):
        lane = lax.broadcasted_iota(jnp.int32, (Y, LANES), 1)
        keep = (lax.axis_index("lev") > 0) & (lane >= LANES - X)
        above = jnp.where(keep, r_ref[:, DX - LANES :], 0.0)
        width = X
        while width < LANES:
            above = above + shift(above, width, 1)
            width *= 2
        att = att_ref[...]
        path = jnp.concatenate([above] * (DX // LANES), axis=1) + cum_ref[...] - att
        turn[...] = (jnp.exp(-path) * (1.0 - jnp.exp(-att))).T
        for x in range(X):
            absorbed = turn[pl.ds(x, D, stride=X), :].T
            o_ref[x] = w_ref[x] + warming_amount * (m_ref[x].astype(F32) * absorbed)

    warmth_final = call(
        heat,
        f32(X, Y, D),
        (attenuation, shaded, far_shade, warmth_moved, jnp.transpose(marine_indicator, (1, 2, 0))),
        scratch=(pltpu.VMEM((DX, Y), F32),),
        name="heat",
    )

    def finish(r_ref, a_ref, o_any, o_ref, sems):
        copies = [pltpu.make_async_copy(o_ref.at[t], o_any.at[t], sems.at[t]) for t in range(T)]
        for t in range(T):
            for w in range(DX // LANES):
                rows = [
                    r_ref[d, t * Y : (t + 1) * Y, w * LANES : (w + 1) * LANES] for d in range(ntrc)
                ]
                here = slice(w * LANES, (w + 1) * LANES)
                o_ref[t, here] = a_ref[t, here] + (react_step * unit) * jnp.concatenate(rows, axis=0).T
            copies[t].start()
        for copy in copies:
            copy.wait()

    species_final = call(
        finish,
        f32(T, DX, YG),
        (returned.astype(F32), advected),
        scratch=(pltpu.VMEM((T, DX, YG), F32), pltpu.SemaphoreType.DMA((T,))),
        name="finish_tracers",
        outs=pl.BlockSpec(memory_space=pl.ANY),
    )
    ocean_outputs = (warmth_final, saltiness_final, zonal_speed_final, meridional_speed_final)
    ocean_outputs = tuple(jnp.transpose(a, (2, 0, 1)) for a in ocean_outputs)
    return ocean_outputs + (species_final.reshape(T, D, X, YG),)


def solution(mesh):
    ocean = P("lev", "cols", "trc")
    in_specs = (ocean,) * 5 + (P("trc", "lev", "cols", None), P(), P(), P())
    out_specs = (ocean,) * 4 + (P("trc", "lev", "cols", None),)
    return jax.shard_map(shards, mesh=mesh, in_specs=in_specs, out_specs=out_specs, check_vma=False)
```

```python
import math

import jax
import jax.numpy as jnp
from jax import lax
from jax.experimental import pallas as pl
from jax.experimental.pallas import tpu as pltpu
from jax.sharding import PartitionSpec as P

viscosity = 0.2
buoyancy = 0.25
marine_advance = 0.05
tracer_step = 0.2
level_step = 0.04
react_step = 0.25
warming_amount = 60.0

speed_bound = 3.0
hydro_bound = 6.0
species_bound = 2.0
coupling_bound = 0.75

LANES = 128
DRY = 1e30
F32 = jnp.float32


def call(kernel, out_shape, args, specs=None, scratch=(), name=None, mib=16, outs=None):
    vmem = pl.BlockSpec(memory_space=pltpu.VMEM)
    outs = jax.tree.map(lambda _: vmem, out_shape) if outs is None else outs
    return pl.pallas_call(
        kernel,
        out_shape=out_shape,
        in_specs=[vmem] * len(args) if specs is None else specs,
        out_specs=outs,
        scratch_shapes=list(scratch),
        compiler_params=pltpu.CompilerParams(vmem_limit_bytes=mib * 1024 * 1024),
        name=name,
    )(*args)


def f32(*shape):
    return jax.ShapeDtypeStruct(shape, F32)


def shift(a, steps, axis):
    return pltpu.roll(a, (-steps) % a.shape[axis], axis)


def minmod(p, r):
    return jnp.maximum(jnp.minimum(p, r), jnp.minimum(jnp.maximum(p, r), 0.0))


def sideways(c, speed, axis):
    d = 0.5 * (shift(c, 1, axis) - c)
    half = minmod(shift(d, -1, axis), d)
    flux = speed * jnp.where(speed > 0.0, c + half, shift(c - half, 1, axis))
    return flux - shift(flux, -1, axis)


def exchange_levels(part):
    return lax.ppermute(part, "lev", [(0, 1), (1, 0)])


def shards(
    potential_warmth,
    saltiness_anomaly,
    zonal_speed,
    meridional_speed,
    marine_indicator,
    species_concentrations,
    coupling_matrix,
    species_guild_number,
    guild_extinction_coefficient,
):
    cols, ntrc, nlev = lax.axis_size("cols"), lax.axis_size("trc"), lax.axis_size("lev")
    D, X, Y = potential_warmth.shape
    T = species_concentrations.shape[0]
    NT = coupling_matrix.shape[0]
    YG = species_concentrations.shape[3]
    assert nlev == 2 and YG == LANES and X % 8 == 0 and Y % 8 == 0 and ntrc % 2 == 0
    assert LANES % D == 0 and D % 8 == 0 and X % (2 * LANES // D) == 0
    H = X if cols > 1 else 0
    XE = X + 2 * H
    W, DX = D * XE, D * X
    G = LANES // D
    XL = XE // G
    RL = LANES // X

    def widen(block, dim):
        if H == 0:
            return block
        ahead = [(i, (i + 1) % cols) for i in range(cols)]
        back = [(i, (i - 1) % cols) for i in range(cols)]
        low = lax.ppermute(block, "cols", ahead)
        high = lax.ppermute(block, "cols", back)
        return jnp.concatenate([low, block, high], axis=dim)

    warmth, salt, zonal, merid, marine = (
        widen(jnp.transpose(a, (1, 2, 0)), 0)
        for a in (potential_warmth, saltiness_anomaly, zonal_speed, meridional_speed, marine_indicator)
    )
    species = widen(species_concentrations, 2)
    NP = ntrc // 2
    pairs_apart = [[2 * g + c for g in range(NP)] for c in range(2)]

    UV_ROWS, DENSE_ROWS = XL * Y, XL * Y // 2
    DRY_CODE = -(2**14)
    SCALES = 31

    def top(bound):
        return 2.0 ** math.ceil(math.log2(bound))

    tops = (top(hydro_bound * 1.001), top(speed_bound), top(speed_bound))
    codes = (2**14 - 1, 2**15 - 1, 2**15 - 1)

    def pack(t_any, s_any, u_any, v_any, m_any, c_any, pay_ref, lo_ref, hi_ref, out_ref, held, wet, sems):
        upper = lax.axis_index("lev") == 0
        first = pl.multiple_of(jnp.where(upper, D - 4, 0) * XE, 8)
        copies = [
            pltpu.make_async_copy(a, held.at[i], sems.at[i])
            for i, a in enumerate((t_any, s_any, u_any, v_any))
        ]
        copies.append(pltpu.make_async_copy(m_any, wet, sems.at[4]))
        for t in range(T):
            copies.append(
                pltpu.make_async_copy(
                    c_any.at[t, pl.ds(first, 4 * XE)],
                    out_ref.at[pl.ds(t * 4 * XE, 4 * XE)],
                    sems.at[5 + t],
                )
            )
        for copy in copies:
            copy.start()
        for copy in copies:
            copy.wait()
        t, s = held[0], held[1]
        sea = wet[...] > 0
        density = jnp.where(sea, 0.8 * s - 0.2 * t, 0.0)
        numbers, halves = 0, []
        for i, a in enumerate((density, held[2], held[3])):
            most = jnp.max(jnp.abs(a), axis=(0, 1, 2), keepdims=True)[0]
            unit, number = tops[i], 0
            for k in range(1, SCALES + 1):
                fits = most <= tops[i] * 2.0**-k
                unit = jnp.where(fits, tops[i] * 2.0**-k, unit)
                number = jnp.where(fits, k, number)
            code = jnp.floor(jnp.clip(a * (1.0 / unit), -1.0, 1.0) * codes[i] + 0.5).astype(jnp.int32)
            if i == 0:
                code = jnp.where(sea, code, DRY_CODE)
            numbers = numbers + number * 32**i
            code = jnp.concatenate([code[g * XL : (g + 1) * XL] for g in range(G)], axis=2)
            halves.append(code.reshape(XL * Y, LANES))
        density, u, v = halves
        lane = lax.broadcasted_iota(jnp.int32, (XL * Y, LANES), 1)
        density = density * 2 + (lax.shift_right_logical(numbers, lane % 16) & 1)
        rows = jnp.concatenate(
            [u * 65536 + (v & 65535), density[:DENSE_ROWS] * 65536 + (density[DENSE_ROWS:] & 65535)],
            axis=0,
        )
        for g in range(NP):
            pay_ref[g] = rows
        lane = lax.broadcasted_iota(jnp.int32, (Y, LANES), 1)
        for i, a in enumerate((t, s)):
            edge = jnp.zeros((Y, LANES), F32)
            for x in range(XE):
                lo_ref[i * XE + x : i * XE + x + 1] = a[x, 0:1]
                hi_ref[i * XE + x : i * XE + x + 1] = a[x, Y - 1 : Y]
                column = jnp.where(upper, a[x, :, D - 1 : D], a[x, :, 0:1])
                edge = jnp.where(lane == x, column, edge)
            out_ref[4 * T * XE + i * Y : 4 * T * XE + (i + 1) * Y] = edge

    species = species.reshape(T, W, YG)
    payload, lo, hi, outer = call(
        pack,
        (
            jax.ShapeDtypeStruct((NP, UV_ROWS + DENSE_ROWS, LANES), jnp.int32),
            f32(2 * XE, D),
            f32(2 * XE, D),
            f32(4 * T * XE + 2 * Y, LANES),
        ),
        (warmth, salt, zonal, merid, marine, species),
        specs=[pl.BlockSpec(memory_space=pl.ANY)] * 6,
        scratch=(
            pltpu.VMEM((4, XE, Y, D), F32),
            pltpu.VMEM((XE, Y, D), jnp.int32),
            pltpu.SemaphoreType.DMA((5 + T,)),
        ),
        name="pack_ocean",
        mib=60,
    )
    mine = lax.all_to_all(
        payload, "trc", split_axis=0, concat_axis=0, tiled=True, axis_index_groups=pairs_apart
    )
    far_outer = exchange_levels(outer)


    def rows(k, n=XE):
        return pl.ds(pl.multiple_of(k * XE, 8), n)

    def widen_levels(c_ref, h_ref, pad, sem):
        lev = lax.axis_index("lev")
        copy = pltpu.make_async_copy(c_ref, pad.at[:, pl.ds(4 * XE, W)], sem)
        copy.start()
        for t in range(T):
            outer = h_ref[t * 4 * XE : (t + 1) * 4 * XE]
            pad[t, 0 : 4 * XE] = jnp.where(lev > 0, outer, 0.0)
            pad[t, (D + 4) * XE :] = jnp.where(lev < nlev - 1, outer, 0.0)
        copy.wait()

    pad = call(
        widen_levels,
        f32(T, (D + 8) * XE, YG),
        (species, far_outer),
        specs=[pl.BlockSpec(memory_space=pl.ANY), pl.BlockSpec(memory_space=pltpu.VMEM)],
        scratch=(pltpu.SemaphoreType.DMA(()),),
        name="widen_levels",
    )
    mine, pad = lax.optimization_barrier((mine, pad))
    other = lax.ppermute(mine, "trc", [(i, i ^ 1) for i in range(ntrc)])

    def plane(ref, i):
        return ref[i * XE : (i + 1) * XE]

    def dense(raw):
        return jnp.where(raw < 0.5 * DRY, raw, 0.0)

    def faces(raw, u, v, before):
        wet = jnp.where(raw < 0.5 * DRY, 1.0, 0.0)
        d = dense(raw)
        total = before + d
        p = buoyancy * (total - 0.5 * d)
        result = []
        for axis, a in enumerate((u, v)):
            mask = wet * shift(wet, 1, axis)
            lap = shift(a, 1, 0) + shift(a, -1, 0) + shift(a, 1, 1) + shift(a, -1, 1) - 4.0 * a
            push = viscosity * lap - (shift(p, 1, axis) - p)
            result.append((mask * (a + marine_advance * push), mask))
        return total, result

    def unpack(a_ref, b_ref, uv_ref, mask_ref, l_ref, f_ref):
        core = lax.axis_index("trc") % 2
        lane = lax.broadcasted_iota(jnp.int32, (YG, LANES), 1)

        def words(at):
            rows = []
            for g in range(NP):
                a, b = a_ref[g, at : at + Y], b_ref[g, at : at + Y]
                rows += [jnp.where(core == 0, a, b), jnp.where(core == 0, b, a)]
            return jnp.concatenate(rows, axis=0)

        def high(w):
            return lax.shift_right_arithmetic(w, 16)

        def low(w):
            return lax.shift_right_arithmetic(lax.shift_left(w, 16), 16)

        bits = high(words(UV_ROWS)) & 1
        numbers = jnp.sum(jnp.where(lane < 16, lax.shift_left(bits, lane % 16), 0), axis=1, keepdims=True)
        units = []
        for i in range(3):
            number = lax.shift_right_logical(numbers, 5 * i) & 31
            unit = jnp.full((YG, 1), tops[i] / codes[i], F32)
            for b in range(5):
                unit = jnp.where(lax.shift_right_logical(number, b) & 1 > 0, unit * 2.0 ** -(2**b), unit)
            units.append(unit)

        def put(f, x, a):
            turned = a.T
            for g in range(G):
                f_ref[f, pl.ds(x + g * XL, D, stride=XE), :] = turned[g * D : (g + 1) * D]

        for x in range(XL):
            w = words(x * Y)
            put(1, x, high(w).astype(F32) * units[1])
            put(2, x, low(w).astype(F32) * units[2])
            if x < XL // 2:
                w = words(UV_ROWS + x * Y)
                for xx, code in ((x, high(w)), (x + XL // 2, low(w))):
                    code = lax.shift_right_arithmetic(code, 1)
                    put(0, xx, jnp.where(code == DRY_CODE, DRY, code.astype(F32) * units[0]))

        def field(f, k):
            return f_ref[f, pl.ds(pl.multiple_of(k * XE, 8), XE)]

        def one(k, carry):
            total, sums = carry
            total, new = faces(field(0, k), field(1, k), field(2, k), total)
            for i, (speed, mask) in enumerate(new):
                uv_ref[i, k] = speed
                mask_ref[i, k] = mask
            parts = (new[0][0], new[1][0], new[0][1], new[1][1])
            return total, tuple(a + b for a, b in zip(sums, parts))

        zero = jnp.zeros((XE, YG), F32)
        total, sums = lax.fori_loop(0, D, one, (zero, (zero,) * 4), unroll=D // 2)
        for i, a in enumerate((total,) + sums):
            l_ref[i * XE : (i + 1) * XE] = a
        first = jnp.where(lax.axis_index("lev") == 0, D - 2, 0)
        for f in range(3):
            for k in range(2):
                at = (5 + 2 * f + k) * XE
                l_ref[at : at + XE] = field(f, first + k)

    near_uv, masks, own_levels = call(
        unpack,
        (f32(2, D, XE, YG), f32(2, D, XE, YG), f32(11 * XE, YG)),
        (mine, other),
        scratch=(pltpu.VMEM((3, W, YG), F32),),
        name="unpack_ocean",
    )
    own_levels, pad = lax.optimization_barrier((own_levels, pad))
    far_levels = exchange_levels(own_levels)

    def half_slope(lo, mid, hi):
        return minmod(0.5 * (mid - lo), 0.5 * (hi - mid))

    def edges(c, axis):
        d = 0.5 * (shift(c, 1, axis) - c)
        half = minmod(shift(d, -1, axis), d)
        return c + half, shift(c - half, 1, axis)

    def slopes(pad, side):
        def one(k, carry):
            lo, mid = carry
            hi = pad[:, rows(k + 2)]
            half = half_slope(lo, mid, hi)
            values = edges(mid, 1) + edges(mid, 2) + (mid + half, mid - half)
            for i, a in enumerate(values):
                side[i, :, rows(k)] = a
            return mid, hi

        count = D + 6
        first = (pad[:, 0:XE], pad[:, XE : 2 * XE])
        lax.fori_loop(0, count, one, first, unroll=count // 5)

    side = call(slopes, f32(6, T, (D + 6) * XE, YG), (pad,), name="first_slopes")
    far_levels, side = lax.optimization_barrier((far_levels, side))

    def speeds(n_ref, m_ref, o_ref, r_ref, uv_ref, fv_ref):
        lev = lax.axis_index("lev")
        above = jnp.where(lev > 0, plane(r_ref, 0), 0.0)
        sum_here = plane(o_ref, 0)

        def pushes(a):
            return [-marine_advance * buoyancy * (shift(a, 1, i) - a) for i in range(2)]

        def spread_out(u, v):
            return u - shift(u, -1, 0) + v - shift(v, -1, 1)

        def far(e, total):
            k = e % 2 if e < 2 else e - D - 2
            total, new = faces(plane(r_ref, 5 + k), plane(r_ref, 7 + k), plane(r_ref, 9 + k), total)
            for i in range(2):
                uv_ref[i, e] = new[i][0]
            return total

        total = above - dense(plane(r_ref, 5)) - dense(plane(r_ref, 6))
        for e in (0, 1):
            total = far(e, total)
        total = above + sum_here
        for e in (D + 2, D + 3):
            total = far(e, total)

        push = pushes(sum_here)
        lower = [plane(r_ref, 1 + i) + plane(r_ref, 3 + i) * push[i] for i in range(2)]
        below = jnp.where(lev < nlev - 1, spread_out(*lower), 0.0)

        def divergence(e):
            return spread_out(uv_ref[0, e], uv_ref[1, e])

        fv_ref[D + 2] = below
        fv_ref[D + 3] = below - divergence(D + 2)
        fv_ref[D + 4] = below - divergence(D + 2) - divergence(D + 3)
        push = pushes(above)

        def climb(j, total):
            k = D - 1 - j
            new = [n_ref[i, k] + m_ref[i, k] * push[i] for i in range(2)]
            for i in range(2):
                uv_ref[i, k + 2] = new[i]
            total = total + spread_out(*new)
            fv_ref[k + 2] = total
            return total

        total = lax.fori_loop(0, D, climb, below, unroll=D)
        fv_ref[2] = jnp.where(lev == 0, 0.0, total)
        for e in (1, 0):
            total = total + divergence(e)
            fv_ref[e] = total

    def advect(n_ref, m_ref, o_ref, r_ref, pad, side, adv_ref, msg_any, uv_ref, fv_ref, mid_pad, held, sems):
        speeds(n_ref, m_ref, o_ref, r_ref, uv_ref, fv_ref)

        def speeds_at(e):
            return tracer_step * uv_ref[0, e][None], tracer_step * uv_ref[1, e][None]

        def fall(e, up, low):
            w = level_step * fv_ref[e]
            return w * jnp.where(w > 0.0, up, low)

        def first_step(e, flux):
            k = rows(e + 1)
            flux_next = fall(e + 1, side[4, :, k], side[5, :, rows(e + 2)])
            change = flux_next - flux
            for i, speed in enumerate(speeds_at(e)):
                f = speed * jnp.where(speed > 0.0, side[2 * i, :, k], side[2 * i + 1, :, k])
                change = change + (f - shift(f, -1, i + 1))
            mid_pad[:, rows(e)] = pad[:, rows(e + 2)] - change
            return flux_next

        flux = fall(0, side[4, :, rows(0)], side[5, :, rows(1)])
        lax.fori_loop(0, D + 4, first_step, flux, unroll=(D + 4) // 2)

        def second_step(k, carry):
            B = 16
            here = mid_pad[:, rows(k + 2, B * XE)].reshape(T, B, XE, YG)
            u = tracer_step * uv_ref[0, pl.ds(k + 2, B)]
            v = tracer_step * uv_ref[1, pl.ds(k + 2, B)]
            flat = sideways(here, v, 3) + sideways(here, u, 2)
            mid, hi, up, flux = carry
            for j in range(B):
                nxt = mid_pad[:, rows(k + j + 4)]
                half = half_slope(mid, hi, nxt)
                flux_next = fall(k + j + 3, up, hi - half)
                new = mid - (flat[:, j] + (flux_next - flux))
                adv_ref[:, pl.ds(pl.multiple_of((k + j) * X, 8), X)] = new[:, H : H + X]
                mid, hi, up, flux = hi, nxt, hi + half, flux_next
            return mid, hi, up, flux

        c = [mid_pad[:, rows(k)] for k in range(4)]
        half = half_slope(c[1], c[2], c[3])
        flux = fall(2, c[1] + half_slope(c[0], c[1], c[2]), c[2] - half)

        def sending(w):
            here = pl.ds(pl.multiple_of(w * LANES, LANES), LANES)
            return pltpu.make_async_copy(held.at[w], msg_any.at[:, :, here], sems.at[w])

        def turn(w):
            here = pl.ds(pl.multiple_of(w * LANES, LANES), LANES)
            turned = [adv_ref[t, here].T for t in range(T)]
            for d in range(ntrc):
                there = [turned[t][d * Y : (d + 1) * Y] for t in range(T)]
                held[w, d] = jnp.concatenate(there, axis=0).astype(jnp.bfloat16)
            sending(w).start()

        def block(w, carry):
            for k in range(0, RL, 16):
                carry = second_step(w * RL + k, carry)
            return carry

        count = DX // LANES
        lax.fori_loop(0, count, block, (c[2], c[3], c[2] + half, flux), unroll=2)
        for w in range(count):
            turn(w)
        for w in range(count):
            sending(w).wait()

    vmem = pl.BlockSpec(memory_space=pltpu.VMEM)
    advected, message, uv, fv = call(
        advect,
        (f32(T, DX, YG), pltpu.HBM((ntrc, T * Y, DX), jnp.bfloat16))
        + (f32(2, D + 4, XE, YG), f32(D + 5, XE, YG)),
        (near_uv, masks, own_levels, far_levels, pad, side),
        scratch=(
            pltpu.VMEM((T, (D + 4) * XE, YG), F32),
            pltpu.VMEM((DX // LANES, ntrc, T * Y, LANES), jnp.bfloat16),
            pltpu.SemaphoreType.DMA((DX // LANES,)),
        ),
        outs=(vmem, pl.BlockSpec(memory_space=pltpu.HBM), vmem, vmem),
        name="advect_tracers",
    )
    message, lo, hi = lax.optimization_barrier((message, lo, hi))
    gathered = lax.all_to_all(message, "trc", split_axis=0, concat_axis=0, tiled=True)
    ring = [(i, (i + 1) % ntrc) for i in range(ntrc)]
    south = lax.ppermute(hi, "trc", ring)
    north = lax.ppermute(lo, "trc", [(b, a) for a, b in ring])
    gathered, south, north = lax.optimization_barrier((gathered, south, north))

    def ocean(
        t_ref, s_ref, uv_ref, fv_ref, l_ref, so_ref, no_ref, sa_ref, wa_ref, ua_ref, va_ref, turn
    ):
        me, lev = lax.axis_index("trc"), lax.axis_index("lev")
        for x in range(XE):
            def level_rows(ref, first):
                return ref[pl.ds(first * XE + x, D, stride=XE), :]

            turn[0, x] = level_rows(uv_ref.at[0], 2).T
            turn[1, x] = level_rows(uv_ref.at[1], 2).T
            turn[2, x] = level_rows(fv_ref, 2).T
            turn[3, x] = level_rows(fv_ref, 3).T
        here = pl.ds(pl.multiple_of(me * Y, 8), Y)
        past = pl.ds(pl.multiple_of(lax.rem(me + ntrc - 1, ntrc) * Y, 8), Y)
        u, v, w, w_next = (turn[i, :, here] for i in range(4))
        v_south = turn[1, :, past][:, Y - 1 : Y]
        level = lax.broadcasted_iota(jnp.int32, (XE, Y, D), 2)
        row = lax.broadcasted_iota(jnp.int32, (XE, Y, D), 1)

        def east(a):
            return jnp.concatenate([a[1:], a[:1]], axis=0)

        def west(a):
            return jnp.concatenate([a[-1:], a[:-1]], axis=0)

        def donor(speed, near, far):
            return jnp.maximum(speed, 0.0) * near + jnp.minimum(speed, 0.0) * far

        def advance(c, i):
            so = jnp.stack([so_ref[i * XE + x : i * XE + x + 1] for x in range(XE)])
            no = jnp.stack([no_ref[i * XE + x : i * XE + x + 1] for x in range(XE)])
            tile = l_ref[4 * T * XE + i * Y : 4 * T * XE + (i + 1) * Y]
            edge = jnp.stack([tile[:, x : x + 1] for x in range(XE)])
            wide = jnp.concatenate([c, jnp.zeros((XE, Y, LANES - D), F32)], axis=2) if D < LANES else c
            upper = shift(wide, -1, 2)[:, :, :D]
            upper = jnp.where(level == 0, jnp.where(lev > 0, edge, 0.0), upper)
            lower = shift(wide, 1, 2)[:, :, :D]
            lower = jnp.where(level == D - 1, jnp.where(lev < nlev - 1, edge, 0.0), lower)
            fe = donor(u, c, east(c))
            fn = donor(v, c, jnp.where(row == Y - 1, no, shift(c, 1, 1)))
            fn_south = jnp.where(row == 0, donor(v_south, so, c[:, 0:1]), shift(fn, -1, 1))
            fall = donor(w_next, c, lower) - donor(w, upper, c)
            return c - marine_advance * ((fe - west(fe)) + (fn - fn_south) + fall)

        sa_ref[...] = advance(s_ref[...], 1)[H : H + X]
        wa_ref[...] = advance(t_ref[...], 0)[H : H + X]
        ua_ref[...] = u[H : H + X]
        va_ref[...] = v[H : H + X]

    saltiness_final, warmth_moved, zonal_speed_final, meridional_speed_final = call(
        ocean,
        (f32(X, Y, D),) * 4,
        (
            warmth,
            salt,
            uv.reshape(2, (D + 4) * XE, YG),
            fv.reshape((D + 5) * XE, YG),
            far_outer,
            south,
            north,
        ),
        scratch=(pltpu.VMEM((4, XE, YG, D), F32),),
        name="own_ocean",
    )

    speed_most = speed_bound + marine_advance * (
        2 * buoyancy * hydro_bound * D * nlev + viscosity * 8 * speed_bound
    )
    growth = 1 + 4 * tracer_step * speed_most + 2 * level_step * (4 * speed_most * D * nlev)
    react_most = NT * coupling_bound * species_bound * growth**2
    unit = 2.0 ** max(0, math.ceil(math.log2(react_most / 65504.0)))

    def spread_columns(c_ref, o_ref):
        n = NT * Y

        def pick(shape, along):
            wide, narrow = (lax.broadcasted_iota(jnp.int32, shape, d) for d in (along, 1 - along))
            return jnp.where(wide // Y == narrow, 1.0, 0.0).astype(jnp.bfloat16)

        tall = jnp.dot(pick((n, NT), 0), c_ref[...], preferred_element_type=F32)
        full = jnp.dot(
            tall.astype(jnp.bfloat16), pick((NT, n), 1), preferred_element_type=F32
        )
        row, lane = (lax.broadcasted_iota(jnp.int32, (n, n), d) for d in (0, 1))
        o_ref[...] = jnp.where(row % Y == lane % Y, full, 0.0).astype(jnp.bfloat16)

    spread = call(
        spread_columns,
        jax.ShapeDtypeStruct((NT * Y, NT * Y), jnp.bfloat16),
        (coupling_matrix,),
        name="spread_coupling",
    )
    flat_tracers = gathered.reshape(NT * Y, DX)
    reaction = jnp.dot(spread, flat_tracers, preferred_element_type=F32)
    reaction = (reaction * (1.0 / unit)).astype(jnp.float16).reshape(ntrc, T * Y, DX)
    returned = lax.all_to_all(reaction, "trc", split_axis=0, concat_axis=0, tiled=True)

    def shade(x_ref, g_ref, k_ref, att_ref, cum_ref):
        att = jnp.zeros((Y, DX), F32)
        for d in range(ntrc):
            rows = x_ref[d].astype(F32)
            for t in range(T):
                att = att + k_ref[g_ref[d * T + t]] * rows[t * Y : (t + 1) * Y]
        att_ref[...] = att
        lane = lax.broadcasted_iota(jnp.int32, (Y, DX), 1)
        total = att
        width = X
        while width < DX:
            total = total + jnp.where(lane < width, 0.0, shift(total, -width, 1))
            width *= 2
        cum_ref[...] = total

    smem = pl.BlockSpec(memory_space=pltpu.SMEM)
    attenuation, shaded = call(
        shade,
        (f32(Y, DX), f32(Y, DX)),
        (gathered, species_guild_number, guild_extinction_coefficient),
        specs=[vmem, smem, smem],
        name="shade",
    )
    far_shade = exchange_levels(shaded)

    def heat(att_ref, cum_ref, r_ref, w_ref, m_ref, o_ref, turn):
        lane = lax.broadcasted_iota(jnp.int32, (Y, LANES), 1)
        keep = (lax.axis_index("lev") > 0) & (lane >= LANES - X)
        above = jnp.where(keep, r_ref[:, DX - LANES :], 0.0)
        width = X
        while width < LANES:
            above = above + shift(above, width, 1)
            width *= 2
        att = att_ref[...]
        path = jnp.concatenate([above] * (DX // LANES), axis=1) + cum_ref[...] - att
        turn[...] = (jnp.exp(-path) * (1.0 - jnp.exp(-att))).T
        for x in range(X):
            absorbed = turn[pl.ds(x, D, stride=X), :].T
            o_ref[x] = w_ref[x] + warming_amount * (m_ref[x].astype(F32) * absorbed)

    warmth_final = call(
        heat,
        f32(X, Y, D),
        (attenuation, shaded, far_shade, warmth_moved, jnp.transpose(marine_indicator, (1, 2, 0))),
        scratch=(pltpu.VMEM((DX, Y), F32),),
        name="heat",
    )

    def finish(r_ref, a_ref, o_any, o_ref, sems):
        copies = [pltpu.make_async_copy(o_ref.at[t], o_any.at[t], sems.at[t]) for t in range(T)]
        for t in range(T):
            for w in range(DX // LANES):
                rows = [
                    r_ref[d, t * Y : (t + 1) * Y, w * LANES : (w + 1) * LANES] for d in range(ntrc)
                ]
                here = slice(w * LANES, (w + 1) * LANES)
                o_ref[t, here] = a_ref[t, here] + (react_step * unit) * jnp.concatenate(rows, axis=0).T
            copies[t].start()
        for copy in copies:
            copy.wait()

    species_final = call(
        finish,
        f32(T, DX, YG),
        (returned.astype(F32), advected),
        scratch=(pltpu.VMEM((T, DX, YG), F32), pltpu.SemaphoreType.DMA((T,))),
        name="finish_tracers",
        outs=pl.BlockSpec(memory_space=pl.ANY),
    )
    ocean_outputs = (warmth_final, saltiness_final, zonal_speed_final, meridional_speed_final)
    ocean_outputs = tuple(jnp.transpose(a, (2, 0, 1)) for a in ocean_outputs)
    return ocean_outputs + (species_final.reshape(T, D, X, YG),)


def solution(mesh):
    ocean = P("lev", "cols", "trc")
    in_specs = (ocean,) * 5 + (P("trc", "lev", "cols", None), P(), P(), P())
    out_specs = (ocean,) * 4 + (P("trc", "lev", "cols", None),)
    return jax.shard_map(shards, mesh=mesh, in_specs=in_specs, out_specs=out_specs, check_vma=False)
```

```python
import math

import jax
import jax.numpy as jnp
from jax import lax
from jax.experimental import pallas as pl
from jax.experimental.pallas import tpu as pltpu
from jax.sharding import PartitionSpec as P

viscosity = 0.2
buoyancy = 0.25
marine_advance = 0.05
tracer_step = 0.2
level_step = 0.04
react_step = 0.25
warming_amount = 60.0

speed_bound = 3.0
hydro_bound = 6.0
species_bound = 2.0
coupling_bound = 0.75

LANES = 128
DRY = 1e30
F32 = jnp.float32


def call(kernel, out_shape, args, specs=None, scratch=(), name=None, mib=16, outs=None):
    vmem = pl.BlockSpec(memory_space=pltpu.VMEM)
    outs = jax.tree.map(lambda _: vmem, out_shape) if outs is None else outs
    return pl.pallas_call(
        kernel,
        out_shape=out_shape,
        in_specs=[vmem] * len(args) if specs is None else specs,
        out_specs=outs,
        scratch_shapes=list(scratch),
        compiler_params=pltpu.CompilerParams(vmem_limit_bytes=mib * 1024 * 1024),
        name=name,
    )(*args)


def f32(*shape):
    return jax.ShapeDtypeStruct(shape, F32)


def shift(a, steps, axis):
    return pltpu.roll(a, (-steps) % a.shape[axis], axis)


def minmod(p, r):
    return jnp.maximum(jnp.minimum(p, r), jnp.minimum(jnp.maximum(p, r), 0.0))


def sideways(c, speed, axis):
    d = 0.5 * (shift(c, 1, axis) - c)
    half = minmod(shift(d, -1, axis), d)
    flux = speed * jnp.where(speed > 0.0, c + half, shift(c - half, 1, axis))
    return flux - shift(flux, -1, axis)


def exchange_levels(part):
    return lax.ppermute(part, "lev", [(0, 1), (1, 0)])


def shards(
    potential_warmth,
    saltiness_anomaly,
    zonal_speed,
    meridional_speed,
    marine_indicator,
    species_concentrations,
    coupling_matrix,
    species_guild_number,
    guild_extinction_coefficient,
):
    cols, ntrc, nlev = lax.axis_size("cols"), lax.axis_size("trc"), lax.axis_size("lev")
    D, X, Y = potential_warmth.shape
    T = species_concentrations.shape[0]
    NT = coupling_matrix.shape[0]
    YG = species_concentrations.shape[3]
    assert nlev == 2 and YG == LANES and X % 8 == 0 and Y % 8 == 0 and ntrc % 2 == 0
    assert LANES % D == 0 and D % 8 == 0 and X % (2 * LANES // D) == 0
    H = X if cols > 1 else 0
    XE = X + 2 * H
    W, DX = D * XE, D * X
    G = LANES // D
    XL = XE // G
    RL = LANES // X

    def widen(block, dim):
        if H == 0:
            return block
        ahead = [(i, (i + 1) % cols) for i in range(cols)]
        back = [(i, (i - 1) % cols) for i in range(cols)]
        low = lax.ppermute(block, "cols", ahead)
        high = lax.ppermute(block, "cols", back)
        return jnp.concatenate([low, block, high], axis=dim)

    warmth, salt, zonal, merid, marine = (
        widen(jnp.transpose(a, (1, 2, 0)), 0)
        for a in (potential_warmth, saltiness_anomaly, zonal_speed, meridional_speed, marine_indicator)
    )
    species = widen(species_concentrations, 2)
    NP = ntrc // 2
    pairs_apart = [[2 * g + c for g in range(NP)] for c in range(2)]

    UV_ROWS, DENSE_ROWS = XL * Y, XL * Y // 2
    DRY_CODE = -(2**14)
    SCALES = 31

    def top(bound):
        return 2.0 ** math.ceil(math.log2(bound))

    tops = (top(hydro_bound * 1.001), top(speed_bound), top(speed_bound))
    codes = (2**14 - 1, 2**15 - 1, 2**15 - 1)

    def pack(t_any, s_any, u_any, v_any, m_any, c_any, pay_ref, lo_ref, hi_ref, out_ref, held, wet, sems):
        upper = lax.axis_index("lev") == 0
        first = pl.multiple_of(jnp.where(upper, D - 4, 0) * XE, 8)
        copies = [
            pltpu.make_async_copy(a, held.at[i], sems.at[i])
            for i, a in enumerate((t_any, s_any, u_any, v_any))
        ]
        copies.append(pltpu.make_async_copy(m_any, wet, sems.at[4]))
        for t in range(T):
            copies.append(
                pltpu.make_async_copy(
                    c_any.at[t, pl.ds(first, 4 * XE)],
                    out_ref.at[pl.ds(t * 4 * XE, 4 * XE)],
                    sems.at[5 + t],
                )
            )
        for copy in copies:
            copy.start()
        for copy in copies:
            copy.wait()
        t, s = held[0], held[1]
        sea = wet[...] > 0
        density = jnp.where(sea, 0.8 * s - 0.2 * t, 0.0)
        numbers, halves = 0, []
        for i, a in enumerate((density, held[2], held[3])):
            most = jnp.max(jnp.abs(a), axis=(0, 1, 2), keepdims=True)[0]
            unit, number = tops[i], 0
            for k in range(1, SCALES + 1):
                fits = most <= tops[i] * 2.0**-k
                unit = jnp.where(fits, tops[i] * 2.0**-k, unit)
                number = jnp.where(fits, k, number)
            code = jnp.floor(jnp.clip(a * (1.0 / unit), -1.0, 1.0) * codes[i] + 0.5).astype(jnp.int32)
            if i == 0:
                code = jnp.where(sea, code, DRY_CODE)
            numbers = numbers + number * 32**i
            code = jnp.concatenate([code[g * XL : (g + 1) * XL] for g in range(G)], axis=2)
            halves.append(code.reshape(XL * Y, LANES))
        density, u, v = halves
        lane = lax.broadcasted_iota(jnp.int32, (XL * Y, LANES), 1)
        density = density * 2 + (lax.shift_right_logical(numbers, lane % 16) & 1)
        rows = jnp.concatenate(
            [u * 65536 + (v & 65535), density[:DENSE_ROWS] * 65536 + (density[DENSE_ROWS:] & 65535)],
            axis=0,
        )
        for g in range(NP):
            pay_ref[g] = rows
        lane = lax.broadcasted_iota(jnp.int32, (Y, LANES), 1)
        for i, a in enumerate((t, s)):
            edge = jnp.zeros((Y, LANES), F32)
            for x in range(XE):
                lo_ref[i * XE + x : i * XE + x + 1] = a[x, 0:1]
                hi_ref[i * XE + x : i * XE + x + 1] = a[x, Y - 1 : Y]
                column = jnp.where(upper, a[x, :, D - 1 : D], a[x, :, 0:1])
                edge = jnp.where(lane == x, column, edge)
            out_ref[4 * T * XE + i * Y : 4 * T * XE + (i + 1) * Y] = edge

    species = species.reshape(T, W, YG)
    payload, lo, hi, outer = call(
        pack,
        (
            jax.ShapeDtypeStruct((NP, UV_ROWS + DENSE_ROWS, LANES), jnp.int32),
            f32(2 * XE, D),
            f32(2 * XE, D),
            f32(4 * T * XE + 2 * Y, LANES),
        ),
        (warmth, salt, zonal, merid, marine, species),
        specs=[pl.BlockSpec(memory_space=pl.ANY)] * 6,
        scratch=(
            pltpu.VMEM((4, XE, Y, D), F32),
            pltpu.VMEM((XE, Y, D), jnp.int32),
            pltpu.SemaphoreType.DMA((5 + T,)),
        ),
        name="pack_ocean",
        mib=60,
    )
    mine = lax.all_to_all(
        payload, "trc", split_axis=0, concat_axis=0, tiled=True, axis_index_groups=pairs_apart
    )
    far_outer = exchange_levels(outer)


    def rows(k, n=XE):
        return pl.ds(pl.multiple_of(k * XE, 8), n)

    def widen_levels(c_ref, h_ref, pad, sem):
        lev = lax.axis_index("lev")
        copy = pltpu.make_async_copy(c_ref, pad.at[:, pl.ds(4 * XE, W)], sem)
        copy.start()
        for t in range(T):
            outer = h_ref[t * 4 * XE : (t + 1) * 4 * XE]
            pad[t, 0 : 4 * XE] = jnp.where(lev > 0, outer, 0.0)
            pad[t, (D + 4) * XE :] = jnp.where(lev < nlev - 1, outer, 0.0)
        copy.wait()

    pad = call(
        widen_levels,
        f32(T, (D + 8) * XE, YG),
        (species, far_outer),
        specs=[pl.BlockSpec(memory_space=pl.ANY), pl.BlockSpec(memory_space=pltpu.VMEM)],
        scratch=(pltpu.SemaphoreType.DMA(()),),
        name="widen_levels",
    )
    mine, pad = lax.optimization_barrier((mine, pad))
    other = lax.ppermute(mine, "trc", [(i, i ^ 1) for i in range(ntrc)])

    def plane(ref, i):
        return ref[i * XE : (i + 1) * XE]

    def dense(raw):
        return jnp.where(raw < 0.5 * DRY, raw, 0.0)

    def faces(raw, u, v, before):
        wet = jnp.where(raw < 0.5 * DRY, 1.0, 0.0)
        d = dense(raw)
        total = before + d
        p = buoyancy * (total - 0.5 * d)
        result = []
        for axis, a in enumerate((u, v)):
            mask = wet * shift(wet, 1, axis)
            lap = shift(a, 1, 0) + shift(a, -1, 0) + shift(a, 1, 1) + shift(a, -1, 1) - 4.0 * a
            push = viscosity * lap - (shift(p, 1, axis) - p)
            result.append((mask * (a + marine_advance * push), mask))
        return total, result

    def unpack(a_ref, b_ref, uv_ref, mask_ref, l_ref, f_ref):
        core = lax.axis_index("trc") % 2
        lane = lax.broadcasted_iota(jnp.int32, (YG, LANES), 1)

        def words(at):
            rows = []
            for g in range(NP):
                a, b = a_ref[g, at : at + Y], b_ref[g, at : at + Y]
                rows += [jnp.where(core == 0, a, b), jnp.where(core == 0, b, a)]
            return jnp.concatenate(rows, axis=0)

        def high(w):
            return lax.shift_right_arithmetic(w, 16)

        def low(w):
            return lax.shift_right_arithmetic(lax.shift_left(w, 16), 16)

        bits = high(words(UV_ROWS)) & 1
        numbers = jnp.sum(jnp.where(lane < 16, lax.shift_left(bits, lane % 16), 0), axis=1, keepdims=True)
        units = []
        for i in range(3):
            number = lax.shift_right_logical(numbers, 5 * i) & 31
            unit = jnp.full((YG, 1), tops[i] / codes[i], F32)
            for b in range(5):
                unit = jnp.where(lax.shift_right_logical(number, b) & 1 > 0, unit * 2.0 ** -(2**b), unit)
            units.append(unit)

        def put(f, x, a):
            turned = a.T
            for g in range(G):
                f_ref[f, pl.ds(x + g * XL, D, stride=XE), :] = turned[g * D : (g + 1) * D]

        for x in range(XL):
            w = words(x * Y)
            put(1, x, high(w).astype(F32) * units[1])
            put(2, x, low(w).astype(F32) * units[2])
            if x < XL // 2:
                w = words(UV_ROWS + x * Y)
                for xx, code in ((x, high(w)), (x + XL // 2, low(w))):
                    code = lax.shift_right_arithmetic(code, 1)
                    put(0, xx, jnp.where(code == DRY_CODE, DRY, code.astype(F32) * units[0]))

        def field(f, k):
            return f_ref[f, pl.ds(pl.multiple_of(k * XE, 8), XE)]

        def one(k, carry):
            total, sums = carry
            total, new = faces(field(0, k), field(1, k), field(2, k), total)
            for i, (speed, mask) in enumerate(new):
                uv_ref[i, k] = speed
                mask_ref[i, k] = mask
            parts = (new[0][0], new[1][0], new[0][1], new[1][1])
            return total, tuple(a + b for a, b in zip(sums, parts))

        zero = jnp.zeros((XE, YG), F32)
        total, sums = lax.fori_loop(0, D, one, (zero, (zero,) * 4), unroll=D // 2)
        for i, a in enumerate((total,) + sums):
            l_ref[i * XE : (i + 1) * XE] = a
        first = jnp.where(lax.axis_index("lev") == 0, D - 2, 0)
        for f in range(3):
            for k in range(2):
                at = (5 + 2 * f + k) * XE
                l_ref[at : at + XE] = field(f, first + k)

    near_uv, masks, own_levels = call(
        unpack,
        (f32(2, D, XE, YG), f32(2, D, XE, YG), f32(11 * XE, YG)),
        (mine, other),
        scratch=(pltpu.VMEM((3, W, YG), F32),),
        name="unpack_ocean",
    )
    own_levels, pad = lax.optimization_barrier((own_levels, pad))
    far_levels = exchange_levels(own_levels)

    def half_slope(lo, mid, hi):
        return minmod(0.5 * (mid - lo), 0.5 * (hi - mid))

    def edges(c, axis):
        d = 0.5 * (shift(c, 1, axis) - c)
        half = minmod(shift(d, -1, axis), d)
        return c + half, shift(c - half, 1, axis)

    def slopes(pad, side):
        def one(k, carry):
            lo, mid = carry
            hi = pad[:, rows(k + 2)]
            half = half_slope(lo, mid, hi)
            values = edges(mid, 1) + edges(mid, 2) + (mid + half, mid - half)
            for i, a in enumerate(values):
                side[i, :, rows(k)] = a
            return mid, hi

        count = D + 6
        first = (pad[:, 0:XE], pad[:, XE : 2 * XE])
        lax.fori_loop(0, count, one, first, unroll=count // 5)

    side = call(slopes, f32(6, T, (D + 6) * XE, YG), (pad,), name="first_slopes")
    far_levels, side = lax.optimization_barrier((far_levels, side))

    def speeds(n_ref, m_ref, o_ref, r_ref, uv_ref, fv_ref):
        lev = lax.axis_index("lev")
        above = jnp.where(lev > 0, plane(r_ref, 0), 0.0)
        sum_here = plane(o_ref, 0)

        def pushes(a):
            return [-marine_advance * buoyancy * (shift(a, 1, i) - a) for i in range(2)]

        def spread_out(u, v):
            return u - shift(u, -1, 0) + v - shift(v, -1, 1)

        def far(e, total):
            k = e % 2 if e < 2 else e - D - 2
            total, new = faces(plane(r_ref, 5 + k), plane(r_ref, 7 + k), plane(r_ref, 9 + k), total)
            for i in range(2):
                uv_ref[i, e] = new[i][0]
            return total

        total = above - dense(plane(r_ref, 5)) - dense(plane(r_ref, 6))
        for e in (0, 1):
            total = far(e, total)
        total = above + sum_here
        for e in (D + 2, D + 3):
            total = far(e, total)

        push = pushes(sum_here)
        lower = [plane(r_ref, 1 + i) + plane(r_ref, 3 + i) * push[i] for i in range(2)]
        below = jnp.where(lev < nlev - 1, spread_out(*lower), 0.0)

        def divergence(e):
            return spread_out(uv_ref[0, e], uv_ref[1, e])

        fv_ref[D + 2] = below
        fv_ref[D + 3] = below - divergence(D + 2)
        fv_ref[D + 4] = below - divergence(D + 2) - divergence(D + 3)
        push = pushes(above)

        def climb(j, total):
            k = D - 1 - j
            new = [n_ref[i, k] + m_ref[i, k] * push[i] for i in range(2)]
            for i in range(2):
                uv_ref[i, k + 2] = new[i]
            total = total + spread_out(*new)
            fv_ref[k + 2] = total
            return total

        total = lax.fori_loop(0, D, climb, below, unroll=D)
        fv_ref[2] = jnp.where(lev == 0, 0.0, total)
        for e in (1, 0):
            total = total + divergence(e)
            fv_ref[e] = total

    def advect(n_ref, m_ref, o_ref, r_ref, pad, side, adv_ref, msg_any, uv_ref, fv_ref, mid_pad, part, held, sems):
        speeds(n_ref, m_ref, o_ref, r_ref, uv_ref, fv_ref)

        def speeds_at(e):
            return tracer_step * uv_ref[0, e][None], tracer_step * uv_ref[1, e][None]

        def fall(e, up, low):
            w = level_step * fv_ref[e]
            return w * jnp.where(w > 0.0, up, low)

        def first_step(e, flux):
            k = rows(e + 1)
            flux_next = fall(e + 1, side[4, :, k], side[5, :, rows(e + 2)])
            change = flux_next - flux
            for i, speed in enumerate(speeds_at(e)):
                f = speed * jnp.where(speed > 0.0, side[2 * i, :, k], side[2 * i + 1, :, k])
                change = change + (f - shift(f, -1, i + 1))
            mid_pad[:, rows(e)] = pad[:, rows(e + 2)] - change
            return flux_next

        flux = fall(0, side[4, :, rows(0)], side[5, :, rows(1)])
        lax.fori_loop(0, D + 4, first_step, flux, unroll=(D + 4) // 2)

        def second_step(k, carry):
            B = RL
            here = mid_pad[:, rows(k + 2, B * XE)].reshape(T, B, XE, YG)
            u = tracer_step * uv_ref[0, pl.ds(k + 2, B)]
            flat = sideways(here, u, 2)
            mid, hi, up, flux = carry
            for j in range(B):
                nxt = mid_pad[:, rows(k + j + 4)]
                half = half_slope(mid, hi, nxt)
                flux_next = fall(k + j + 3, up, hi - half)
                new = mid - (flat[:, j] + (flux_next - flux))
                part[:, pl.ds(pl.multiple_of((k + j) * X, 8), X)] = new[:, H : H + X]
                mid, hi, up, flux = hi, nxt, hi + half, flux_next
            return mid, hi, up, flux

        c = [mid_pad[:, rows(k)] for k in range(4)]
        half = half_slope(c[1], c[2], c[3])
        flux = fall(2, c[1] + half_slope(c[0], c[1], c[2]), c[2] - half)

        def sending(w):
            here = pl.ds(pl.multiple_of(w * LANES, LANES), LANES)
            return pltpu.make_async_copy(held.at[w], msg_any.at[:, :, here], sems.at[w])

        def turn(w):
            here = pl.ds(w * LANES, LANES)

            def turned(a):
                return a.reshape(RL, XE, YG)[:, H : H + X].reshape(LANES, YG).T

            v = turned(tracer_step * uv_ref[1, pl.ds(w * RL + 2, RL)])
            new = []
            for t in range(T):
                c = turned(mid_pad[t, rows(w * RL + 2, RL * XE)])
                new.append(part[t, here].T - sideways(c, v, 0))
                adv_ref[t, :, here] = new[t]
            for d in range(ntrc):
                there = [new[t][d * Y : (d + 1) * Y] for t in range(T)]
                held[w, d] = jnp.concatenate(there, axis=0).astype(jnp.bfloat16)
            sending(w).start()

        def block(w, carry):
            return second_step(w * RL, carry)

        count = DX // LANES
        lax.fori_loop(0, count, block, (c[2], c[3], c[2] + half, flux))
        for w in range(count):
            turn(w)
        for w in range(count):
            sending(w).wait()

    vmem = pl.BlockSpec(memory_space=pltpu.VMEM)
    advected, message, uv, fv = call(
        advect,
        (f32(T, YG, DX), pltpu.HBM((ntrc, T * Y, DX), jnp.bfloat16))
        + (f32(2, D + 4, XE, YG), f32(D + 5, XE, YG)),
        (near_uv, masks, own_levels, far_levels, pad, side),
        scratch=(
            pltpu.VMEM((T, (D + 4) * XE, YG), F32),
            pltpu.VMEM((T, DX, YG), F32),
            pltpu.VMEM((DX // LANES, ntrc, T * Y, LANES), jnp.bfloat16),
            pltpu.SemaphoreType.DMA((DX // LANES,)),
        ),
        outs=(vmem, pl.BlockSpec(memory_space=pltpu.HBM), vmem, vmem),
        name="advect_tracers",
    )
    message, lo, hi = lax.optimization_barrier((message, lo, hi))
    gathered = lax.all_to_all(message, "trc", split_axis=0, concat_axis=0, tiled=True)
    ring = [(i, (i + 1) % ntrc) for i in range(ntrc)]
    south = lax.ppermute(hi, "trc", ring)
    north = lax.ppermute(lo, "trc", [(b, a) for a, b in ring])
    gathered, south, north = lax.optimization_barrier((gathered, south, north))

    def ocean(
        t_ref, s_ref, uv_ref, fv_ref, l_ref, so_ref, no_ref, sa_ref, wa_ref, ua_ref, va_ref, turn
    ):
        me, lev = lax.axis_index("trc"), lax.axis_index("lev")
        for x in range(XE):
            def level_rows(ref, first):
                return ref[pl.ds(first * XE + x, D, stride=XE), :]

            turn[0, x] = level_rows(uv_ref.at[0], 2).T
            turn[1, x] = level_rows(uv_ref.at[1], 2).T
            turn[2, x] = level_rows(fv_ref, 2).T
            turn[3, x] = level_rows(fv_ref, 3).T
        here = pl.ds(pl.multiple_of(me * Y, 8), Y)
        past = pl.ds(pl.multiple_of(lax.rem(me + ntrc - 1, ntrc) * Y, 8), Y)
        u, v, w, w_next = (turn[i, :, here] for i in range(4))
        v_south = turn[1, :, past][:, Y - 1 : Y]
        level = lax.broadcasted_iota(jnp.int32, (XE, Y, D), 2)
        row = lax.broadcasted_iota(jnp.int32, (XE, Y, D), 1)

        def east(a):
            return jnp.concatenate([a[1:], a[:1]], axis=0)

        def west(a):
            return jnp.concatenate([a[-1:], a[:-1]], axis=0)

        def donor(speed, near, far):
            return jnp.maximum(speed, 0.0) * near + jnp.minimum(speed, 0.0) * far

        def advance(c, i):
            so = jnp.stack([so_ref[i * XE + x : i * XE + x + 1] for x in range(XE)])
            no = jnp.stack([no_ref[i * XE + x : i * XE + x + 1] for x in range(XE)])
            tile = l_ref[4 * T * XE + i * Y : 4 * T * XE + (i + 1) * Y]
            edge = jnp.stack([tile[:, x : x + 1] for x in range(XE)])
            wide = jnp.concatenate([c, jnp.zeros((XE, Y, LANES - D), F32)], axis=2) if D < LANES else c
            upper = shift(wide, -1, 2)[:, :, :D]
            upper = jnp.where(level == 0, jnp.where(lev > 0, edge, 0.0), upper)
            lower = shift(wide, 1, 2)[:, :, :D]
            lower = jnp.where(level == D - 1, jnp.where(lev < nlev - 1, edge, 0.0), lower)
            fe = donor(u, c, east(c))
            fn = donor(v, c, jnp.where(row == Y - 1, no, shift(c, 1, 1)))
            fn_south = jnp.where(row == 0, donor(v_south, so, c[:, 0:1]), shift(fn, -1, 1))
            fall = donor(w_next, c, lower) - donor(w, upper, c)
            return c - marine_advance * ((fe - west(fe)) + (fn - fn_south) + fall)

        sa_ref[...] = advance(s_ref[...], 1)[H : H + X]
        wa_ref[...] = advance(t_ref[...], 0)[H : H + X]
        ua_ref[...] = u[H : H + X]
        va_ref[...] = v[H : H + X]

    saltiness_final, warmth_moved, zonal_speed_final, meridional_speed_final = call(
        ocean,
        (f32(X, Y, D),) * 4,
        (
            warmth,
            salt,
            uv.reshape(2, (D + 4) * XE, YG),
            fv.reshape((D + 5) * XE, YG),
            far_outer,
            south,
            north,
        ),
        scratch=(pltpu.VMEM((4, XE, YG, D), F32),),
        name="own_ocean",
    )

    speed_most = speed_bound + marine_advance * (
        2 * buoyancy * hydro_bound * D * nlev + viscosity * 8 * speed_bound
    )
    growth = 1 + 4 * tracer_step * speed_most + 2 * level_step * (4 * speed_most * D * nlev)
    react_most = NT * coupling_bound * species_bound * growth**2
    unit = 2.0 ** max(0, math.ceil(math.log2(react_most / 65504.0)))

    def spread_columns(c_ref, o_ref):
        n = NT * Y

        def pick(shape, along):
            wide, narrow = (lax.broadcasted_iota(jnp.int32, shape, d) for d in (along, 1 - along))
            return jnp.where(wide // Y == narrow, 1.0, 0.0).astype(jnp.bfloat16)

        tall = jnp.dot(pick((n, NT), 0), c_ref[...], preferred_element_type=F32)
        full = jnp.dot(
            tall.astype(jnp.bfloat16), pick((NT, n), 1), preferred_element_type=F32
        )
        row, lane = (lax.broadcasted_iota(jnp.int32, (n, n), d) for d in (0, 1))
        o_ref[...] = jnp.where(row % Y == lane % Y, full, 0.0).astype(jnp.bfloat16)

    spread = call(
        spread_columns,
        jax.ShapeDtypeStruct((NT * Y, NT * Y), jnp.bfloat16),
        (coupling_matrix,),
        name="spread_coupling",
    )
    flat_tracers = gathered.reshape(NT * Y, DX)
    reaction = jnp.dot(spread, flat_tracers, preferred_element_type=F32)
    reaction = (reaction * (1.0 / unit)).astype(jnp.float16).reshape(ntrc, T * Y, DX)
    returned = lax.all_to_all(reaction, "trc", split_axis=0, concat_axis=0, tiled=True)

    def shade(x_ref, g_ref, k_ref, att_ref, cum_ref):
        att = jnp.zeros((Y, DX), F32)
        for d in range(ntrc):
            rows = x_ref[d].astype(F32)
            for t in range(T):
                att = att + k_ref[g_ref[d * T + t]] * rows[t * Y : (t + 1) * Y]
        att_ref[...] = att
        lane = lax.broadcasted_iota(jnp.int32, (Y, DX), 1)
        total = att
        width = X
        while width < DX:
            total = total + jnp.where(lane < width, 0.0, shift(total, -width, 1))
            width *= 2
        cum_ref[...] = total

    smem = pl.BlockSpec(memory_space=pltpu.SMEM)
    attenuation, shaded = call(
        shade,
        (f32(Y, DX), f32(Y, DX)),
        (gathered, species_guild_number, guild_extinction_coefficient),
        specs=[vmem, smem, smem],
        name="shade",
    )
    far_shade = exchange_levels(shaded)

    def heat(att_ref, cum_ref, r_ref, w_ref, m_ref, o_ref, turn):
        lane = lax.broadcasted_iota(jnp.int32, (Y, LANES), 1)
        keep = (lax.axis_index("lev") > 0) & (lane >= LANES - X)
        above = jnp.where(keep, r_ref[:, DX - LANES :], 0.0)
        width = X
        while width < LANES:
            above = above + shift(above, width, 1)
            width *= 2
        att = att_ref[...]
        path = jnp.concatenate([above] * (DX // LANES), axis=1) + cum_ref[...] - att
        turn[...] = (jnp.exp(-path) * (1.0 - jnp.exp(-att))).T
        for x in range(X):
            absorbed = turn[pl.ds(x, D, stride=X), :].T
            o_ref[x] = w_ref[x] + warming_amount * (m_ref[x].astype(F32) * absorbed)

    warmth_final = call(
        heat,
        f32(X, Y, D),
        (attenuation, shaded, far_shade, warmth_moved, jnp.transpose(marine_indicator, (1, 2, 0))),
        scratch=(pltpu.VMEM((DX, Y), F32),),
        name="heat",
    )

    def finish(r_ref, a_ref, o_any, o_ref, sems):
        copies = [pltpu.make_async_copy(o_ref.at[t], o_any.at[t], sems.at[t]) for t in range(T)]
        for t in range(T):
            for w in range(DX // LANES):
                rows = [
                    r_ref[d, t * Y : (t + 1) * Y, w * LANES : (w + 1) * LANES] for d in range(ntrc)
                ]
                here = slice(w * LANES, (w + 1) * LANES)
                o_ref[t, here] = (a_ref[t, :, here] + (react_step * unit) * jnp.concatenate(rows, axis=0)).T
            copies[t].start()
        for copy in copies:
            copy.wait()

    species_final = call(
        finish,
        f32(T, DX, YG),
        (returned.astype(F32), advected),
        scratch=(pltpu.VMEM((T, DX, YG), F32), pltpu.SemaphoreType.DMA((T,))),
        name="finish_tracers",
        outs=pl.BlockSpec(memory_space=pl.ANY),
    )
    ocean_outputs = (warmth_final, saltiness_final, zonal_speed_final, meridional_speed_final)
    ocean_outputs = tuple(jnp.transpose(a, (2, 0, 1)) for a in ocean_outputs)
    return ocean_outputs + (species_final.reshape(T, D, X, YG),)


def solution(mesh):
    ocean = P("lev", "cols", "trc")
    in_specs = (ocean,) * 5 + (P("trc", "lev", "cols", None), P(), P(), P())
    out_specs = (ocean,) * 4 + (P("trc", "lev", "cols", None),)
    return jax.shard_map(shards, mesh=mesh, in_specs=in_specs, out_specs=out_specs, check_vma=False)
```

```python
import math

import jax
import jax.numpy as jnp
from jax import lax
from jax.experimental import pallas as pl
from jax.experimental.pallas import tpu as pltpu
from jax.sharding import PartitionSpec as P

viscosity = 0.2
buoyancy = 0.25
marine_advance = 0.05
tracer_step = 0.2
level_step = 0.04
react_step = 0.25
warming_amount = 60.0

speed_bound = 3.0
hydro_bound = 6.0
species_bound = 2.0
coupling_bound = 0.75

LANES = 128
DRY = 1e30
F32 = jnp.float32


def call(kernel, out_shape, args, specs=None, scratch=(), name=None, mib=16, outs=None):
    vmem = pl.BlockSpec(memory_space=pltpu.VMEM)
    outs = jax.tree.map(lambda _: vmem, out_shape) if outs is None else outs
    return pl.pallas_call(
        kernel,
        out_shape=out_shape,
        in_specs=[vmem] * len(args) if specs is None else specs,
        out_specs=outs,
        scratch_shapes=list(scratch),
        compiler_params=pltpu.CompilerParams(vmem_limit_bytes=mib * 1024 * 1024),
        name=name,
    )(*args)


def f32(*shape):
    return jax.ShapeDtypeStruct(shape, F32)


def shift(a, steps, axis):
    return pltpu.roll(a, (-steps) % a.shape[axis], axis)


def minmod(p, r):
    return jnp.maximum(jnp.minimum(p, r), jnp.minimum(jnp.maximum(p, r), 0.0))


def sideways(c, speed, axis):
    d = 0.5 * (shift(c, 1, axis) - c)
    half = minmod(shift(d, -1, axis), d)
    flux = speed * jnp.where(speed > 0.0, c + half, shift(c - half, 1, axis))
    return flux - shift(flux, -1, axis)


def exchange_levels(part):
    return lax.ppermute(part, "lev", [(0, 1), (1, 0)])


def shards(
    potential_warmth,
    saltiness_anomaly,
    zonal_speed,
    meridional_speed,
    marine_indicator,
    species_concentrations,
    coupling_matrix,
    species_guild_number,
    guild_extinction_coefficient,
):
    cols, ntrc, nlev = lax.axis_size("cols"), lax.axis_size("trc"), lax.axis_size("lev")
    D, X, Y = potential_warmth.shape
    T = species_concentrations.shape[0]
    NT = coupling_matrix.shape[0]
    YG = species_concentrations.shape[3]
    assert nlev == 2 and YG == LANES and X % 8 == 0 and Y % 8 == 0 and ntrc % 2 == 0
    assert LANES % D == 0 and D % 8 == 0 and X % (2 * LANES // D) == 0
    H = X if cols > 1 else 0
    XE = X + 2 * H
    W, DX = D * XE, D * X
    G = LANES // D
    XL = XE // G
    RL = LANES // X

    def widen(block, dim):
        if H == 0:
            return block
        ahead = [(i, (i + 1) % cols) for i in range(cols)]
        back = [(i, (i - 1) % cols) for i in range(cols)]
        low = lax.ppermute(block, "cols", ahead)
        high = lax.ppermute(block, "cols", back)
        return jnp.concatenate([low, block, high], axis=dim)

    warmth, salt, zonal, merid, marine = (
        widen(jnp.transpose(a, (1, 2, 0)), 0)
        for a in (potential_warmth, saltiness_anomaly, zonal_speed, meridional_speed, marine_indicator)
    )
    species = widen(species_concentrations, 2)
    NP = ntrc // 2
    pairs_apart = [[2 * g + c for g in range(NP)] for c in range(2)]

    ROWS = XL * Y
    MOST = 2**20 - 1
    DRY_CODE = -(2**20)
    SCALES = 31

    def top(bound):
        return 2.0 ** math.ceil(math.log2(bound))

    tops = (top(hydro_bound * 1.001), top(speed_bound), top(speed_bound))

    def pack(t_any, s_any, u_any, v_any, m_any, c_any, pay_ref, lo_ref, hi_ref, out_ref, held, wet, sems):
        upper = lax.axis_index("lev") == 0
        first = pl.multiple_of(jnp.where(upper, D - 4, 0) * XE, 8)
        copies = [
            pltpu.make_async_copy(a, held.at[i], sems.at[i])
            for i, a in enumerate((t_any, s_any, u_any, v_any))
        ]
        copies.append(pltpu.make_async_copy(m_any, wet, sems.at[4]))
        for t in range(T):
            copies.append(
                pltpu.make_async_copy(
                    c_any.at[t, pl.ds(first, 4 * XE)],
                    out_ref.at[pl.ds(t * 4 * XE, 4 * XE)],
                    sems.at[5 + t],
                )
            )
        for copy in copies:
            copy.start()
        for copy in copies:
            copy.wait()
        t, s = held[0], held[1]
        sea = wet[...] > 0
        density = jnp.where(sea, 0.8 * s - 0.2 * t, 0.0)
        numbers, halves = 0, []
        for i, a in enumerate((density, held[2], held[3])):
            most = jnp.max(jnp.abs(a), axis=(0, 1, 2), keepdims=True)[0]
            unit, number = tops[i], 0
            for k in range(1, SCALES + 1):
                fits = most <= tops[i] * 2.0**-k
                unit = jnp.where(fits, tops[i] * 2.0**-k, unit)
                number = jnp.where(fits, k, number)
            code = jnp.floor(jnp.clip(a * (1.0 / unit), -1.0, 1.0) * MOST + 0.5).astype(jnp.int32)
            if i == 0:
                code = jnp.where(sea, code, DRY_CODE)
            numbers = numbers + number * 32**i
            code = jnp.concatenate([code[g * XL : (g + 1) * XL] for g in range(G)], axis=2)
            halves.append(code.reshape(XL * Y, LANES))
        density, u, v = halves
        lane = lax.broadcasted_iota(jnp.int32, (XL * Y, LANES), 1)
        bit = lax.shift_right_logical(numbers, lane % 16) & 1
        first = lax.shift_left(u, 11) | (lax.shift_right_arithmetic(v, 10) & 2047)
        second = lax.shift_left(v & 1023, 22) | lax.shift_left(density & (2**21 - 1), 1) | bit
        rows = jnp.concatenate([first, second], axis=0)
        for g in range(NP):
            pay_ref[g] = rows
        lane = lax.broadcasted_iota(jnp.int32, (Y, LANES), 1)
        for i, a in enumerate((t, s)):
            edge = jnp.zeros((Y, LANES), F32)
            for x in range(XE):
                lo_ref[i * XE + x : i * XE + x + 1] = a[x, 0:1]
                hi_ref[i * XE + x : i * XE + x + 1] = a[x, Y - 1 : Y]
                column = jnp.where(upper, a[x, :, D - 1 : D], a[x, :, 0:1])
                edge = jnp.where(lane == x, column, edge)
            out_ref[4 * T * XE + i * Y : 4 * T * XE + (i + 1) * Y] = edge

    species = species.reshape(T, W, YG)
    payload, lo, hi, outer = call(
        pack,
        (
            jax.ShapeDtypeStruct((NP, 2 * ROWS, LANES), jnp.int32),
            f32(2 * XE, D),
            f32(2 * XE, D),
            f32(4 * T * XE + 2 * Y, LANES),
        ),
        (warmth, salt, zonal, merid, marine, species),
        specs=[pl.BlockSpec(memory_space=pl.ANY)] * 6,
        scratch=(
            pltpu.VMEM((4, XE, Y, D), F32),
            pltpu.VMEM((XE, Y, D), jnp.int32),
            pltpu.SemaphoreType.DMA((5 + T,)),
        ),
        name="pack_ocean",
        mib=60,
    )
    mine = lax.all_to_all(
        payload, "trc", split_axis=0, concat_axis=0, tiled=True, axis_index_groups=pairs_apart
    )
    far_outer = exchange_levels(outer)


    def rows(k, n=XE):
        return pl.ds(pl.multiple_of(k * XE, 8), n)

    def widen_levels(c_ref, h_ref, pad, sem):
        lev = lax.axis_index("lev")
        copy = pltpu.make_async_copy(c_ref, pad.at[:, pl.ds(4 * XE, W)], sem)
        copy.start()
        for t in range(T):
            outer = h_ref[t * 4 * XE : (t + 1) * 4 * XE]
            pad[t, 0 : 4 * XE] = jnp.where(lev > 0, outer, 0.0)
            pad[t, (D + 4) * XE :] = jnp.where(lev < nlev - 1, outer, 0.0)
        copy.wait()

    pad = call(
        widen_levels,
        f32(T, (D + 8) * XE, YG),
        (species, far_outer),
        specs=[pl.BlockSpec(memory_space=pl.ANY), pl.BlockSpec(memory_space=pltpu.VMEM)],
        scratch=(pltpu.SemaphoreType.DMA(()),),
        name="widen_levels",
    )
    mine, pad = lax.optimization_barrier((mine, pad))
    other = lax.ppermute(mine, "trc", [(i, i ^ 1) for i in range(ntrc)])

    def plane(ref, i):
        return ref[i * XE : (i + 1) * XE]

    def dense(raw):
        return jnp.where(raw < 0.5 * DRY, raw, 0.0)

    def beside(a, axis):
        return shift(a, 1, axis) + shift(a, -1, axis)

    def faces(raw, speeds, along_y, before):
        wet = jnp.where(raw < 0.5 * DRY, 1.0, 0.0)
        d = dense(raw)
        total = before + d
        p = buoyancy * (total - 0.5 * d)
        result = []
        for axis, (a, sides) in enumerate(zip(speeds, along_y)):
            mask = wet * shift(wet, 1, axis)
            lap = beside(a, 0) + sides - 4.0 * a
            push = viscosity * lap - (shift(p, 1, axis) - p)
            result.append((mask * (a + marine_advance * push), mask))
        return total, result

    def unpack(a_ref, b_ref, uv_ref, mask_ref, l_ref, f_ref):
        core = lax.axis_index("trc") % 2
        lane = lax.broadcasted_iota(jnp.int32, (YG, LANES), 1)

        def words(at):
            rows = []
            for g in range(NP):
                a, b = a_ref[g, at : at + Y], b_ref[g, at : at + Y]
                rows += [jnp.where(core == 0, a, b), jnp.where(core == 0, b, a)]
            return jnp.concatenate(rows, axis=0)

        bits = words(ROWS) & 1
        numbers = jnp.sum(jnp.where(lane < 16, lax.shift_left(bits, lane % 16), 0), axis=1, keepdims=True)
        units = []
        for i in range(3):
            number = lax.shift_right_logical(numbers, 5 * i) & 31
            unit = jnp.full((YG, 1), tops[i] / MOST, F32)
            for b in range(5):
                unit = jnp.where(lax.shift_right_logical(number, b) & 1 > 0, unit * 2.0 ** -(2**b), unit)
            units.append(unit)

        def put(f, x, a):
            turned = a.T
            for g in range(G):
                f_ref[f, pl.ds(x + g * XL, D, stride=XE), :] = turned[g * D : (g + 1) * D]

        for x in range(XL):
            first, second = words(x * Y), words(ROWS + x * Y)
            u = lax.shift_right_arithmetic(first, 11)
            v = lax.shift_right_arithmetic(lax.shift_left(first, 21), 21)
            v = lax.shift_left(v, 10) | lax.shift_right_logical(second, 22)
            density = lax.shift_right_arithmetic(lax.shift_left(second, 10), 11)
            put(0, x, jnp.where(density == DRY_CODE, DRY, density.astype(F32) * units[0]))
            for i, a in enumerate((u, v)):
                a = a.astype(F32) * units[1 + i]
                put(1 + i, x, a)
                put(3 + i, x, beside(a, 0))

        def field(f, k):
            return f_ref[f, pl.ds(pl.multiple_of(k * XE, 8), XE)]

        def one(k, carry):
            total, sums = carry
            f = [field(i, k) for i in range(5)]
            total, new = faces(f[0], f[1:3], f[3:5], total)
            for i, (speed, mask) in enumerate(new):
                uv_ref[i, k] = speed
                mask_ref[i, k] = mask
            parts = (new[0][0], new[1][0], new[0][1], new[1][1])
            return total, tuple(a + b for a, b in zip(sums, parts))

        zero = jnp.zeros((XE, YG), F32)
        total, sums = lax.fori_loop(0, D, one, (zero, (zero,) * 4), unroll=D)
        for i, a in enumerate((total,) + sums):
            l_ref[i * XE : (i + 1) * XE] = a
        first = jnp.where(lax.axis_index("lev") == 0, D - 2, 0)
        for f in range(3):
            for k in range(2):
                at = (5 + 2 * f + k) * XE
                l_ref[at : at + XE] = field(f, first + k)

    near_uv, masks, own_levels = call(
        unpack,
        (f32(2, D, XE, YG), f32(2, D, XE, YG), f32(11 * XE, YG)),
        (mine, other),
        scratch=(pltpu.VMEM((5, W, YG), F32),),
        name="unpack_ocean",
    )
    own_levels, pad = lax.optimization_barrier((own_levels, pad))
    far_levels = exchange_levels(own_levels)

    def half_slope(lo, mid, hi):
        return minmod(0.5 * (mid - lo), 0.5 * (hi - mid))

    def edges(c, axis):
        d = 0.5 * (shift(c, 1, axis) - c)
        half = minmod(shift(d, -1, axis), d)
        return c + half, shift(c - half, 1, axis)

    def slopes(pad, side):
        def one(k, carry):
            lo, mid = carry
            hi = pad[:, rows(k + 2)]
            half = half_slope(lo, mid, hi)
            values = edges(mid, 1) + edges(mid, 2) + (mid + half, mid - half)
            for i, a in enumerate(values):
                side[i, :, rows(k)] = a
            return mid, hi

        count = D + 6
        first = (pad[:, 0:XE], pad[:, XE : 2 * XE])
        lax.fori_loop(0, count, one, first, unroll=count // 5)

    side = call(slopes, f32(6, T, (D + 6) * XE, YG), (pad,), name="first_slopes")
    far_levels, side = lax.optimization_barrier((far_levels, side))

    def speeds(n_ref, m_ref, o_ref, r_ref, uv_ref, fv_ref):
        lev = lax.axis_index("lev")
        above = jnp.where(lev > 0, plane(r_ref, 0), 0.0)
        sum_here = plane(o_ref, 0)

        def pushes(a):
            return [-marine_advance * buoyancy * (shift(a, 1, i) - a) for i in range(2)]

        def spread_out(u, v):
            return u - shift(u, -1, 0) + v - shift(v, -1, 1)

        def far(e, total):
            k = e % 2 if e < 2 else e - D - 2
            speeds = plane(r_ref, 7 + k), plane(r_ref, 9 + k)
            sides = [beside(a, 1) for a in speeds]
            total, new = faces(plane(r_ref, 5 + k), speeds, sides, total)
            for i in range(2):
                uv_ref[i, e] = new[i][0]
            return total

        total = above - dense(plane(r_ref, 5)) - dense(plane(r_ref, 6))
        for e in (0, 1):
            total = far(e, total)
        total = above + sum_here
        for e in (D + 2, D + 3):
            total = far(e, total)

        push = pushes(sum_here)
        lower = [plane(r_ref, 1 + i) + plane(r_ref, 3 + i) * push[i] for i in range(2)]
        below = jnp.where(lev < nlev - 1, spread_out(*lower), 0.0)

        def divergence(e):
            return spread_out(uv_ref[0, e], uv_ref[1, e])

        fv_ref[D + 2] = below
        fv_ref[D + 3] = below - divergence(D + 2)
        fv_ref[D + 4] = below - divergence(D + 2) - divergence(D + 3)
        push = pushes(above)

        def climb(j, total):
            k = D - 1 - j
            new = [n_ref[i, k] + m_ref[i, k] * push[i] for i in range(2)]
            for i in range(2):
                uv_ref[i, k + 2] = new[i]
            total = total + spread_out(*new)
            fv_ref[k + 2] = total
            return total

        total = lax.fori_loop(0, D, climb, below, unroll=D)
        fv_ref[2] = jnp.where(lev == 0, 0.0, total)
        for e in (1, 0):
            total = total + divergence(e)
            fv_ref[e] = total

    def advect(n_ref, m_ref, o_ref, r_ref, pad, side, adv_ref, msg_any, uv_ref, fv_ref, mid_pad, part, held, sems):
        speeds(n_ref, m_ref, o_ref, r_ref, uv_ref, fv_ref)

        def speeds_at(e):
            return tracer_step * uv_ref[0, e][None], tracer_step * uv_ref[1, e][None]

        def fall(e, up, low):
            w = level_step * fv_ref[e]
            return w * jnp.where(w > 0.0, up, low)

        def first_step(e, flux):
            k = rows(e + 1)
            flux_next = fall(e + 1, side[4, :, k], side[5, :, rows(e + 2)])
            change = flux_next - flux
            for i, speed in enumerate(speeds_at(e)):
                f = speed * jnp.where(speed > 0.0, side[2 * i, :, k], side[2 * i + 1, :, k])
                change = change + (f - shift(f, -1, i + 1))
            mid_pad[:, rows(e)] = pad[:, rows(e + 2)] - change
            return flux_next

        flux = fall(0, side[4, :, rows(0)], side[5, :, rows(1)])
        lax.fori_loop(0, D + 4, first_step, flux, unroll=D + 4)

        def second_step(k, carry):
            B = RL
            here = mid_pad[:, rows(k + 2, B * XE)].reshape(T, B, XE, YG)
            u = tracer_step * uv_ref[0, pl.ds(k + 2, B)]
            flat = sideways(here, u, 2)
            mid, hi, up, flux = carry
            for j in range(B):
                nxt = mid_pad[:, rows(k + j + 4)]
                half = half_slope(mid, hi, nxt)
                flux_next = fall(k + j + 3, up, hi - half)
                new = mid - (flat[:, j] + (flux_next - flux))
                part[:, pl.ds(pl.multiple_of((k + j) * X, 8), X)] = new[:, H : H + X]
                mid, hi, up, flux = hi, nxt, hi + half, flux_next
            return mid, hi, up, flux

        c = [mid_pad[:, rows(k)] for k in range(4)]
        half = half_slope(c[1], c[2], c[3])
        flux = fall(2, c[1] + half_slope(c[0], c[1], c[2]), c[2] - half)

        def sending(w):
            here = pl.ds(pl.multiple_of(w * LANES, LANES), LANES)
            return pltpu.make_async_copy(held.at[w], msg_any.at[:, :, here], sems.at[w])

        def turn(w):
            here = pl.ds(w * LANES, LANES)

            def turned(a):
                return a.reshape(RL, XE, YG)[:, H : H + X].reshape(LANES, YG).T

            v = turned(tracer_step * uv_ref[1, pl.ds(w * RL + 2, RL)])
            new = []
            for t in range(T):
                c = turned(mid_pad[t, rows(w * RL + 2, RL * XE)])
                new.append(part[t, here].T - sideways(c, v, 0))
                adv_ref[t, :, here] = new[t]
            for d in range(ntrc):
                there = [new[t][d * Y : (d + 1) * Y] for t in range(T)]
                held[w, d] = jnp.concatenate(there, axis=0).astype(jnp.bfloat16)
            sending(w).start()

        def block(w, carry):
            return second_step(w * RL, carry)

        count = DX // LANES
        lax.fori_loop(0, count, block, (c[2], c[3], c[2] + half, flux))
        for w in range(count):
            turn(w)
        for w in range(count):
            sending(w).wait()

    vmem = pl.BlockSpec(memory_space=pltpu.VMEM)
    advected, message, uv, fv = call(
        advect,
        (f32(T, YG, DX), pltpu.HBM((ntrc, T * Y, DX), jnp.bfloat16))
        + (f32(2, D + 4, XE, YG), f32(D + 5, XE, YG)),
        (near_uv, masks, own_levels, far_levels, pad, side),
        scratch=(
            pltpu.VMEM((T, (D + 4) * XE, YG), F32),
            pltpu.VMEM((T, DX, YG), F32),
            pltpu.VMEM((DX // LANES, ntrc, T * Y, LANES), jnp.bfloat16),
            pltpu.SemaphoreType.DMA((DX // LANES,)),
        ),
        outs=(vmem, pl.BlockSpec(memory_space=pltpu.HBM), vmem, vmem),
        name="advect_tracers",
    )
    message, lo, hi = lax.optimization_barrier((message, lo, hi))
    gathered = lax.all_to_all(message, "trc", split_axis=0, concat_axis=0, tiled=True)
    ring = [(i, (i + 1) % ntrc) for i in range(ntrc)]
    south = lax.ppermute(hi, "trc", ring)
    north = lax.ppermute(lo, "trc", [(b, a) for a, b in ring])
    gathered, south, north = lax.optimization_barrier((gathered, south, north))

    def ocean(
        t_ref, s_ref, uv_ref, fv_ref, l_ref, so_ref, no_ref, sa_ref, wa_ref, ua_ref, va_ref, turn
    ):
        me, lev = lax.axis_index("trc"), lax.axis_index("lev")
        for x in range(XE):
            def level_rows(ref, first):
                return ref[pl.ds(first * XE + x, D, stride=XE), :]

            turn[0, x] = level_rows(uv_ref.at[0], 2).T
            turn[1, x] = level_rows(uv_ref.at[1], 2).T
            turn[2, x] = level_rows(fv_ref, 2).T
            turn[3, x] = level_rows(fv_ref, 3).T
        here = pl.ds(pl.multiple_of(me * Y, 8), Y)
        past = pl.ds(pl.multiple_of(lax.rem(me + ntrc - 1, ntrc) * Y, 8), Y)
        u, v, w, w_next = (turn[i, :, here] for i in range(4))
        v_south = turn[1, :, past][:, Y - 1 : Y]
        level = lax.broadcasted_iota(jnp.int32, (XE, Y, D), 2)
        row = lax.broadcasted_iota(jnp.int32, (XE, Y, D), 1)

        def east(a):
            return jnp.concatenate([a[1:], a[:1]], axis=0)

        def west(a):
            return jnp.concatenate([a[-1:], a[:-1]], axis=0)

        def donor(speed, near, far):
            return jnp.maximum(speed, 0.0) * near + jnp.minimum(speed, 0.0) * far

        def advance(c, i):
            so = jnp.stack([so_ref[i * XE + x : i * XE + x + 1] for x in range(XE)])
            no = jnp.stack([no_ref[i * XE + x : i * XE + x + 1] for x in range(XE)])
            tile = l_ref[4 * T * XE + i * Y : 4 * T * XE + (i + 1) * Y]
            edge = jnp.stack([tile[:, x : x + 1] for x in range(XE)])
            wide = jnp.concatenate([c, jnp.zeros((XE, Y, LANES - D), F32)], axis=2) if D < LANES else c
            upper = shift(wide, -1, 2)[:, :, :D]
            upper = jnp.where(level == 0, jnp.where(lev > 0, edge, 0.0), upper)
            lower = shift(wide, 1, 2)[:, :, :D]
            lower = jnp.where(level == D - 1, jnp.where(lev < nlev - 1, edge, 0.0), lower)
            fe = donor(u, c, east(c))
            fn = donor(v, c, jnp.where(row == Y - 1, no, shift(c, 1, 1)))
            fn_south = jnp.where(row == 0, donor(v_south, so, c[:, 0:1]), shift(fn, -1, 1))
            fall = donor(w_next, c, lower) - donor(w, upper, c)
            return c - marine_advance * ((fe - west(fe)) + (fn - fn_south) + fall)

        sa_ref[...] = advance(s_ref[...], 1)[H : H + X]
        wa_ref[...] = advance(t_ref[...], 0)[H : H + X]
        ua_ref[...] = u[H : H + X]
        va_ref[...] = v[H : H + X]

    saltiness_final, warmth_moved, zonal_speed_final, meridional_speed_final = call(
        ocean,
        (f32(X, Y, D),) * 4,
        (
            warmth,
            salt,
            uv.reshape(2, (D + 4) * XE, YG),
            fv.reshape((D + 5) * XE, YG),
            far_outer,
            south,
            north,
        ),
        scratch=(pltpu.VMEM((4, XE, YG, D), F32),),
        name="own_ocean",
    )

    speed_most = speed_bound + marine_advance * (
        2 * buoyancy * hydro_bound * D * nlev + viscosity * 8 * speed_bound
    )
    growth = 1 + 4 * tracer_step * speed_most + 2 * level_step * (4 * speed_most * D * nlev)
    react_most = NT * coupling_bound * species_bound * growth**2
    unit = 2.0 ** max(0, math.ceil(math.log2(react_most / 65504.0)))

    def spread_columns(c_ref, o_ref):
        n = NT * Y

        def pick(shape, along):
            wide, narrow = (lax.broadcasted_iota(jnp.int32, shape, d) for d in (along, 1 - along))
            return jnp.where(wide // Y == narrow, 1.0, 0.0).astype(jnp.bfloat16)

        tall = jnp.dot(pick((n, NT), 0), c_ref[...], preferred_element_type=F32)
        full = jnp.dot(
            tall.astype(jnp.bfloat16), pick((NT, n), 1), preferred_element_type=F32
        )
        row, lane = (lax.broadcasted_iota(jnp.int32, (n, n), d) for d in (0, 1))
        o_ref[...] = jnp.where(row % Y == lane % Y, full, 0.0).astype(jnp.bfloat16)

    spread = call(
        spread_columns,
        jax.ShapeDtypeStruct((NT * Y, NT * Y), jnp.bfloat16),
        (coupling_matrix,),
        name="spread_coupling",
    )
    flat_tracers = gathered.reshape(NT * Y, DX)
    reaction = jnp.dot(spread, flat_tracers, preferred_element_type=F32)
    reaction = (reaction * (1.0 / unit)).astype(jnp.float16).reshape(ntrc, T * Y, DX)
    returned = lax.all_to_all(reaction, "trc", split_axis=0, concat_axis=0, tiled=True)

    def shade(x_ref, g_ref, k_ref, att_ref, cum_ref):
        att = jnp.zeros((Y, DX), F32)
        for d in range(ntrc):
            rows = x_ref[d].astype(F32)
            for t in range(T):
                att = att + k_ref[g_ref[d * T + t]] * rows[t * Y : (t + 1) * Y]
        att_ref[...] = att
        lane = lax.broadcasted_iota(jnp.int32, (Y, DX), 1)
        total = att
        width = X
        while width < DX:
            total = total + jnp.where(lane < width, 0.0, shift(total, -width, 1))
            width *= 2
        cum_ref[...] = total

    smem = pl.BlockSpec(memory_space=pltpu.SMEM)
    attenuation, shaded = call(
        shade,
        (f32(Y, DX), f32(Y, DX)),
        (gathered, species_guild_number, guild_extinction_coefficient),
        specs=[vmem, smem, smem],
        name="shade",
    )
    far_shade = exchange_levels(shaded)

    def heat(att_ref, cum_ref, r_ref, w_ref, m_ref, o_ref, turn):
        lane = lax.broadcasted_iota(jnp.int32, (Y, LANES), 1)
        keep = (lax.axis_index("lev") > 0) & (lane >= LANES - X)
        above = jnp.where(keep, r_ref[:, DX - LANES :], 0.0)
        width = X
        while width < LANES:
            above = above + shift(above, width, 1)
            width *= 2
        att = att_ref[...]
        path = jnp.concatenate([above] * (DX // LANES), axis=1) + cum_ref[...] - att
        turn[...] = (jnp.exp(-path) * (1.0 - jnp.exp(-att))).T
        for x in range(X):
            absorbed = turn[pl.ds(x, D, stride=X), :].T
            o_ref[x] = w_ref[x] + warming_amount * (m_ref[x].astype(F32) * absorbed)

    warmth_final = call(
        heat,
        f32(X, Y, D),
        (attenuation, shaded, far_shade, warmth_moved, jnp.transpose(marine_indicator, (1, 2, 0))),
        scratch=(pltpu.VMEM((DX, Y), F32),),
        name="heat",
    )

    def finish(r_ref, a_ref, o_any, o_ref, sems):
        copies = [pltpu.make_async_copy(o_ref.at[t], o_any.at[t], sems.at[t]) for t in range(T)]
        for t in range(T):
            for w in range(DX // LANES):
                rows = [
                    r_ref[d, t * Y : (t + 1) * Y, w * LANES : (w + 1) * LANES] for d in range(ntrc)
                ]
                here = slice(w * LANES, (w + 1) * LANES)
                o_ref[t, here] = (a_ref[t, :, here] + (react_step * unit) * jnp.concatenate(rows, axis=0)).T
            copies[t].start()
        for copy in copies:
            copy.wait()

    species_final = call(
        finish,
        f32(T, DX, YG),
        (returned.astype(F32), advected),
        scratch=(pltpu.VMEM((T, DX, YG), F32), pltpu.SemaphoreType.DMA((T,))),
        name="finish_tracers",
        outs=pl.BlockSpec(memory_space=pl.ANY),
    )
    ocean_outputs = (warmth_final, saltiness_final, zonal_speed_final, meridional_speed_final)
    ocean_outputs = tuple(jnp.transpose(a, (2, 0, 1)) for a in ocean_outputs)
    return ocean_outputs + (species_final.reshape(T, D, X, YG),)


def solution(mesh):
    ocean = P("lev", "cols", "trc")
    in_specs = (ocean,) * 5 + (P("trc", "lev", "cols", None), P(), P(), P())
    out_specs = (ocean,) * 4 + (P("trc", "lev", "cols", None),)
    return jax.shard_map(shards, mesh=mesh, in_specs=in_specs, out_specs=out_specs, check_vma=False)
```

```python
import math
import random

import jax
import jax.numpy as jnp
from jax import lax
from jax.experimental import pallas as pl
from jax.experimental.pallas import tpu as pltpu
from jax.sharding import PartitionSpec as P

viscosity = 0.2
buoyancy = 0.25
marine_advance = 0.05
tracer_step = 0.2
level_step = 0.04
react_step = 0.25
warming_amount = 60.0

speed_bound = 3.0
hydro_bound = 6.0
species_bound = 2.0
coupling_bound = 0.75

LANES = 128
DRY = 1e30
F32 = jnp.float32


def call(kernel, out_shape, args, specs=None, scratch=(), name=None, mib=16, outs=None):
    vmem = pl.BlockSpec(memory_space=pltpu.VMEM)
    outs = jax.tree.map(lambda _: vmem, out_shape) if outs is None else outs
    return pl.pallas_call(
        kernel,
        out_shape=out_shape,
        in_specs=[vmem] * len(args) if specs is None else specs,
        out_specs=outs,
        scratch_shapes=list(scratch),
        compiler_params=pltpu.CompilerParams(vmem_limit_bytes=mib * 1024 * 1024),
        name=name,
    )(*args)


def f32(*shape):
    return jax.ShapeDtypeStruct(shape, F32)


def shift(a, steps, axis):
    return pltpu.roll(a, (-steps) % a.shape[axis], axis)


def minmod(p, r):
    return jnp.maximum(jnp.minimum(p, r), jnp.minimum(jnp.maximum(p, r), 0.0))


def sideways(c, speed, axis):
    d = 0.5 * (shift(c, 1, axis) - c)
    half = minmod(shift(d, -1, axis), d)
    flux = speed * jnp.where(speed > 0.0, c + half, shift(c - half, 1, axis))
    return flux - shift(flux, -1, axis)


def exchange_levels(part):
    return lax.ppermute(part, "lev", [(0, 1), (1, 0)])


def shards(
    potential_warmth,
    saltiness_anomaly,
    zonal_speed,
    meridional_speed,
    marine_indicator,
    species_concentrations,
    coupling_matrix,
    species_guild_number,
    guild_extinction_coefficient,
):
    cols, ntrc, nlev = lax.axis_size("cols"), lax.axis_size("trc"), lax.axis_size("lev")
    D, X, Y = potential_warmth.shape
    T = species_concentrations.shape[0]
    NT = coupling_matrix.shape[0]
    YG = species_concentrations.shape[3]
    assert nlev == 2 and YG == LANES and X % 8 == 0 and Y % 8 == 0 and ntrc % 2 == 0
    assert LANES % D == 0 and D % 8 == 0 and X % (2 * LANES // D) == 0
    H = X if cols > 1 else 0
    XE = X + 2 * H
    W, DX = D * XE, D * X
    G = LANES // D
    XL = XE // G
    RL = LANES // X

    def widen(block, dim):
        if H == 0:
            return block
        ahead = [(i, (i + 1) % cols) for i in range(cols)]
        back = [(i, (i - 1) % cols) for i in range(cols)]
        low = lax.ppermute(block, "cols", ahead)
        high = lax.ppermute(block, "cols", back)
        return jnp.concatenate([low, block, high], axis=dim)

    warmth, salt, zonal, merid, marine = (
        widen(jnp.transpose(a, (1, 2, 0)), 0)
        for a in (potential_warmth, saltiness_anomaly, zonal_speed, meridional_speed, marine_indicator)
    )
    species = widen(species_concentrations, 2)
    NP = ntrc // 2
    order = list(range(ntrc))
    random.Random(4).shuffle(order)
    place = [order.index(d) for d in range(ntrc)]
    pairs_apart = [[2 * g + c for g in range(NP)] for c in range(2)]

    ROWS = XL * Y
    MOST = 2**20 - 1
    DRY_CODE = -(2**20)
    SCALES = 31

    def top(bound):
        return 2.0 ** math.ceil(math.log2(bound))

    tops = (top(hydro_bound * 1.001), top(speed_bound), top(speed_bound))

    def pack(t_any, s_any, u_any, v_any, m_any, c_any, pay_ref, lo_ref, hi_ref, out_ref, held, wet, sems):
        upper = lax.axis_index("lev") == 0
        first = pl.multiple_of(jnp.where(upper, D - 4, 0) * XE, 8)
        copies = [
            pltpu.make_async_copy(a, held.at[i], sems.at[i])
            for i, a in enumerate((t_any, s_any, u_any, v_any))
        ]
        copies.append(pltpu.make_async_copy(m_any, wet, sems.at[4]))
        for t in range(T):
            copies.append(
                pltpu.make_async_copy(
                    c_any.at[t, pl.ds(first, 4 * XE)],
                    out_ref.at[pl.ds(t * 4 * XE, 4 * XE)],
                    sems.at[5 + t],
                )
            )
        for copy in copies:
            copy.start()
        for copy in copies:
            copy.wait()
        t, s = held[0], held[1]
        sea = wet[...] > 0
        density = jnp.where(sea, 0.8 * s - 0.2 * t, 0.0)
        numbers, halves = 0, []
        for i, a in enumerate((density, held[2], held[3])):
            most = jnp.max(jnp.abs(a), axis=(0, 1, 2), keepdims=True)[0]
            unit, number = tops[i], 0
            for k in range(1, SCALES + 1):
                fits = most <= tops[i] * 2.0**-k
                unit = jnp.where(fits, tops[i] * 2.0**-k, unit)
                number = jnp.where(fits, k, number)
            code = jnp.floor(jnp.clip(a * (1.0 / unit), -1.0, 1.0) * MOST + 0.5).astype(jnp.int32)
            if i == 0:
                code = jnp.where(sea, code, DRY_CODE)
            numbers = numbers + number * 32**i
            code = jnp.concatenate([code[g * XL : (g + 1) * XL] for g in range(G)], axis=2)
            halves.append(code.reshape(XL * Y, LANES))
        density, u, v = halves
        lane = lax.broadcasted_iota(jnp.int32, (XL * Y, LANES), 1)
        bit = lax.shift_right_logical(numbers, lane % 16) & 1
        first = lax.shift_left(u, 11) | (lax.shift_right_arithmetic(v, 10) & 2047)
        second = lax.shift_left(v & 1023, 22) | lax.shift_left(density & (2**21 - 1), 1) | bit
        rows = jnp.concatenate([first, second], axis=0)
        for g in range(NP):
            pay_ref[g] = rows
        lane = lax.broadcasted_iota(jnp.int32, (Y, LANES), 1)
        for i, a in enumerate((t, s)):
            edge = jnp.zeros((Y, LANES), F32)
            for x in range(XE):
                lo_ref[i * XE + x : i * XE + x + 1] = a[x, 0:1]
                hi_ref[i * XE + x : i * XE + x + 1] = a[x, Y - 1 : Y]
                column = jnp.where(upper, a[x, :, D - 1 : D], a[x, :, 0:1])
                edge = jnp.where(lane == x, column, edge)
            out_ref[4 * T * XE + i * Y : 4 * T * XE + (i + 1) * Y] = edge

    species = species.reshape(T, W, YG)
    payload, lo, hi, outer = call(
        pack,
        (
            jax.ShapeDtypeStruct((NP, 2 * ROWS, LANES), jnp.int32),
            f32(2 * XE, D),
            f32(2 * XE, D),
            f32(4 * T * XE + 2 * Y, LANES),
        ),
        (warmth, salt, zonal, merid, marine, species),
        specs=[pl.BlockSpec(memory_space=pl.ANY)] * 6,
        scratch=(
            pltpu.VMEM((4, XE, Y, D), F32),
            pltpu.VMEM((XE, Y, D), jnp.int32),
            pltpu.SemaphoreType.DMA((5 + T,)),
        ),
        name="pack_ocean",
        mib=60,
    )
    mine = lax.all_to_all(
        payload, "trc", split_axis=0, concat_axis=0, tiled=True, axis_index_groups=pairs_apart
    )
    far_outer = exchange_levels(outer)


    def rows(k, n=XE):
        return pl.ds(pl.multiple_of(k * XE, 8), n)

    def widen_levels(c_ref, h_ref, pad, sem):
        lev = lax.axis_index("lev")
        copy = pltpu.make_async_copy(c_ref, pad.at[:, pl.ds(4 * XE, W)], sem)
        copy.start()
        for t in range(T):
            outer = h_ref[t * 4 * XE : (t + 1) * 4 * XE]
            pad[t, 0 : 4 * XE] = jnp.where(lev > 0, outer, 0.0)
            pad[t, (D + 4) * XE :] = jnp.where(lev < nlev - 1, outer, 0.0)
        copy.wait()

    pad = call(
        widen_levels,
        f32(T, (D + 8) * XE, YG),
        (species, far_outer),
        specs=[pl.BlockSpec(memory_space=pl.ANY), pl.BlockSpec(memory_space=pltpu.VMEM)],
        scratch=(pltpu.SemaphoreType.DMA(()),),
        name="widen_levels",
    )
    mine, pad = lax.optimization_barrier((mine, pad))
    other = lax.ppermute(mine, "trc", [(i, i ^ 1) for i in range(ntrc)])

    def plane(ref, i):
        return ref[i * XE : (i + 1) * XE]

    def dense(raw):
        return jnp.where(raw < 0.5 * DRY, raw, 0.0)

    def beside(a, axis):
        return shift(a, 1, axis) + shift(a, -1, axis)

    def faces(raw, speeds, along_y, before):
        wet = jnp.where(raw < 0.5 * DRY, 1.0, 0.0)
        d = dense(raw)
        total = before + d
        p = buoyancy * (total - 0.5 * d)
        result = []
        for axis, (a, sides) in enumerate(zip(speeds, along_y)):
            mask = wet * shift(wet, 1, axis)
            lap = beside(a, 0) + sides - 4.0 * a
            push = viscosity * lap - (shift(p, 1, axis) - p)
            result.append((mask * (a + marine_advance * push), mask))
        return total, result

    def unpack(a_ref, b_ref, uv_ref, mask_ref, l_ref, f_ref):
        core = lax.axis_index("trc") % 2
        lane = lax.broadcasted_iota(jnp.int32, (YG, LANES), 1)

        def words(at):
            rows = []
            for g in range(NP):
                a, b = a_ref[g, at : at + Y], b_ref[g, at : at + Y]
                rows += [jnp.where(core == 0, a, b), jnp.where(core == 0, b, a)]
            return jnp.concatenate(rows, axis=0)

        bits = words(ROWS) & 1
        numbers = jnp.sum(jnp.where(lane < 16, lax.shift_left(bits, lane % 16), 0), axis=1, keepdims=True)
        units = []
        for i in range(3):
            number = lax.shift_right_logical(numbers, 5 * i) & 31
            unit = jnp.full((YG, 1), tops[i] / MOST, F32)
            for b in range(5):
                unit = jnp.where(lax.shift_right_logical(number, b) & 1 > 0, unit * 2.0 ** -(2**b), unit)
            units.append(unit)

        def put(f, x, a):
            turned = a.T
            for g in range(G):
                f_ref[f, pl.ds(x + g * XL, D, stride=XE), :] = turned[g * D : (g + 1) * D]

        for x in range(XL):
            first, second = words(x * Y), words(ROWS + x * Y)
            u = lax.shift_right_arithmetic(first, 11)
            v = lax.shift_right_arithmetic(lax.shift_left(first, 21), 21)
            v = lax.shift_left(v, 10) | lax.shift_right_logical(second, 22)
            density = lax.shift_right_arithmetic(lax.shift_left(second, 10), 11)
            put(0, x, jnp.where(density == DRY_CODE, DRY, density.astype(F32) * units[0]))
            for i, a in enumerate((u, v)):
                a = a.astype(F32) * units[1 + i]
                put(1 + i, x, a)
                put(3 + i, x, beside(a, 0))

        def field(f, k):
            return f_ref[f, pl.ds(pl.multiple_of(k * XE, 8), XE)]

        def one(k, carry):
            total, sums = carry
            f = [field(i, k) for i in range(5)]
            total, new = faces(f[0], f[1:3], f[3:5], total)
            for i, (speed, mask) in enumerate(new):
                uv_ref[i, k] = speed
                mask_ref[i, k] = mask
            parts = (new[0][0], new[1][0], new[0][1], new[1][1])
            return total, tuple(a + b for a, b in zip(sums, parts))

        zero = jnp.zeros((XE, YG), F32)
        total, sums = lax.fori_loop(0, D, one, (zero, (zero,) * 4), unroll=D)
        for i, a in enumerate((total,) + sums):
            l_ref[i * XE : (i + 1) * XE] = a
        first = jnp.where(lax.axis_index("lev") == 0, D - 2, 0)
        for f in range(3):
            for k in range(2):
                at = (5 + 2 * f + k) * XE
                l_ref[at : at + XE] = field(f, first + k)

    near_uv, masks, own_levels = call(
        unpack,
        (f32(2, D, XE, YG), f32(2, D, XE, YG), f32(11 * XE, YG)),
        (mine, other),
        scratch=(pltpu.VMEM((5, W, YG), F32),),
        name="unpack_ocean",
    )
    own_levels, pad = lax.optimization_barrier((own_levels, pad))
    far_levels = exchange_levels(own_levels)

    def half_slope(lo, mid, hi):
        return minmod(0.5 * (mid - lo), 0.5 * (hi - mid))

    def edges(c, axis):
        d = 0.5 * (shift(c, 1, axis) - c)
        half = minmod(shift(d, -1, axis), d)
        return c + half, shift(c - half, 1, axis)

    def slopes(pad, side):
        def one(k, carry):
            lo, mid = carry
            hi = pad[:, rows(k + 2)]
            half = half_slope(lo, mid, hi)
            values = edges(mid, 1) + edges(mid, 2) + (mid + half, mid - half)
            for i, a in enumerate(values):
                side[i, :, rows(k)] = a
            return mid, hi

        count = D + 6
        first = (pad[:, 0:XE], pad[:, XE : 2 * XE])
        lax.fori_loop(0, count, one, first, unroll=count // 5)

    side = call(slopes, f32(6, T, (D + 6) * XE, YG), (pad,), name="first_slopes")
    far_levels, side = lax.optimization_barrier((far_levels, side))

    def speeds(n_ref, m_ref, o_ref, r_ref, uv_ref, fv_ref):
        lev = lax.axis_index("lev")
        above = jnp.where(lev > 0, plane(r_ref, 0), 0.0)
        sum_here = plane(o_ref, 0)

        def pushes(a):
            return [-marine_advance * buoyancy * (shift(a, 1, i) - a) for i in range(2)]

        def spread_out(u, v):
            return u - shift(u, -1, 0) + v - shift(v, -1, 1)

        def far(e, total):
            k = e % 2 if e < 2 else e - D - 2
            speeds = plane(r_ref, 7 + k), plane(r_ref, 9 + k)
            sides = [beside(a, 1) for a in speeds]
            total, new = faces(plane(r_ref, 5 + k), speeds, sides, total)
            for i in range(2):
                uv_ref[i, e] = new[i][0]
            return total

        total = above - dense(plane(r_ref, 5)) - dense(plane(r_ref, 6))
        for e in (0, 1):
            total = far(e, total)
        total = above + sum_here
        for e in (D + 2, D + 3):
            total = far(e, total)

        push = pushes(sum_here)
        lower = [plane(r_ref, 1 + i) + plane(r_ref, 3 + i) * push[i] for i in range(2)]
        below = jnp.where(lev < nlev - 1, spread_out(*lower), 0.0)

        def divergence(e):
            return spread_out(uv_ref[0, e], uv_ref[1, e])

        fv_ref[D + 2] = below
        fv_ref[D + 3] = below - divergence(D + 2)
        fv_ref[D + 4] = below - divergence(D + 2) - divergence(D + 3)
        push = pushes(above)

        def climb(j, total):
            k = D - 1 - j
            new = [n_ref[i, k] + m_ref[i, k] * push[i] for i in range(2)]
            for i in range(2):
                uv_ref[i, k + 2] = new[i]
            total = total + spread_out(*new)
            fv_ref[k + 2] = total
            return total

        total = lax.fori_loop(0, D, climb, below, unroll=D)
        fv_ref[2] = jnp.where(lev == 0, 0.0, total)
        for e in (1, 0):
            total = total + divergence(e)
            fv_ref[e] = total

    def advect(n_ref, m_ref, o_ref, r_ref, pad, side, adv_ref, msg_any, uv_ref, fv_ref, mid_pad, part, held, sems):
        speeds(n_ref, m_ref, o_ref, r_ref, uv_ref, fv_ref)

        def speeds_at(e):
            return tracer_step * uv_ref[0, e][None], tracer_step * uv_ref[1, e][None]

        def fall(e, up, low):
            w = level_step * fv_ref[e]
            return w * jnp.where(w > 0.0, up, low)

        def first_step(e, flux):
            k = rows(e + 1)
            flux_next = fall(e + 1, side[4, :, k], side[5, :, rows(e + 2)])
            change = flux_next - flux
            for i, speed in enumerate(speeds_at(e)):
                f = speed * jnp.where(speed > 0.0, side[2 * i, :, k], side[2 * i + 1, :, k])
                change = change + (f - shift(f, -1, i + 1))
            mid_pad[:, rows(e)] = pad[:, rows(e + 2)] - change
            return flux_next

        flux = fall(0, side[4, :, rows(0)], side[5, :, rows(1)])
        lax.fori_loop(0, D + 4, first_step, flux, unroll=D + 4)

        def second_step(k, carry):
            B = RL
            here = mid_pad[:, rows(k + 2, B * XE)].reshape(T, B, XE, YG)
            u = tracer_step * uv_ref[0, pl.ds(k + 2, B)]
            flat = sideways(here, u, 2)
            mid, hi, up, flux = carry
            for j in range(B):
                nxt = mid_pad[:, rows(k + j + 4)]
                half = half_slope(mid, hi, nxt)
                flux_next = fall(k + j + 3, up, hi - half)
                new = mid - (flat[:, j] + (flux_next - flux))
                part[:, pl.ds(pl.multiple_of((k + j) * X, 8), X)] = new[:, H : H + X]
                mid, hi, up, flux = hi, nxt, hi + half, flux_next
            return mid, hi, up, flux

        c = [mid_pad[:, rows(k)] for k in range(4)]
        half = half_slope(c[1], c[2], c[3])
        flux = fall(2, c[1] + half_slope(c[0], c[1], c[2]), c[2] - half)

        def sending(w):
            here = pl.ds(pl.multiple_of(w * LANES, LANES), LANES)
            return pltpu.make_async_copy(held.at[w], msg_any.at[:, :, here], sems.at[w])

        def turn(w):
            here = pl.ds(w * LANES, LANES)

            def turned(a):
                return a.reshape(RL, XE, YG)[:, H : H + X].reshape(LANES, YG).T

            v = turned(tracer_step * uv_ref[1, pl.ds(w * RL + 2, RL)])
            new = []
            for t in range(T):
                c = turned(mid_pad[t, rows(w * RL + 2, RL * XE)])
                new.append(part[t, here].T - sideways(c, v, 0))
                adv_ref[t, :, here] = new[t]
            for d in range(ntrc):
                there = [new[t][d * Y : (d + 1) * Y] for t in range(T)]
                held[w, place[d]] = jnp.concatenate(there, axis=0).astype(jnp.bfloat16)
            sending(w).start()

        def block(w, carry):
            return second_step(w * RL, carry)

        count = DX // LANES
        lax.fori_loop(0, count, block, (c[2], c[3], c[2] + half, flux))
        for w in range(count):
            turn(w)
        for w in range(count):
            sending(w).wait()

    vmem = pl.BlockSpec(memory_space=pltpu.VMEM)
    advected, message, uv, fv = call(
        advect,
        (f32(T, YG, DX), pltpu.HBM((ntrc, T * Y, DX), jnp.bfloat16))
        + (f32(2, D + 4, XE, YG), f32(D + 5, XE, YG)),
        (near_uv, masks, own_levels, far_levels, pad, side),
        scratch=(
            pltpu.VMEM((T, (D + 4) * XE, YG), F32),
            pltpu.VMEM((T, DX, YG), F32),
            pltpu.VMEM((DX // LANES, ntrc, T * Y, LANES), jnp.bfloat16),
            pltpu.SemaphoreType.DMA((DX // LANES,)),
        ),
        outs=(vmem, pl.BlockSpec(memory_space=pltpu.HBM), vmem, vmem),
        name="advect_tracers",
    )
    message, lo, hi = lax.optimization_barrier((message, lo, hi))
    gathered = lax.all_to_all(
        message, "trc", split_axis=0, concat_axis=0, tiled=True, axis_index_groups=[order]
    )
    ring = [(i, (i + 1) % ntrc) for i in range(ntrc)]
    south = lax.ppermute(hi, "trc", ring)
    north = lax.ppermute(lo, "trc", [(b, a) for a, b in ring])
    gathered, south, north = lax.optimization_barrier((gathered, south, north))

    def ocean(
        t_ref, s_ref, uv_ref, fv_ref, l_ref, so_ref, no_ref, sa_ref, wa_ref, ua_ref, va_ref, turn
    ):
        me, lev = lax.axis_index("trc"), lax.axis_index("lev")
        for x in range(XE):
            def level_rows(ref, first):
                return ref[pl.ds(first * XE + x, D, stride=XE), :]

            turn[0, x] = level_rows(uv_ref.at[0], 2).T
            turn[1, x] = level_rows(uv_ref.at[1], 2).T
            turn[2, x] = level_rows(fv_ref, 2).T
            turn[3, x] = level_rows(fv_ref, 3).T
        here = pl.ds(pl.multiple_of(me * Y, 8), Y)
        past = pl.ds(pl.multiple_of(lax.rem(me + ntrc - 1, ntrc) * Y, 8), Y)
        u, v, w, w_next = (turn[i, :, here] for i in range(4))
        v_south = turn[1, :, past][:, Y - 1 : Y]
        level = lax.broadcasted_iota(jnp.int32, (XE, Y, D), 2)
        row = lax.broadcasted_iota(jnp.int32, (XE, Y, D), 1)

        def east(a):
            return jnp.concatenate([a[1:], a[:1]], axis=0)

        def west(a):
            return jnp.concatenate([a[-1:], a[:-1]], axis=0)

        def donor(speed, near, far):
            return jnp.maximum(speed, 0.0) * near + jnp.minimum(speed, 0.0) * far

        def advance(c, i):
            so = jnp.stack([so_ref[i * XE + x : i * XE + x + 1] for x in range(XE)])
            no = jnp.stack([no_ref[i * XE + x : i * XE + x + 1] for x in range(XE)])
            tile = l_ref[4 * T * XE + i * Y : 4 * T * XE + (i + 1) * Y]
            edge = jnp.stack([tile[:, x : x + 1] for x in range(XE)])
            wide = jnp.concatenate([c, jnp.zeros((XE, Y, LANES - D), F32)], axis=2) if D < LANES else c
            upper = shift(wide, -1, 2)[:, :, :D]
            upper = jnp.where(level == 0, jnp.where(lev > 0, edge, 0.0), upper)
            lower = shift(wide, 1, 2)[:, :, :D]
            lower = jnp.where(level == D - 1, jnp.where(lev < nlev - 1, edge, 0.0), lower)
            fe = donor(u, c, east(c))
            fn = donor(v, c, jnp.where(row == Y - 1, no, shift(c, 1, 1)))
            fn_south = jnp.where(row == 0, donor(v_south, so, c[:, 0:1]), shift(fn, -1, 1))
            fall = donor(w_next, c, lower) - donor(w, upper, c)
            return c - marine_advance * ((fe - west(fe)) + (fn - fn_south) + fall)

        sa_ref[...] = advance(s_ref[...], 1)[H : H + X]
        wa_ref[...] = advance(t_ref[...], 0)[H : H + X]
        ua_ref[...] = u[H : H + X]
        va_ref[...] = v[H : H + X]

    saltiness_final, warmth_moved, zonal_speed_final, meridional_speed_final = call(
        ocean,
        (f32(X, Y, D),) * 4,
        (
            warmth,
            salt,
            uv.reshape(2, (D + 4) * XE, YG),
            fv.reshape((D + 5) * XE, YG),
            far_outer,
            south,
            north,
        ),
        scratch=(pltpu.VMEM((4, XE, YG, D), F32),),
        name="own_ocean",
    )

    speed_most = speed_bound + marine_advance * (
        2 * buoyancy * hydro_bound * D * nlev + viscosity * 8 * speed_bound
    )
    growth = 1 + 4 * tracer_step * speed_most + 2 * level_step * (4 * speed_most * D * nlev)
    react_most = NT * coupling_bound * species_bound * growth**2
    unit = 2.0 ** max(0, math.ceil(math.log2(react_most / 65504.0)))

    def spread_columns(c_ref, o_ref):
        n = NT * Y

        def pick(shape, along):
            wide, narrow = (lax.broadcasted_iota(jnp.int32, shape, d) for d in (along, 1 - along))
            device = sum(jnp.where(wide // (T * Y) == p, d, 0) for p, d in enumerate(order))
            tracer = device * T + (wide // Y) % T
            return jnp.where(tracer == narrow, 1.0, 0.0).astype(jnp.bfloat16)

        tall = jnp.dot(pick((n, NT), 0), c_ref[...], preferred_element_type=F32)
        full = jnp.dot(
            tall.astype(jnp.bfloat16), pick((NT, n), 1), preferred_element_type=F32
        )
        row, lane = (lax.broadcasted_iota(jnp.int32, (n, n), d) for d in (0, 1))
        o_ref[...] = jnp.where(row % Y == lane % Y, full, 0.0).astype(jnp.bfloat16)

    spread = call(
        spread_columns,
        jax.ShapeDtypeStruct((NT * Y, NT * Y), jnp.bfloat16),
        (coupling_matrix,),
        name="spread_coupling",
    )
    flat_tracers = gathered.reshape(NT * Y, DX)
    reaction = jnp.dot(spread, flat_tracers, preferred_element_type=F32)
    reaction = (reaction * (1.0 / unit)).astype(jnp.float16).reshape(ntrc, T * Y, DX)
    returned = lax.all_to_all(
        reaction, "trc", split_axis=0, concat_axis=0, tiled=True, axis_index_groups=[order]
    )

    def shade(x_ref, g_ref, k_ref, att_ref, cum_ref):
        att = jnp.zeros((Y, DX), F32)
        for d in range(ntrc):
            rows = x_ref[d].astype(F32)
            for t in range(T):
                att = att + k_ref[g_ref[order[d] * T + t]] * rows[t * Y : (t + 1) * Y]
        att_ref[...] = att
        lane = lax.broadcasted_iota(jnp.int32, (Y, DX), 1)
        total = att
        width = X
        while width < DX:
            total = total + jnp.where(lane < width, 0.0, shift(total, -width, 1))
            width *= 2
        cum_ref[...] = total

    smem = pl.BlockSpec(memory_space=pltpu.SMEM)
    attenuation, shaded = call(
        shade,
        (f32(Y, DX), f32(Y, DX)),
        (gathered, species_guild_number, guild_extinction_coefficient),
        specs=[vmem, smem, smem],
        name="shade",
    )
    far_shade = exchange_levels(shaded)

    def heat(att_ref, cum_ref, r_ref, w_ref, m_ref, o_ref, turn):
        lane = lax.broadcasted_iota(jnp.int32, (Y, LANES), 1)
        keep = (lax.axis_index("lev") > 0) & (lane >= LANES - X)
        above = jnp.where(keep, r_ref[:, DX - LANES :], 0.0)
        width = X
        while width < LANES:
            above = above + shift(above, width, 1)
            width *= 2
        att = att_ref[...]
        path = jnp.concatenate([above] * (DX // LANES), axis=1) + cum_ref[...] - att
        turn[...] = (jnp.exp(-path) * (1.0 - jnp.exp(-att))).T
        for x in range(X):
            absorbed = turn[pl.ds(x, D, stride=X), :].T
            o_ref[x] = w_ref[x] + warming_amount * (m_ref[x].astype(F32) * absorbed)

    warmth_final = call(
        heat,
        f32(X, Y, D),
        (attenuation, shaded, far_shade, warmth_moved, jnp.transpose(marine_indicator, (1, 2, 0))),
        scratch=(pltpu.VMEM((DX, Y), F32),),
        name="heat",
    )

    def finish(r_ref, a_ref, o_any, o_ref, sems):
        copies = [pltpu.make_async_copy(o_ref.at[t], o_any.at[t], sems.at[t]) for t in range(T)]
        for t in range(T):
            for w in range(DX // LANES):
                rows = [
                    r_ref[place[d], t * Y : (t + 1) * Y, w * LANES : (w + 1) * LANES]
                    for d in range(ntrc)
                ]
                here = slice(w * LANES, (w + 1) * LANES)
                o_ref[t, here] = (a_ref[t, :, here] + (react_step * unit) * jnp.concatenate(rows, axis=0)).T
            copies[t].start()
        for copy in copies:
            copy.wait()

    species_final = call(
        finish,
        f32(T, DX, YG),
        (returned.astype(F32), advected),
        scratch=(pltpu.VMEM((T, DX, YG), F32), pltpu.SemaphoreType.DMA((T,))),
        name="finish_tracers",
        outs=pl.BlockSpec(memory_space=pl.ANY),
    )
    ocean_outputs = (warmth_final, saltiness_final, zonal_speed_final, meridional_speed_final)
    ocean_outputs = tuple(jnp.transpose(a, (2, 0, 1)) for a in ocean_outputs)
    return ocean_outputs + (species_final.reshape(T, D, X, YG),)


def solution(mesh):
    ocean = P("lev", "cols", "trc")
    in_specs = (ocean,) * 5 + (P("trc", "lev", "cols", None), P(), P(), P())
    out_specs = (ocean,) * 4 + (P("trc", "lev", "cols", None),)
    return jax.shard_map(shards, mesh=mesh, in_specs=in_specs, out_specs=out_specs, check_vma=False)
```

```python
import math
import random

import jax
import jax.numpy as jnp
from jax import lax
from jax.experimental import pallas as pl
from jax.experimental.pallas import tpu as pltpu
from jax.sharding import PartitionSpec as P

viscosity = 0.2
buoyancy = 0.25
marine_advance = 0.05
tracer_step = 0.2
level_step = 0.04
react_step = 0.25
warming_amount = 60.0

speed_bound = 3.0
hydro_bound = 6.0
species_bound = 2.0
coupling_bound = 0.75

LANES = 128
DRY = 1e30
F32 = jnp.float32


def call(kernel, out_shape, args, specs=None, scratch=(), name=None, mib=16, outs=None):
    vmem = pl.BlockSpec(memory_space=pltpu.VMEM)
    outs = jax.tree.map(lambda _: vmem, out_shape) if outs is None else outs
    return pl.pallas_call(
        kernel,
        out_shape=out_shape,
        in_specs=[vmem] * len(args) if specs is None else specs,
        out_specs=outs,
        scratch_shapes=list(scratch),
        compiler_params=pltpu.CompilerParams(vmem_limit_bytes=mib * 1024 * 1024),
        name=name,
    )(*args)


def f32(*shape):
    return jax.ShapeDtypeStruct(shape, F32)


def shift(a, steps, axis):
    return pltpu.roll(a, (-steps) % a.shape[axis], axis)


def minmod(p, r):
    return jnp.maximum(jnp.minimum(p, r), jnp.minimum(jnp.maximum(p, r), 0.0))


def sideways(c, speed, axis):
    d = 0.5 * (shift(c, 1, axis) - c)
    half = minmod(shift(d, -1, axis), d)
    flux = speed * jnp.where(speed > 0.0, c + half, shift(c - half, 1, axis))
    return flux - shift(flux, -1, axis)


def exchange_levels(part):
    return lax.ppermute(part, "lev", [(0, 1), (1, 0)])


def shards(
    potential_warmth,
    saltiness_anomaly,
    zonal_speed,
    meridional_speed,
    marine_indicator,
    species_concentrations,
    coupling_matrix,
    species_guild_number,
    guild_extinction_coefficient,
):
    cols, ntrc, nlev = lax.axis_size("cols"), lax.axis_size("trc"), lax.axis_size("lev")
    D, X, Y = potential_warmth.shape
    T = species_concentrations.shape[0]
    NT = coupling_matrix.shape[0]
    YG = species_concentrations.shape[3]
    assert nlev == 2 and YG == LANES and X % 8 == 0 and Y % 8 == 0 and ntrc % 2 == 0
    assert LANES % D == 0 and D % 8 == 0 and X % (2 * LANES // D) == 0
    H = X if cols > 1 else 0
    XE = X + 2 * H
    W, DX = D * XE, D * X
    G = LANES // D
    XL = XE // G
    RL = LANES // X

    def widen(block, dim):
        if H == 0:
            return block
        ahead = [(i, (i + 1) % cols) for i in range(cols)]
        back = [(i, (i - 1) % cols) for i in range(cols)]
        low = lax.ppermute(block, "cols", ahead)
        high = lax.ppermute(block, "cols", back)
        return jnp.concatenate([low, block, high], axis=dim)

    warmth, salt, zonal, merid, marine = (
        widen(jnp.transpose(a, (1, 2, 0)), 0)
        for a in (potential_warmth, saltiness_anomaly, zonal_speed, meridional_speed, marine_indicator)
    )
    species = widen(species_concentrations, 2)
    NP = ntrc // 2
    order = list(range(ntrc))
    random.Random(4).shuffle(order)
    place = [order.index(d) for d in range(ntrc)]
    back = list(range(ntrc))
    random.Random(3).shuffle(back)
    back_place = [back.index(d) for d in range(ntrc)]
    pairs_apart = [[2 * g + c for g in range(NP)] for c in range(2)]

    ROWS = XL * Y
    MOST = 2**20 - 1
    DRY_CODE = -(2**20)
    SCALES = 31

    def top(bound):
        return 2.0 ** math.ceil(math.log2(bound))

    tops = (top(hydro_bound * 1.001), top(speed_bound), top(speed_bound))

    def pack(t_any, s_any, u_any, v_any, m_any, c_any, pay_ref, lo_ref, hi_ref, out_ref, held, wet, sems):
        upper = lax.axis_index("lev") == 0
        first = pl.multiple_of(jnp.where(upper, D - 4, 0) * XE, 8)
        copies = [
            pltpu.make_async_copy(a, held.at[i], sems.at[i])
            for i, a in enumerate((t_any, s_any, u_any, v_any))
        ]
        copies.append(pltpu.make_async_copy(m_any, wet, sems.at[4]))
        for t in range(T):
            copies.append(
                pltpu.make_async_copy(
                    c_any.at[t, pl.ds(first, 4 * XE)],
                    out_ref.at[pl.ds(t * 4 * XE, 4 * XE)],
                    sems.at[5 + t],
                )
            )
        for copy in copies:
            copy.start()
        for copy in copies:
            copy.wait()
        t, s = held[0], held[1]
        sea = wet[...] > 0
        density = jnp.where(sea, 0.8 * s - 0.2 * t, 0.0)
        numbers, halves = 0, []
        for i, a in enumerate((density, held[2], held[3])):
            most = jnp.max(jnp.abs(a), axis=(0, 1, 2), keepdims=True)[0]
            unit, number = tops[i], 0
            for k in range(1, SCALES + 1):
                fits = most <= tops[i] * 2.0**-k
                unit = jnp.where(fits, tops[i] * 2.0**-k, unit)
                number = jnp.where(fits, k, number)
            code = jnp.floor(jnp.clip(a * (1.0 / unit), -1.0, 1.0) * MOST + 0.5).astype(jnp.int32)
            if i == 0:
                code = jnp.where(sea, code, DRY_CODE)
            numbers = numbers + number * 32**i
            code = jnp.concatenate([code[g * XL : (g + 1) * XL] for g in range(G)], axis=2)
            halves.append(code.reshape(XL * Y, LANES))
        density, u, v = halves
        lane = lax.broadcasted_iota(jnp.int32, (XL * Y, LANES), 1)
        bit = lax.shift_right_logical(numbers, lane % 16) & 1
        first = lax.shift_left(u, 11) | (lax.shift_right_arithmetic(v, 10) & 2047)
        second = lax.shift_left(v & 1023, 22) | lax.shift_left(density & (2**21 - 1), 1) | bit
        rows = jnp.concatenate([first, second], axis=0)
        for g in range(NP):
            pay_ref[g] = rows
        lane = lax.broadcasted_iota(jnp.int32, (Y, LANES), 1)
        for i, a in enumerate((t, s)):
            edge = jnp.zeros((Y, LANES), F32)
            for x in range(XE):
                lo_ref[i * XE + x : i * XE + x + 1] = a[x, 0:1]
                hi_ref[i * XE + x : i * XE + x + 1] = a[x, Y - 1 : Y]
                column = jnp.where(upper, a[x, :, D - 1 : D], a[x, :, 0:1])
                edge = jnp.where(lane == x, column, edge)
            out_ref[4 * T * XE + i * Y : 4 * T * XE + (i + 1) * Y] = edge

    species = species.reshape(T, W, YG)
    payload, lo, hi, outer = call(
        pack,
        (
            jax.ShapeDtypeStruct((NP, 2 * ROWS, LANES), jnp.int32),
            f32(2 * XE, D),
            f32(2 * XE, D),
            f32(4 * T * XE + 2 * Y, LANES),
        ),
        (warmth, salt, zonal, merid, marine, species),
        specs=[pl.BlockSpec(memory_space=pl.ANY)] * 6,
        scratch=(
            pltpu.VMEM((4, XE, Y, D), F32),
            pltpu.VMEM((XE, Y, D), jnp.int32),
            pltpu.SemaphoreType.DMA((5 + T,)),
        ),
        name="pack_ocean",
        mib=60,
    )
    mine = lax.all_to_all(
        payload, "trc", split_axis=0, concat_axis=0, tiled=True, axis_index_groups=pairs_apart
    )
    far_outer = exchange_levels(outer)


    def rows(k, n=XE):
        return pl.ds(pl.multiple_of(k * XE, 8), n)

    def widen_levels(c_ref, h_ref, pad, sem):
        lev = lax.axis_index("lev")
        copy = pltpu.make_async_copy(c_ref, pad.at[:, pl.ds(4 * XE, W)], sem)
        copy.start()
        for t in range(T):
            outer = h_ref[t * 4 * XE : (t + 1) * 4 * XE]
            pad[t, 0 : 4 * XE] = jnp.where(lev > 0, outer, 0.0)
            pad[t, (D + 4) * XE :] = jnp.where(lev < nlev - 1, outer, 0.0)
        copy.wait()

    pad = call(
        widen_levels,
        f32(T, (D + 8) * XE, YG),
        (species, far_outer),
        specs=[pl.BlockSpec(memory_space=pl.ANY), pl.BlockSpec(memory_space=pltpu.VMEM)],
        scratch=(pltpu.SemaphoreType.DMA(()),),
        name="widen_levels",
    )
    mine, pad = lax.optimization_barrier((mine, pad))
    other = lax.ppermute(mine, "trc", [(i, i ^ 1) for i in range(ntrc)])

    def plane(ref, i):
        return ref[i * XE : (i + 1) * XE]

    def dense(raw):
        return jnp.where(raw < 0.5 * DRY, raw, 0.0)

    def beside(a, axis):
        return shift(a, 1, axis) + shift(a, -1, axis)

    def faces(raw, speeds, along_y, before):
        wet = jnp.where(raw < 0.5 * DRY, 1.0, 0.0)
        d = dense(raw)
        total = before + d
        p = buoyancy * (total - 0.5 * d)
        result = []
        for axis, (a, sides) in enumerate(zip(speeds, along_y)):
            mask = wet * shift(wet, 1, axis)
            lap = beside(a, 0) + sides - 4.0 * a
            push = viscosity * lap - (shift(p, 1, axis) - p)
            result.append((mask * (a + marine_advance * push), mask))
        return total, result

    def unpack(a_ref, b_ref, uv_ref, mask_ref, l_ref, f_ref):
        core = lax.axis_index("trc") % 2
        lane = lax.broadcasted_iota(jnp.int32, (YG, LANES), 1)

        def words(at):
            rows = []
            for g in range(NP):
                a, b = a_ref[g, at : at + Y], b_ref[g, at : at + Y]
                rows += [jnp.where(core == 0, a, b), jnp.where(core == 0, b, a)]
            return jnp.concatenate(rows, axis=0)

        bits = words(ROWS) & 1
        numbers = jnp.sum(jnp.where(lane < 16, lax.shift_left(bits, lane % 16), 0), axis=1, keepdims=True)
        units = []
        for i in range(3):
            number = lax.shift_right_logical(numbers, 5 * i) & 31
            unit = jnp.full((YG, 1), tops[i] / MOST, F32)
            for b in range(5):
                unit = jnp.where(lax.shift_right_logical(number, b) & 1 > 0, unit * 2.0 ** -(2**b), unit)
            units.append(unit)

        def put(f, x, a):
            turned = a.T
            for g in range(G):
                f_ref[f, pl.ds(x + g * XL, D, stride=XE), :] = turned[g * D : (g + 1) * D]

        for x in range(XL):
            first, second = words(x * Y), words(ROWS + x * Y)
            u = lax.shift_right_arithmetic(first, 11)
            v = lax.shift_right_arithmetic(lax.shift_left(first, 21), 21)
            v = lax.shift_left(v, 10) | lax.shift_right_logical(second, 22)
            density = lax.shift_right_arithmetic(lax.shift_left(second, 10), 11)
            put(0, x, jnp.where(density == DRY_CODE, DRY, density.astype(F32) * units[0]))
            for i, a in enumerate((u, v)):
                a = a.astype(F32) * units[1 + i]
                put(1 + i, x, a)
                put(3 + i, x, beside(a, 0))

        def field(f, k):
            return f_ref[f, pl.ds(pl.multiple_of(k * XE, 8), XE)]

        def one(k, carry):
            total, sums = carry
            f = [field(i, k) for i in range(5)]
            total, new = faces(f[0], f[1:3], f[3:5], total)
            for i, (speed, mask) in enumerate(new):
                uv_ref[i, k] = speed
                mask_ref[i, k] = mask
            parts = (new[0][0], new[1][0], new[0][1], new[1][1])
            return total, tuple(a + b for a, b in zip(sums, parts))

        zero = jnp.zeros((XE, YG), F32)
        total, sums = lax.fori_loop(0, D, one, (zero, (zero,) * 4), unroll=D)
        for i, a in enumerate((total,) + sums):
            l_ref[i * XE : (i + 1) * XE] = a
        first = jnp.where(lax.axis_index("lev") == 0, D - 2, 0)
        for f in range(3):
            for k in range(2):
                at = (5 + 2 * f + k) * XE
                l_ref[at : at + XE] = field(f, first + k)

    near_uv, masks, own_levels = call(
        unpack,
        (f32(2, D, XE, YG), f32(2, D, XE, YG), f32(11 * XE, YG)),
        (mine, other),
        scratch=(pltpu.VMEM((5, W, YG), F32),),
        name="unpack_ocean",
    )
    own_levels, pad = lax.optimization_barrier((own_levels, pad))
    far_levels = exchange_levels(own_levels)

    def half_slope(lo, mid, hi):
        return minmod(0.5 * (mid - lo), 0.5 * (hi - mid))

    def edges(c, axis):
        d = 0.5 * (shift(c, 1, axis) - c)
        half = minmod(shift(d, -1, axis), d)
        return c + half, shift(c - half, 1, axis)

    def slopes(pad, side):
        def one(k, carry):
            lo, mid = carry
            hi = pad[:, rows(k + 2)]
            half = half_slope(lo, mid, hi)
            values = edges(mid, 1) + edges(mid, 2) + (mid + half, mid - half)
            for i, a in enumerate(values):
                side[i, :, rows(k)] = a
            return mid, hi

        count = D + 6
        first = (pad[:, 0:XE], pad[:, XE : 2 * XE])
        lax.fori_loop(0, count, one, first, unroll=count // 5)

    side = call(slopes, f32(6, T, (D + 6) * XE, YG), (pad,), name="first_slopes")
    far_levels, side = lax.optimization_barrier((far_levels, side))

    def speeds(n_ref, m_ref, o_ref, r_ref, uv_ref, fv_ref):
        lev = lax.axis_index("lev")
        above = jnp.where(lev > 0, plane(r_ref, 0), 0.0)
        sum_here = plane(o_ref, 0)

        def pushes(a):
            return [-marine_advance * buoyancy * (shift(a, 1, i) - a) for i in range(2)]

        def spread_out(u, v):
            return u - shift(u, -1, 0) + v - shift(v, -1, 1)

        def far(e, total):
            k = e % 2 if e < 2 else e - D - 2
            speeds = plane(r_ref, 7 + k), plane(r_ref, 9 + k)
            sides = [beside(a, 1) for a in speeds]
            total, new = faces(plane(r_ref, 5 + k), speeds, sides, total)
            for i in range(2):
                uv_ref[i, e] = new[i][0]
            return total

        total = above - dense(plane(r_ref, 5)) - dense(plane(r_ref, 6))
        for e in (0, 1):
            total = far(e, total)
        total = above + sum_here
        for e in (D + 2, D + 3):
            total = far(e, total)

        push = pushes(sum_here)
        lower = [plane(r_ref, 1 + i) + plane(r_ref, 3 + i) * push[i] for i in range(2)]
        below = jnp.where(lev < nlev - 1, spread_out(*lower), 0.0)

        def divergence(e):
            return spread_out(uv_ref[0, e], uv_ref[1, e])

        fv_ref[D + 2] = below
        fv_ref[D + 3] = below - divergence(D + 2)
        fv_ref[D + 4] = below - divergence(D + 2) - divergence(D + 3)
        push = pushes(above)

        def climb(j, total):
            k = D - 1 - j
            new = [n_ref[i, k] + m_ref[i, k] * push[i] for i in range(2)]
            for i in range(2):
                uv_ref[i, k + 2] = new[i]
            total = total + spread_out(*new)
            fv_ref[k + 2] = total
            return total

        total = lax.fori_loop(0, D, climb, below, unroll=D)
        fv_ref[2] = jnp.where(lev == 0, 0.0, total)
        for e in (1, 0):
            total = total + divergence(e)
            fv_ref[e] = total

    def advect(n_ref, m_ref, o_ref, r_ref, pad, side, adv_ref, msg_any, uv_ref, fv_ref, mid_pad, part, held, sems):
        speeds(n_ref, m_ref, o_ref, r_ref, uv_ref, fv_ref)

        def speeds_at(e):
            return tracer_step * uv_ref[0, e][None], tracer_step * uv_ref[1, e][None]

        def fall(e, up, low):
            w = level_step * fv_ref[e]
            return w * jnp.where(w > 0.0, up, low)

        def first_step(e, flux):
            k = rows(e + 1)
            flux_next = fall(e + 1, side[4, :, k], side[5, :, rows(e + 2)])
            change = flux_next - flux
            for i, speed in enumerate(speeds_at(e)):
                f = speed * jnp.where(speed > 0.0, side[2 * i, :, k], side[2 * i + 1, :, k])
                change = change + (f - shift(f, -1, i + 1))
            mid_pad[:, rows(e)] = pad[:, rows(e + 2)] - change
            return flux_next

        flux = fall(0, side[4, :, rows(0)], side[5, :, rows(1)])
        lax.fori_loop(0, D + 4, first_step, flux, unroll=D + 4)

        def second_step(k, carry):
            B = RL
            here = mid_pad[:, rows(k + 2, B * XE)].reshape(T, B, XE, YG)
            u = tracer_step * uv_ref[0, pl.ds(k + 2, B)]
            flat = sideways(here, u, 2)
            mid, hi, up, flux = carry
            for j in range(B):
                nxt = mid_pad[:, rows(k + j + 4)]
                half = half_slope(mid, hi, nxt)
                flux_next = fall(k + j + 3, up, hi - half)
                new = mid - (flat[:, j] + (flux_next - flux))
                part[:, pl.ds(pl.multiple_of((k + j) * X, 8), X)] = new[:, H : H + X]
                mid, hi, up, flux = hi, nxt, hi + half, flux_next
            return mid, hi, up, flux

        c = [mid_pad[:, rows(k)] for k in range(4)]
        half = half_slope(c[1], c[2], c[3])
        flux = fall(2, c[1] + half_slope(c[0], c[1], c[2]), c[2] - half)

        def sending(w):
            here = pl.ds(pl.multiple_of(w * LANES, LANES), LANES)
            return pltpu.make_async_copy(held.at[w], msg_any.at[:, :, here], sems.at[w])

        def turn(w):
            here = pl.ds(w * LANES, LANES)

            def turned(a):
                return a.reshape(RL, XE, YG)[:, H : H + X].reshape(LANES, YG).T

            v = turned(tracer_step * uv_ref[1, pl.ds(w * RL + 2, RL)])
            new = []
            for t in range(T):
                c = turned(mid_pad[t, rows(w * RL + 2, RL * XE)])
                new.append(part[t, here].T - sideways(c, v, 0))
                adv_ref[t, :, here] = new[t]
            for d in range(ntrc):
                there = [new[t][d * Y : (d + 1) * Y] for t in range(T)]
                held[w, place[d]] = jnp.concatenate(there, axis=0).astype(jnp.bfloat16)
            sending(w).start()

        def block(w, carry):
            return second_step(w * RL, carry)

        count = DX // LANES
        lax.fori_loop(0, count, block, (c[2], c[3], c[2] + half, flux))
        for w in range(count):
            turn(w)
        for w in range(count):
            sending(w).wait()

    vmem = pl.BlockSpec(memory_space=pltpu.VMEM)
    advected, message, uv, fv = call(
        advect,
        (f32(T, YG, DX), pltpu.HBM((ntrc, T * Y, DX), jnp.bfloat16))
        + (f32(2, D + 4, XE, YG), f32(D + 5, XE, YG)),
        (near_uv, masks, own_levels, far_levels, pad, side),
        scratch=(
            pltpu.VMEM((T, (D + 4) * XE, YG), F32),
            pltpu.VMEM((T, DX, YG), F32),
            pltpu.VMEM((DX // LANES, ntrc, T * Y, LANES), jnp.bfloat16),
            pltpu.SemaphoreType.DMA((DX // LANES,)),
        ),
        outs=(vmem, pl.BlockSpec(memory_space=pltpu.HBM), vmem, vmem),
        name="advect_tracers",
    )
    message, lo, hi = lax.optimization_barrier((message, lo, hi))
    gathered = lax.all_to_all(
        message, "trc", split_axis=0, concat_axis=0, tiled=True, axis_index_groups=[order]
    )
    ring = [(i, (i + 1) % ntrc) for i in range(ntrc)]
    south = lax.ppermute(hi, "trc", ring)
    north = lax.ppermute(lo, "trc", [(b, a) for a, b in ring])
    gathered, south, north = lax.optimization_barrier((gathered, south, north))

    def ocean(
        t_ref, s_ref, uv_ref, fv_ref, l_ref, so_ref, no_ref, sa_ref, wa_ref, ua_ref, va_ref, turn
    ):
        me, lev = lax.axis_index("trc"), lax.axis_index("lev")
        for x in range(XE):
            def level_rows(ref, first):
                return ref[pl.ds(first * XE + x, D, stride=XE), :]

            turn[0, x] = level_rows(uv_ref.at[0], 2).T
            turn[1, x] = level_rows(uv_ref.at[1], 2).T
            turn[2, x] = level_rows(fv_ref, 2).T
            turn[3, x] = level_rows(fv_ref, 3).T
        here = pl.ds(pl.multiple_of(me * Y, 8), Y)
        past = pl.ds(pl.multiple_of(lax.rem(me + ntrc - 1, ntrc) * Y, 8), Y)
        u, v, w, w_next = (turn[i, :, here] for i in range(4))
        v_south = turn[1, :, past][:, Y - 1 : Y]
        level = lax.broadcasted_iota(jnp.int32, (XE, Y, D), 2)
        row = lax.broadcasted_iota(jnp.int32, (XE, Y, D), 1)

        def east(a):
            return jnp.concatenate([a[1:], a[:1]], axis=0)

        def west(a):
            return jnp.concatenate([a[-1:], a[:-1]], axis=0)

        def donor(speed, near, far):
            return jnp.maximum(speed, 0.0) * near + jnp.minimum(speed, 0.0) * far

        def advance(c, i):
            so = jnp.stack([so_ref[i * XE + x : i * XE + x + 1] for x in range(XE)])
            no = jnp.stack([no_ref[i * XE + x : i * XE + x + 1] for x in range(XE)])
            tile = l_ref[4 * T * XE + i * Y : 4 * T * XE + (i + 1) * Y]
            edge = jnp.stack([tile[:, x : x + 1] for x in range(XE)])
            wide = jnp.concatenate([c, jnp.zeros((XE, Y, LANES - D), F32)], axis=2) if D < LANES else c
            upper = shift(wide, -1, 2)[:, :, :D]
            upper = jnp.where(level == 0, jnp.where(lev > 0, edge, 0.0), upper)
            lower = shift(wide, 1, 2)[:, :, :D]
            lower = jnp.where(level == D - 1, jnp.where(lev < nlev - 1, edge, 0.0), lower)
            fe = donor(u, c, east(c))
            fn = donor(v, c, jnp.where(row == Y - 1, no, shift(c, 1, 1)))
            fn_south = jnp.where(row == 0, donor(v_south, so, c[:, 0:1]), shift(fn, -1, 1))
            fall = donor(w_next, c, lower) - donor(w, upper, c)
            return c - marine_advance * ((fe - west(fe)) + (fn - fn_south) + fall)

        sa_ref[...] = advance(s_ref[...], 1)[H : H + X]
        wa_ref[...] = advance(t_ref[...], 0)[H : H + X]
        ua_ref[...] = u[H : H + X]
        va_ref[...] = v[H : H + X]

    saltiness_final, warmth_moved, zonal_speed_final, meridional_speed_final = call(
        ocean,
        (f32(X, Y, D),) * 4,
        (
            warmth,
            salt,
            uv.reshape(2, (D + 4) * XE, YG),
            fv.reshape((D + 5) * XE, YG),
            far_outer,
            south,
            north,
        ),
        scratch=(pltpu.VMEM((4, XE, YG, D), F32),),
        name="own_ocean",
    )

    speed_most = speed_bound + marine_advance * (
        2 * buoyancy * hydro_bound * D * nlev + viscosity * 8 * speed_bound
    )
    growth = 1 + 4 * tracer_step * speed_most + 2 * level_step * (4 * speed_most * D * nlev)
    react_most = NT * coupling_bound * species_bound * growth**2
    unit = 2.0 ** max(0, math.ceil(math.log2(react_most / 65504.0)))

    def spread_columns(c_ref, o_ref):
        n = NT * Y

        def pick(shape, along):
            wide, narrow = (lax.broadcasted_iota(jnp.int32, shape, d) for d in (along, 1 - along))
            device = sum(jnp.where(wide // (T * Y) == p, d, 0) for p, d in enumerate((back, order)[along]))
            tracer = device * T + (wide // Y) % T
            return jnp.where(tracer == narrow, 1.0, 0.0).astype(jnp.bfloat16)

        tall = jnp.dot(pick((n, NT), 0), c_ref[...], preferred_element_type=F32)
        full = jnp.dot(
            tall.astype(jnp.bfloat16), pick((NT, n), 1), preferred_element_type=F32
        )
        row, lane = (lax.broadcasted_iota(jnp.int32, (n, n), d) for d in (0, 1))
        o_ref[...] = jnp.where(row % Y == lane % Y, full, 0.0).astype(jnp.bfloat16)

    spread = call(
        spread_columns,
        jax.ShapeDtypeStruct((NT * Y, NT * Y), jnp.bfloat16),
        (coupling_matrix,),
        name="spread_coupling",
    )
    flat_tracers = gathered.reshape(NT * Y, DX)
    reaction = jnp.dot(spread, flat_tracers, preferred_element_type=F32)
    reaction = (reaction * (1.0 / unit)).astype(jnp.float16).reshape(ntrc, T * Y, DX)
    returned = lax.all_to_all(
        reaction, "trc", split_axis=0, concat_axis=0, tiled=True, axis_index_groups=[back]
    )

    def shade(x_ref, g_ref, k_ref, att_ref, cum_ref):
        att = jnp.zeros((Y, DX), F32)
        for d in range(ntrc):
            rows = x_ref[d].astype(F32)
            for t in range(T):
                att = att + k_ref[g_ref[order[d] * T + t]] * rows[t * Y : (t + 1) * Y]
        att_ref[...] = att
        lane = lax.broadcasted_iota(jnp.int32, (Y, DX), 1)
        total = att
        width = X
        while width < DX:
            total = total + jnp.where(lane < width, 0.0, shift(total, -width, 1))
            width *= 2
        cum_ref[...] = total

    smem = pl.BlockSpec(memory_space=pltpu.SMEM)
    attenuation, shaded = call(
        shade,
        (f32(Y, DX), f32(Y, DX)),
        (gathered, species_guild_number, guild_extinction_coefficient),
        specs=[vmem, smem, smem],
        name="shade",
    )
    far_shade = exchange_levels(shaded)

    def heat(att_ref, cum_ref, r_ref, w_ref, m_ref, o_ref, turn):
        lane = lax.broadcasted_iota(jnp.int32, (Y, LANES), 1)
        keep = (lax.axis_index("lev") > 0) & (lane >= LANES - X)
        above = jnp.where(keep, r_ref[:, DX - LANES :], 0.0)
        width = X
        while width < LANES:
            above = above + shift(above, width, 1)
            width *= 2
        att = att_ref[...]
        path = jnp.concatenate([above] * (DX // LANES), axis=1) + cum_ref[...] - att
        turn[...] = (jnp.exp(-path) * (1.0 - jnp.exp(-att))).T
        for x in range(X):
            absorbed = turn[pl.ds(x, D, stride=X), :].T
            o_ref[x] = w_ref[x] + warming_amount * (m_ref[x].astype(F32) * absorbed)

    warmth_final = call(
        heat,
        f32(X, Y, D),
        (attenuation, shaded, far_shade, warmth_moved, jnp.transpose(marine_indicator, (1, 2, 0))),
        scratch=(pltpu.VMEM((DX, Y), F32),),
        name="heat",
    )

    def finish(r_ref, a_ref, o_any, o_ref, sems):
        copies = [pltpu.make_async_copy(o_ref.at[t], o_any.at[t], sems.at[t]) for t in range(T)]
        for t in range(T):
            for w in range(DX // LANES):
                rows = [
                    r_ref[back_place[d], t * Y : (t + 1) * Y, w * LANES : (w + 1) * LANES]
                    for d in range(ntrc)
                ]
                here = slice(w * LANES, (w + 1) * LANES)
                o_ref[t, here] = (a_ref[t, :, here] + (react_step * unit) * jnp.concatenate(rows, axis=0)).T
            copies[t].start()
        for copy in copies:
            copy.wait()

    species_final = call(
        finish,
        f32(T, DX, YG),
        (returned.astype(F32), advected),
        scratch=(pltpu.VMEM((T, DX, YG), F32), pltpu.SemaphoreType.DMA((T,))),
        name="finish_tracers",
        outs=pl.BlockSpec(memory_space=pl.ANY),
    )
    ocean_outputs = (warmth_final, saltiness_final, zonal_speed_final, meridional_speed_final)
    ocean_outputs = tuple(jnp.transpose(a, (2, 0, 1)) for a in ocean_outputs)
    return ocean_outputs + (species_final.reshape(T, D, X, YG),)


def solution(mesh):
    ocean = P("lev", "cols", "trc")
    in_specs = (ocean,) * 5 + (P("trc", "lev", "cols", None), P(), P(), P())
    out_specs = (ocean,) * 4 + (P("trc", "lev", "cols", None),)
    return jax.shard_map(shards, mesh=mesh, in_specs=in_specs, out_specs=out_specs, check_vma=False)
```
